128 devices in a mesh: dp: 8 (over x, core), expert: 16 (over z, y).
Axes of the slice: x: 4, y: 4, z: 4, core: 2. Of those that a mesh axis runs over, the one named last changes fastest.
Arguments:
- x_saved: bfloat16 [8, 32, 1280, 1024], P('dp', 'expert'), may hold values from -6 to 6
- d_out: bfloat16 [32768, 1024], P(('dp', 'expert')), may hold values from -6 to 6
- routes: int32 [32768, 8], P(('dp', 'expert')), may hold values from 0 to 31, all different within a row; in each aligned block of 256 rows (0 to 255, 256 to 511, ...) at most 80 rows name the same one
- probs: float32 [32768, 8], P(('dp', 'expert')), may hold values from 0.1 to 0.9
- w_gate: bfloat16 [32, 1024, 512], P('expert'), may hold values from -0.1875 to 0.1875
- w_up: bfloat16 [32, 1024, 512], P('expert'), may hold values from -0.1875 to 0.1875
- w_down: bfloat16 [32, 512, 1024], P('expert'), may hold values from -0.25 to 0.25
- res_gate: bfloat16 [8, 32, 1024, 512], P('dp', 'expert'), may hold values from -6 to 6
- res_up: bfloat16 [8, 32, 1024, 512], P('dp', 'expert'), may hold values from -6 to 6
- res_down: bfloat16 [8, 32, 512, 1024], P('dp', 'expert'), may hold values from -1.5 to 1.5
Outputs:
- d_tokens: bfloat16 [32768, 1024], P(('dp', 'expert'))
- grad_gate: float32 [32, 1024, 512], P('expert', 'dp')
- grad_up: float32 [32, 1024, 512], P('expert', 'dp')
- grad_down: float32 [32, 512, 1024], P('expert', None, 'dp')
- new_res_gate: bfloat16 [8, 32, 1024, 512], P('dp', 'expert')
- new_res_up: bfloat16 [8, 32, 1024, 512], P('dp', 'expert')
- new_res_down: bfloat16 [8, 32, 512, 1024], P('dp', 'expert')
The draws below stay inside these ranges and needn't reach their ends.
Inputs may be any that keep to these rules, and one draw needn't show every extreme that they name: `routes`: the 8 entries of a row differ. In the rows of one device (aligned blocks of 256 rows) each expert is named by at most 80 rows, a bound that some block reaches.
All inputs are finite; a program needn't handle non-finite values. Where the reference program divides by a largest or mean magnitude, that divisor is 1e-20 or more.
Results may differ from the reference program's by a relative error of at most 0.007.
Values may be sent and summed in bfloat16 or wider, within the bound.
No kernel may reach another device: no remote copies, remote signals or barrier semaphores. Data moves between devices by JAX's collectives and lax.ppermute only.
A program may use at most 192 MiB of HBM per device.

```python
import math
import jax
import jax.numpy as jnp
import numpy as np
from jax import lax

D = 1024
EXPERTS = 32
TOP = 8
HID_DEV = 512
TOK_DEV = 256
GROUP = 1
VEXP = 32
CAP = 80
SLOTS = 1280
TOKENS = 32768
N_DP = 8
N_EXPERT = 16


def level_of(key, shape, pieces, least, top_value):
    factor_of = 1.0
    for position, shards_of in pieces:
        steps = jax.random.uniform(jax.random.fold_in(jax.random.fold_in(key, 6), position), (shards_of,), jnp.float32, least / len(pieces), top_value / len(pieces))
        factor_of = factor_of * jnp.repeat(jnp.exp(steps), shape[position] // shards_of).reshape((-1,) + (1,) * (len(shape) - 1 - position))
    return factor_of


def routed_block(stream_key, own, number, rows, amount, top, reach, skew):
    order = jax.random.permutation(stream_key, amount)
    crowded, usual = shares(amount, rows * top, reach, skew, True), shares(amount, rows * top, reach, skew, False)
    places = jnp.arange(amount)

    def named(tallies, rotation):
        used = int((tallies > 0).sum())
        fixed = max(1, used // 4)
        shifted = fixed + (places - fixed + rotation * (used - fixed)) % max(1, amount - fixed)
        return jnp.zeros((amount,), jnp.int32).at[order[jnp.where(places < fixed, places, shifted)]].set(jnp.asarray(tallies, jnp.int32))

    tallies = jnp.where(number % 4 == 0, named(crowded, number // 4), named(usual, number - number // 4 - 1))
    mixed = jax.random.permutation(jax.random.fold_in(own, 3), amount)
    source_of, receiver = mixed[0:amount // 2 * 2:2], mixed[1:amount // 2 * 2:2]
    margin = jnp.minimum(tallies[source_of] - 1, reach - tallies[receiver]) // 2
    margin = jnp.where((source_of == order[0]) | (receiver == order[0]) | (tallies[receiver] == 0), 0, jnp.maximum(margin, 0))
    shifted = jax.random.randint(jax.random.fold_in(own, 4), (amount // 2,), 0, 1 << 20) % (margin + 1)
    tallies = tallies.at[source_of].add(-shifted).at[receiver].add(shifted)
    items = jnp.searchsorted(jnp.cumsum(tallies), jnp.arange(rows * top), side="right").astype(jnp.int32)
    table = items.reshape(top, rows).T
    table = table[jax.random.permutation(jax.random.fold_in(own, 1), rows)]
    rotation = jax.random.randint(jax.random.fold_in(own, 2), (rows, 1), 0, top)
    return jnp.take_along_axis(table, (jnp.arange(top)[None, :] + rotation) % top, axis=1)


def shares(number_of, total, bound, lean, full):
    portions = [(1 << 20) // math.isqrt(rank ** lean) + 1 for rank in range(1, number_of + 1)]
    largest = bound if full else min(bound, max(-(-total // number_of), total * portions[0] // sum(portions)))
    least = 1 if total - largest >= number_of - 1 else 0
    given, surplus = [largest] + [least] * (number_of - 1), total - largest - least * (number_of - 1)
    while surplus > 0:
        movable = [i for i in range(1, number_of) if given[i] < largest] or [i for i in range(1, number_of) if given[i] < bound]
        whole, remaining = sum([portions[i] for i in movable]), surplus
        for i in movable:
            more = min(bound - given[i], max(1, remaining * portions[i] // whole), surplus)
            given[i] = given[i] + more
            surplus = surplus - more
    return np.array(given)


def scatter_about(rng, dims, deviation, bound, split=(), kind=jnp.bfloat16):
    values = jax.random.normal(rng, dims, jnp.float32) * deviation
    if len(split) > 0:
        values = level_of(rng, dims, split, -0.22, 0.18) * values
    return jnp.clip(values, min=-bound, max=bound).astype(kind)


def setup_inputs(seed: int = 0) -> dict:
    key_of = jax.random.split(jax.random.key(seed), 11)
    x_saved = scatter_about(key_of[0], (N_DP, VEXP, SLOTS, D), 1.0, 6.0, ((0, 8), (1, 16)))
    d_out = scatter_about(key_of[1], (TOKENS, D), 1.0, 6.0, ((0, 128),))
    routes_keys = jax.random.split(jax.random.fold_in(key_of[2], 1), TOKENS // TOK_DEV)
    routes_turns = jax.random.permutation(jax.random.fold_in(key_of[2], 3), TOKENS // TOK_DEV)
    routes = jax.vmap(lambda own, number: routed_block(jax.random.fold_in(key_of[2], 2), own, number, TOK_DEV, EXPERTS, TOP, CAP, 1))(routes_keys, routes_turns).reshape((TOKENS, TOP))
    probs = jnp.clip(0.1 + 0.79999997 * jax.random.uniform(key_of[3], (TOKENS, TOP), jnp.float32) ** level_of(key_of[3], (TOKENS, TOP), ((0, 128),), -0.2, 0.2), 0.1, 0.9)
    w_gate = scatter_about(key_of[4], (VEXP, D, HID_DEV), D ** -0.5, 0.1875, ((0, 16),))
    w_up = scatter_about(key_of[5], (VEXP, D, HID_DEV), D ** -0.5, 0.1875, ((0, 16),))
    w_down = scatter_about(key_of[6], (VEXP, HID_DEV, D), HID_DEV ** -0.5, 0.25, ((0, 16),))
    res_gate = scatter_about(key_of[7], (N_DP, VEXP, D, HID_DEV), 1.0, 6.0, ((0, 8), (1, 16)))
    res_up = scatter_about(key_of[8], (N_DP, VEXP, D, HID_DEV), 1.0, 6.0, ((0, 8), (1, 16)))
    res_down = scatter_about(key_of[9], (N_DP, VEXP, HID_DEV, D), 0.25, 1.5, ((0, 8), (1, 16)))
    return dict(x_saved=x_saved, d_out=d_out, routes=routes, probs=probs, w_gate=w_gate, w_up=w_up, w_down=w_down, res_gate=res_gate, res_up=res_up, res_down=res_down)


loss_unscale = 0.0625
epsilon = 1e-5


def gate_terms(gate_pre):
    logistic = jax.nn.sigmoid(gate_pre)
    return gate_pre * logistic, logistic * (1.0 + gate_pre * (1.0 - logistic))


def expert_rows(saved_rows, cotangent_in, gate_weight, up_weight, down_weight):
    gate_pre = jnp.dot(saved_rows, gate_weight, preferred_element_type=jnp.float32)
    up_pre = jnp.dot(saved_rows, up_weight, preferred_element_type=jnp.float32)
    gate_act, gate_slope = gate_terms(gate_pre)
    hidden = (gate_act * up_pre).astype(jnp.bfloat16)
    grad_hidden = jnp.dot(cotangent_in, down_weight.T, preferred_element_type=jnp.float32)
    grad_a = (grad_hidden * up_pre * gate_slope).astype(jnp.bfloat16)
    grad_b = (grad_hidden * gate_act).astype(jnp.bfloat16)
    row_grads = (jnp.dot(grad_a, gate_weight.T, preferred_element_type=jnp.float32)
                 + jnp.dot(grad_b, up_weight.T, preferred_element_type=jnp.float32)).astype(jnp.bfloat16)
    grad_gate = loss_unscale * jnp.dot(saved_rows.T, grad_a, preferred_element_type=jnp.float32)
    grad_up = loss_unscale * jnp.dot(saved_rows.T, grad_b, preferred_element_type=jnp.float32)
    grad_down = loss_unscale * jnp.dot(hidden.T, cotangent_in, preferred_element_type=jnp.float32)
    return row_grads, grad_gate, grad_up, grad_down


def compress(local_grad, residual):
    carried = local_grad + residual.astype(jnp.float32)
    magnitude = jnp.mean(jnp.abs(carried), axis=-1, keepdims=True) + epsilon
    compressed = (magnitude * jnp.tanh(carried / magnitude)).astype(jnp.bfloat16)
    kept = lax.optimization_barrier(compressed)
    leftover = (carried - kept.astype(jnp.float32)).astype(jnp.bfloat16)
    return compressed, leftover


def reference(x_saved, d_out, routes, probs, w_gate, w_up, w_down, res_gate, res_up, res_down):
    route_count = TOK_DEV * TOP
    route_flat = routes.reshape(N_DP, N_EXPERT, route_count)
    route_weights = probs.reshape(N_DP, N_EXPERT, route_count)
    token_rows = d_out.reshape(N_DP, N_EXPERT, TOK_DEV, D)
    source = jnp.arange(N_EXPERT, dtype=jnp.int32)[:, None, None]
    labels = jnp.arange(EXPERTS, dtype=jnp.int32)
    shard_ids = jnp.arange(GROUP, dtype=jnp.int32)

    def replica(totals, inputs):
        routes_here, weights_here, rows_here, saved_here, resid_gate, resid_up, resid_down = inputs
        onehot = (routes_here[:, :, None] == labels).astype(jnp.int32)
        before = jnp.cumsum(onehot, axis=1) - onehot
        route_rank = jnp.sum(before * onehot, axis=2)
        shard_index = routes_here[:, :, None] * GROUP + shard_ids
        destination = (shard_index * SLOTS + source * CAP + route_rank[:, :, None]).reshape(-1).astype(jnp.int32)
        spread = jnp.repeat(rows_here.astype(jnp.float32), TOP, axis=1)
        scaled = (weights_here[:, :, None] * spread).astype(jnp.bfloat16)
        copies = jnp.broadcast_to(scaled[:, :, None, :], (N_EXPERT, route_count, GROUP, D)).reshape(-1, D)
        cotangent_in = jnp.zeros((VEXP * SLOTS, D), jnp.bfloat16).at[destination].set(copies)
        row_grads, grad_gate, grad_up, grad_down = lax.map(
            lambda expert_args: expert_rows(*expert_args),
            (saved_here, cotangent_in.reshape(VEXP, SLOTS, D), w_gate, w_up, w_down))
        picked = row_grads.reshape(VEXP * SLOTS, D)[destination].astype(jnp.float32)
        token_grads = jnp.sum(picked.reshape(N_EXPERT * TOK_DEV, TOP * GROUP, D), axis=1).astype(jnp.bfloat16)
        sent_gate, left_gate = compress(grad_gate, resid_gate)
        sent_up, left_up = compress(grad_up, resid_up)
        sent_down, left_down = compress(grad_down, resid_down)
        totals = (totals[0] + sent_gate.astype(jnp.float32),
                  totals[1] + sent_up.astype(jnp.float32),
                  totals[2] + sent_down.astype(jnp.float32))
        return totals, (token_grads, left_gate, left_up, left_down)

    initial = (jnp.zeros((VEXP, D, HID_DEV), jnp.float32),
               jnp.zeros((VEXP, D, HID_DEV), jnp.float32),
               jnp.zeros((VEXP, HID_DEV, D), jnp.float32))
    totals, outputs = lax.scan(replica, initial,
                               (route_flat, route_weights, token_rows, x_saved, res_gate, res_up, res_down))
    d_tokens = outputs[0].reshape(TOKENS, D)
    return (d_tokens, totals[0] / N_DP, totals[1] / N_DP, totals[2] / N_DP,
            outputs[1], outputs[2], outputs[3])
```

```python
import functools

import jax
import jax.numpy as jnp
from jax import lax
from jax.experimental import pallas as pl
from jax.experimental.pallas import tpu as pltpu
from jax.sharding import PartitionSpec as P

loss_unscale = 0.0625
epsilon = 1e-05

SIDE = 4
OFFSETS = (0, -1, 1, 2)
CAP = 80
TOK = 256
D = 1024
HID = 512
BF = jnp.bfloat16
F32 = jnp.float32
VMEM_LIMIT = 56 * 2**20


def expert_index(core, first, second):
    return jnp.where(core == 0, first * SIDE + second, second * SIDE + first)


def pairs(axis, step):
    out = []
    for dp in range(8):
        core = dp % 2
        for z in range(SIDE):
            for y in range(SIDE):
                along_z = (axis == 0) == (core == 0)
                z2, y2 = ((z + step) % SIDE, y) if along_z else (z, (y + step) % SIDE)
                out.append((dp * 16 + z * SIDE + y, dp * 16 + z2 * SIDE + y2))
    return out


def hop(value, axis, step):
    return lax.ppermute(value, ("dp", "expert"), pairs(axis, step))


def nt(left, right):
    return lax.dot_general(left, right, (((1,), (1,)), ((), ())), preferred_element_type=F32)


def forward_kernel(perm, *refs):
    xs, (wg, wu, xt, ht, m12, rows) = refs[:8], refs[8:]
    for i in range(8):
        rows[i * CAP : (i + 1) * CAP, :] = xs[i][0, 0]
    saved = rows[...]
    gate = jnp.dot(saved, wg[0], preferred_element_type=F32)
    up = jnp.dot(saved, wu[0], preferred_element_type=F32)
    logistic = jax.nn.sigmoid(gate)
    act = gate * logistic
    m12[0, :, :HID] = up * (logistic * (1.0 + gate * (1.0 - logistic)))
    m12[0, :, HID:] = act
    ht[0] = (act * up).astype(BF).T
    xt[0] = saved.T


def forward_terms(perm, x, wg, wu):
    blocks = x.reshape(2, 16, CAP, D)

    def block_at(i):
        return pl.BlockSpec((1, 1, CAP, D), lambda e, h, p: (e, p[8 * h + i], 0, 0))

    half = 8 * CAP
    return pl.pallas_call(
        forward_kernel,
        grid_spec=pltpu.PrefetchScalarGridSpec(
            num_scalar_prefetch=1,
            grid=(2, 2),
            in_specs=[block_at(i) for i in range(8)]
            + [pl.BlockSpec((1, D, HID), lambda e, h, p: (e, 0, 0))] * 2,
            out_specs=[
                pl.BlockSpec((1, D, half), lambda e, h, p: (e, 0, h)),
                pl.BlockSpec((1, HID, half), lambda e, h, p: (e, 0, h)),
                pl.BlockSpec((1, half, 2 * HID), lambda e, h, p: (e, h, 0)),
            ],
            scratch_shapes=[pltpu.VMEM((half, D), BF)],
        ),
        out_shape=[
            jax.ShapeDtypeStruct((2, D, 16 * CAP), BF),
            jax.ShapeDtypeStruct((2, HID, 16 * CAP), BF),
            jax.ShapeDtypeStruct((2, 16 * CAP, 2 * HID), F32),
        ],
        compiler_params=pltpu.CompilerParams(vmem_limit_bytes=VMEM_LIMIT),
        cost_estimate=pl.CostEstimate(flops=5_400_000_000, bytes_accessed=30_000_000, transcendentals=1_310_720),
        name="forward_terms",
    )(perm, *([blocks] * 8), wg, wu)


def slots_kernel(perm, first, meta, info):
    eid = first[0]
    before = (
        lax.broadcasted_iota(jnp.int32, (TOK, TOK), 0) < lax.broadcasted_iota(jnp.int32, (TOK, TOK), 1)
    ).astype(BF)
    for b in range(16):
        block = meta[perm[b]]
        routes, probs = block[:8], block[8:]
        named, weight = [], []
        for e in range(2):
            hit = routes == (eid + e).astype(F32)
            named.append(jnp.sum(jnp.where(hit, 1.0, 0.0), axis=0, keepdims=True))
            weight.append(jnp.sum(jnp.where(hit, probs, 0.0), axis=0, keepdims=True))
        mask = jnp.concatenate(named + [jnp.zeros((6, TOK), F32)], axis=0)
        rank = jnp.dot(mask.astype(BF), before, preferred_element_type=F32)
        key = jnp.where(mask > 0.5, rank, -1.0)
        info[b] = jnp.concatenate([key[:2], weight[0], weight[1], jnp.zeros((4, TOK), F32)], axis=0)


def slot_info(perm, first, meta):
    return pl.pallas_call(
        slots_kernel,
        in_specs=[
            pl.BlockSpec(memory_space=pltpu.SMEM),
            pl.BlockSpec(memory_space=pltpu.SMEM),
            pl.BlockSpec(memory_space=pltpu.VMEM),
        ],
        out_specs=pl.BlockSpec(memory_space=pltpu.VMEM),
        out_shape=jax.ShapeDtypeStruct((16, 8, TOK), F32),
        cost_estimate=pl.CostEstimate(flops=20_000_000, bytes_accessed=400_000, transcendentals=0),
        name="slot_info",
    )(perm, first, meta)


def group_kernel(parts, chained, *refs):
    tokens, refs = refs[:parts], refs[parts:]
    info, m12, wd, wg, wu = refs[:5]
    refs = refs[5 + (2 if chained else 0) :]
    cot, gab, partial, onehot, rows = refs
    e = pl.program_id(0)
    per = 4 // parts

    @pl.when(e == 0)
    def _():
        slot = lax.broadcasted_iota(jnp.int32, (CAP, TOK), 0).astype(F32)
        for i in range(4):
            halves, scales = [], []
            for k in range(2):
                hit = slot == info[i, k : k + 1, :]
                halves.append(jnp.where(hit, 1.0, 0.0).astype(BF))
                scales.append(jnp.sum(jnp.where(hit, info[i, 2 + k : 3 + k, :], 0.0), axis=1, keepdims=True))
            chosen = jnp.concatenate(halves, axis=0)
            onehot[i] = chosen
            source = tokens[i // per][(i % per) * TOK : (i % per + 1) * TOK, :]
            taken = jnp.dot(chosen, source, preferred_element_type=F32)
            scaled = (taken * jnp.concatenate(scales, axis=0)).astype(BF)
            cot[0, i * CAP : (i + 1) * CAP, :] = scaled[:CAP]
            cot[1, i * CAP : (i + 1) * CAP, :] = scaled[CAP:]

    grad_hidden = nt(cot[e], wd[0])
    grad_a = (grad_hidden * m12[0, :, :HID]).astype(BF)
    grad_b = (grad_hidden * m12[0, :, HID:]).astype(BF)
    gab[0, :, :HID] = grad_a
    gab[0, :, HID:] = grad_b
    row_grads = (nt(grad_a, wg[0]) + nt(grad_b, wu[0])).astype(BF)
    for i in range(4):
        rows[e, i] = row_grads[i * CAP : (i + 1) * CAP]

    @pl.when(e == 1)
    def _():
        for i in range(4):
            both = jnp.concatenate([rows[0, i], rows[1, i]], axis=0)
            partial[i * TOK : (i + 1) * TOK, :] = lax.dot_general(
                onehot[i], both, (((0,), (0,)), ((), ())), preferred_element_type=F32
            ).astype(BF)


def group_pass(group, tokens, info, m12, wd, wg, wu, carried):
    parts = len(tokens)
    group_rows = 4 * CAP
    any_spec = pl.BlockSpec(memory_space=pl.ANY)
    chained = carried is not None
    args = [*tokens, info, m12, wd, wg, wu] + (list(carried) if chained else [])
    slots = jax.ShapeDtypeStruct((2, 16 * CAP, D), BF)
    return pl.pallas_call(
        functools.partial(group_kernel, parts, chained),
        grid=(2,),
        in_specs=[pl.BlockSpec((4 * TOK // parts, D), lambda e: (0, 0))] * parts
        + [
            pl.BlockSpec((4, 8, TOK), lambda e: (group, 0, 0)),
            pl.BlockSpec((1, group_rows, 2 * HID), lambda e: (e, group, 0)),
            pl.BlockSpec((1, HID, D), lambda e: (e, 0, 0)),
            pl.BlockSpec((1, D, HID), lambda e: (e, 0, 0)),
            pl.BlockSpec((1, D, HID), lambda e: (e, 0, 0)),
        ]
        + ([any_spec, any_spec] if chained else []),
        out_specs=[
            pl.BlockSpec((2, group_rows, D), lambda e: (0, group, 0)),
            pl.BlockSpec((1, group_rows, D), lambda e: (e, group, 0)),
            pl.BlockSpec((4 * TOK, D), lambda e: (0, 0)),
        ],
        out_shape=[slots, slots, jax.ShapeDtypeStruct((4 * TOK, D), BF)],
        scratch_shapes=[pltpu.VMEM((4, 2 * CAP, TOK), BF), pltpu.VMEM((2, 4, CAP, D), BF)],
        input_output_aliases={parts + 5: 0, parts + 6: 1} if chained else {},
        compiler_params=pltpu.CompilerParams(vmem_limit_bytes=VMEM_LIMIT),
        cost_estimate=pl.CostEstimate(flops=2_700_000_000, bytes_accessed=18_000_000, transcendentals=0),
        name=f"group_{group}",
    )(*args)


def compress(local_grad, residual):
    carried = local_grad * loss_unscale + residual.astype(F32)
    magnitude = jnp.mean(jnp.abs(carried), axis=-1, keepdims=True) + epsilon
    compressed = (magnitude * jnp.tanh(carried * (1.0 / magnitude))).astype(BF)
    return compressed, (carried - compressed.astype(F32)).astype(BF)


def gate_up_kernel(xt, gab, res_gate, res_up, sent, left_gate, left_up):
    grads = jnp.dot(xt[0], gab[0], preferred_element_type=F32)
    for m, (res, left) in enumerate(((res_gate, left_gate), (res_up, left_up))):
        compressed, left[0] = compress(grads[:, m * HID : (m + 1) * HID], res[0])
        sent[0, m, 0] = compressed[:128]
        sent[1, m, 0] = compressed[128:]


def gate_up_grads(xt, gab, res_gate, res_up):
    tile = pl.BlockSpec((1, 256, HID), lambda e, t: (e, t, 0))
    res_shape = jax.ShapeDtypeStruct((2, D, HID), BF)
    return pl.pallas_call(
        gate_up_kernel,
        grid=(2, 4),
        in_specs=[
            pl.BlockSpec((1, 256, 16 * CAP), lambda e, t: (e, t, 0)),
            pl.BlockSpec((1, 16 * CAP, 2 * HID), lambda e, t: (e, 0, 0)),
            tile,
            tile,
        ],
        out_specs=[pl.BlockSpec((2, 2, 1, 128, HID), lambda e, t: (t, 0, e, 0, 0)), tile, tile],
        out_shape=[jax.ShapeDtypeStruct((8, 3, 2, 128, HID), BF), res_shape, res_shape],
        compiler_params=pltpu.CompilerParams(vmem_limit_bytes=VMEM_LIMIT),
        cost_estimate=pl.CostEstimate(flops=5_400_000_000, bytes_accessed=22_000_000, transcendentals=2_000_000),
        name="gate_up_grads",
    )(xt, gab, res_gate, res_up)


def down_kernel(ht, cot, res, _, sent, left):
    compressed, left[0] = compress(jnp.dot(ht[0], cot[0], preferred_element_type=F32), res[0])
    for owner in range(8):
        for q in range(2):
            sent[owner, 0, 0, :, q * 128 : (q + 1) * 128] = compressed[
                q * 128 : (q + 1) * 128, owner * 128 : (owner + 1) * 128
            ]


def down_grads(ht, cot, res, sent):
    tile = pl.BlockSpec((1, 256, D), lambda e, t: (e, t, 0))
    return pl.pallas_call(
        down_kernel,
        grid=(2, 2),
        in_specs=[
            pl.BlockSpec((1, 256, 16 * CAP), lambda e, t: (e, t, 0)),
            pl.BlockSpec((1, 16 * CAP, D), lambda e, t: (e, 0, 0)),
            tile,
            pl.BlockSpec(memory_space=pl.ANY),
        ],
        out_specs=[pl.BlockSpec((8, 1, 1, 128, 256), lambda e, t: (0, 2, e, 0, t)), tile],
        out_shape=[jax.ShapeDtypeStruct((8, 3, 2, 128, HID), BF), jax.ShapeDtypeStruct((2, HID, D), BF)],
        input_output_aliases={3: 0},
        compiler_params=pltpu.CompilerParams(vmem_limit_bytes=VMEM_LIMIT),
        cost_estimate=pl.CostEstimate(flops=2_700_000_000, bytes_accessed=14_000_000, transcendentals=1_000_000),
        name="down_grads",
    )(ht, cot, res, sent)


def add(*terms):
    total = terms[0].astype(F32)
    for term in terms[1:]:
        total = total + term.astype(F32)
    return total.astype(BF)


def on_device(x_saved, d_out, routes, probs, w_gate, w_up, w_down, res_gate, res_up, res_down):
    place = lax.axis_index("expert")
    core = lax.axis_index("dp") % 2
    first = jnp.where(core == 0, place // SIDE, place % SIDE)
    second = jnp.where(core == 0, place % SIDE, place // SIDE)
    offsets = jnp.array(OFFSETS, jnp.int32)
    perm = expert_index(
        core, ((first + offsets) % SIDE)[None, :], ((second + offsets) % SIDE)[:, None]
    ).reshape(-1).astype(jnp.int32)

    near_plus, near_minus = hop(d_out, 0, 1), hop(d_out, 0, -1)
    far_plus, far_minus = hop(near_plus[:128], 0, 1), hop(near_minus[128:], 0, -1)
    group0 = jnp.concatenate([d_out, near_plus, near_minus, far_plus, far_minus], axis=0)
    group1, group2 = hop(group0, 1, 1), hop(group0, 1, -1)
    group3 = (hop(group1[:512], 1, 1), hop(group2[512:], 1, -1))

    meta = lax.all_gather(
        jnp.concatenate([routes.astype(F32).T, probs.T], axis=0), "expert", axis=0, tiled=False
    )
    info = slot_info(perm, (place * 2).astype(jnp.int32).reshape(1), meta)
    xt, ht, m12 = forward_terms(perm, x_saved[0], w_gate, w_up)

    run = functools.partial(group_pass, info=info, m12=m12, wd=w_down, wg=w_gate, wu=w_up)
    cot, gab, part0 = run(0, (group0,), carried=None)
    cot, gab, part1 = run(1, (group1,), carried=(cot, gab))
    cot, gab, part2 = run(2, (group2,), carried=(cot, gab))
    cot, gab, part3 = run(3, group3, carried=(cot, gab))

    over_plus, over_minus = hop(part3[:512], 1, 1), hop(part3[512:], 1, -1)
    to_plus = jnp.concatenate([add(part2[:512], over_plus), part2[512:]], axis=0)
    to_minus = jnp.concatenate([part1[:512], add(part1[512:], over_minus)], axis=0)
    column = add(part0, hop(to_plus, 1, 1), hop(to_minus, 1, -1))
    over_plus, over_minus = hop(column[768:896], 0, 1), hop(column[896:], 0, -1)
    to_plus = jnp.concatenate([add(column[512:640], over_plus), column[640:768]], axis=0)
    to_minus = jnp.concatenate([column[256:384], add(column[384:512], over_minus)], axis=0)
    d_tokens = add(column[:256], hop(to_plus, 0, 1), hop(to_minus, 0, -1))

    sent, left_gate, left_up = gate_up_grads(xt, gab, res_gate[0], res_up[0])
    sent, left_down = down_grads(ht, cot, res_down[0], sent)
    total = lax.psum_scatter(sent.reshape(8 * 3 * 2 * 128, HID), "dp", scatter_dimension=0, tiled=True)
    mean = total.reshape(3, 2, 128, HID).astype(F32) / 8.0
    mean_down = mean[2].reshape(2, 128, 4, 128).transpose(0, 2, 1, 3).reshape(2, HID, 128)
    return (d_tokens, mean[0], mean[1], mean_down, left_gate[None], left_up[None], left_down[None])


def solution(mesh):
    in_specs = (
        P("dp", "expert", None, None),
        P(("dp", "expert"), None),
        P(("dp", "expert"), None),
        P(("dp", "expert"), None),
        P("expert", None, None),
        P("expert", None, None),
        P("expert", None, None),
        P("dp", "expert", None, None),
        P("dp", "expert", None, None),
        P("dp", "expert", None, None),
    )
    out_specs = (
        P(("dp", "expert"), None),
        P("expert", "dp", None),
        P("expert", "dp", None),
        P("expert", None, "dp"),
        P("dp", "expert", None, None),
        P("dp", "expert", None, None),
        P("dp", "expert", None, None),
    )
    return jax.shard_map(
        on_device, mesh=mesh, in_specs=in_specs, out_specs=out_specs, check_vma=False
    )
```

```python
import functools

import jax
import jax.numpy as jnp
from jax import lax
from jax.experimental import pallas as pl
from jax.experimental.pallas import tpu as pltpu
from jax.sharding import PartitionSpec as P

loss_unscale = 0.0625
epsilon = 1e-05

SIDE = 4
OFFSETS = (0, -1, 1, 2)
CAP = 80
TOK = 256
PACK = TOK + 16
D = 1024
HID = 512
BF = jnp.bfloat16
F32 = jnp.float32
VMEM_LIMIT = 56 * 2**20


def expert_index(core, first, second):
    return jnp.where(core == 0, first * SIDE + second, second * SIDE + first)


def pairs(axis, step):
    out = []
    for dp in range(8):
        core = dp % 2
        for z in range(SIDE):
            for y in range(SIDE):
                along_z = (axis == 0) == (core == 0)
                z2, y2 = ((z + step) % SIDE, y) if along_z else (z, (y + step) % SIDE)
                out.append((dp * 16 + z * SIDE + y, dp * 16 + z2 * SIDE + y2))
    return out


def hop(value, axis, step):
    return lax.ppermute(value, ("dp", "expert"), pairs(axis, step))


def dp_hop(value, move):
    return lax.ppermute(
        value, "dp", [(x * 2 + c, move(x, c)[0] % SIDE * 2 + move(x, c)[1]) for x in range(SIDE) for c in range(2)]
    )


def nt(left, right):
    return lax.dot_general(left, right, (((1,), (1,)), ((), ())), preferred_element_type=F32)


def pack_kernel(tokens, routes, probs, out):
    out[:TOK, :] = tokens[...]
    weights = probs[...].T
    high = weights.astype(BF)
    left = weights - high.astype(F32)
    middle = left.astype(BF)
    low = (left - middle.astype(F32)).astype(BF)
    out[TOK : TOK + 8, :] = jnp.concatenate(
        [routes[...].astype(F32).T.astype(BF), high, middle, low], axis=1
    )
    out[TOK + 8 :, :] = jnp.zeros((8, D), BF)


def pack(tokens, routes, probs):
    return pl.pallas_call(
        pack_kernel,
        out_shape=jax.ShapeDtypeStruct((PACK, D), BF),
        cost_estimate=pl.CostEstimate(flops=0, bytes_accessed=1_100_000, transcendentals=0),
        name="pack",
    )(tokens, routes, probs)


def forward_kernel(chained, perm, *refs):
    xs, (wg, wu), refs = refs[:8], refs[8:10], refs[10 + (3 if chained else 0) :]
    xt, ht, m12, rows = refs
    for i in range(8):
        rows[i * CAP : (i + 1) * CAP, :] = xs[i][0, 0]
    half = 4 * CAP
    pre = []
    for h in range(2):
        saved = rows[h * half : (h + 1) * half, :]
        pre.append(
            (
                jnp.dot(saved, wg[0], preferred_element_type=F32),
                jnp.dot(saved, wu[0], preferred_element_type=F32),
            )
        )
    xt[0] = rows[...].T
    hidden = []
    for h, (gate, up) in enumerate(pre):
        logistic = jax.nn.sigmoid(gate)
        act = gate * logistic
        m12[0, h * half : (h + 1) * half, :HID] = up * (logistic * (1.0 + gate * (1.0 - logistic)))
        m12[0, h * half : (h + 1) * half, HID:] = act
        hidden.append((act * up).astype(BF))
    ht[0] = jnp.concatenate(hidden, axis=0).T


def forward_terms(e, perm, x, wg, wu, carried):
    blocks = x.reshape(2, 16, CAP, D)
    chained = carried is not None

    def block_at(i):
        return pl.BlockSpec((1, 1, CAP, D), lambda h, p: (e, p[8 * h + i], 0, 0))

    half = 8 * CAP
    return pl.pallas_call(
        functools.partial(forward_kernel, chained),
        grid_spec=pltpu.PrefetchScalarGridSpec(
            num_scalar_prefetch=1,
            grid=(2,),
            in_specs=[block_at(i) for i in range(8)]
            + [pl.BlockSpec((1, D, HID), lambda h, p: (e, 0, 0))] * 2
            + [pl.BlockSpec(memory_space=pl.ANY)] * (3 if chained else 0),
            out_specs=[
                pl.BlockSpec((1, D, half), lambda h, p: (e, 0, h)),
                pl.BlockSpec((1, HID, half), lambda h, p: (e, 0, h)),
                pl.BlockSpec((1, half, 2 * HID), lambda h, p: (e, h, 0)),
            ],
            scratch_shapes=[pltpu.VMEM((half, D), BF)],
        ),
        out_shape=[
            jax.ShapeDtypeStruct((2, D, 16 * CAP), BF),
            jax.ShapeDtypeStruct((2, HID, 16 * CAP), BF),
            jax.ShapeDtypeStruct((2, 16 * CAP, 2 * HID), F32),
        ],
        input_output_aliases={11 + i: i for i in range(3)} if chained else {},
        compiler_params=pltpu.CompilerParams(vmem_limit_bytes=VMEM_LIMIT),
        cost_estimate=pl.CostEstimate(flops=2_700_000_000, bytes_accessed=15_000_000, transcendentals=655_360),
        name="forward_terms",
    )(perm, *([blocks] * 8), wg, wu, *(carried or ()))


def groups_kernel(groups, pieces, chained, eid, *refs):
    count, lent = len(groups), sum(len(p) for p in pieces)
    tokens, refs = refs[:lent], refs[lent:]
    m12, wd, wg, wu = refs[:4]
    refs = refs[4 + (2 if chained else 0) :]
    cot, gab, partials, refs = refs[0], refs[1], refs[2 : 2 + 2 * count], refs[2 + 2 * count :]
    tok_v, m12_v, wd_v, wg_v, wu_v, cot_v, gab_v, part_v, onehot, rows, sem_in, sem_out = refs

    loads, token_loads, factor_loads, at = [], [], [], 0

    def load(source, target):
        loads.append(pltpu.make_async_copy(source, target, sem_in.at[len(loads)]))
        loads[-1].start()
        return loads[-1]

    weight_loads = None
    for n, group in enumerate(groups):
        offset, mine = 0, []
        for height in pieces[n]:
            mine.append(load(tokens[at], tok_v.at[n, pl.ds(offset, height)]))
            at, offset = at + 1, offset + height
        token_loads.append(mine)
        if n == 0:
            down_load = load(wd, wd_v)
        factor_loads.append(load(m12.at[:, pl.ds(group * 4 * CAP, 4 * CAP)], m12_v.at[n]))
        if n == 0:
            weight_loads = [load(wg, wg_v), load(wu, wu_v)]

    stores = []

    def store(source, target):
        stores.append(pltpu.make_async_copy(source, target, sem_out.at[len(stores)]))
        stores[-1].start()

    before = (
        lax.broadcasted_iota(jnp.int32, (TOK, TOK), 0) < lax.broadcasted_iota(jnp.int32, (TOK, TOK), 1)
    ).astype(BF)
    slot = lax.broadcasted_iota(jnp.int32, (CAP, TOK), 0).astype(F32)
    for n, group in enumerate(groups):
        for item in token_loads[n]:
            item.wait()
        named, weights = [], []
        for i in range(4):
            meta = tok_v[n, i * PACK + TOK : (i + 1) * PACK, :].astype(F32)[:8]
            routes = meta[:, :TOK]
            probs = meta[:, TOK : 2 * TOK] + meta[:, 2 * TOK : 3 * TOK] + meta[:, 3 * TOK :]
            for k in range(2):
                hit = routes == (eid[0] + k).astype(F32)
                named.append(jnp.sum(jnp.where(hit, 1.0, 0.0), axis=0, keepdims=True))
                weights.append(jnp.sum(jnp.where(hit, probs, 0.0), axis=0, keepdims=True))
        mask = jnp.concatenate(named, axis=0)
        rank = jnp.dot(mask.astype(BF), before, preferred_element_type=F32)
        key = jnp.where(mask > 0.5, rank, -1.0)
        for i in range(4):
            halves, scales = [], []
            for k in range(2):
                hit = slot == key[2 * i + k : 2 * i + k + 1, :]
                halves.append(jnp.where(hit, 1.0, 0.0).astype(BF))
                scales.append(jnp.sum(jnp.where(hit, weights[2 * i + k], 0.0), axis=1, keepdims=True))
            chosen = jnp.concatenate(halves, axis=0)
            onehot[i] = chosen
            taken = jnp.dot(chosen, tok_v[n, i * PACK : i * PACK + TOK, :], preferred_element_type=F32)
            scaled = (taken * jnp.concatenate(scales, axis=0)).astype(BF)
            cot_v[n, 0, i * CAP : (i + 1) * CAP, :] = scaled[:CAP]
            cot_v[n, 1, i * CAP : (i + 1) * CAP, :] = scaled[CAP:]
        place = pl.ds(group * 4 * CAP, 4 * CAP)
        store(cot_v.at[n], cot.at[:, place])
        if n == 0:
            down_load.wait()
        factor_loads[n].wait()
        for e in range(2):
            grad_hidden = nt(cot_v[n, e], wd_v[e])
            gab_v[n, e, :, :HID] = (grad_hidden * m12_v[n, e, :, :HID]).astype(BF)
            gab_v[n, e, :, HID:] = (grad_hidden * m12_v[n, e, :, HID:]).astype(BF)
        store(gab_v.at[n], gab.at[:, place])
        if n == 0:
            for item in weight_loads:
                item.wait()
        for e in range(2):
            row_grads = (nt(gab_v[n, e, :, :HID], wg_v[e]) + nt(gab_v[n, e, :, HID:], wu_v[e])).astype(BF)
            for i in range(4):
                rows[i, e * CAP : (e + 1) * CAP, :] = row_grads[i * CAP : (i + 1) * CAP]
        for i in range(4):
            part_v[n, i * TOK : (i + 1) * TOK, :] = lax.dot_general(
                onehot[i], rows[i], (((0,), (0,)), ((), ())), preferred_element_type=F32
            ).astype(BF)
            if i % 2 == 1:
                store(part_v.at[n, pl.ds((i - 1) * TOK, 2 * TOK)], partials[2 * n + i // 2])
    for item in stores:
        item.wait()


def groups_pass(groups, tokens, eid, m12, wd, wg, wu, carried):
    chained = carried is not None
    count = len(groups)
    pieces = [[t.shape[0] for t in mine] for mine in tokens]
    lent = sum(len(p) for p in pieces)
    anywhere = pl.BlockSpec(memory_space=pl.ANY)
    slots = jax.ShapeDtypeStruct((2, 16 * CAP, D), BF)
    args = [t for mine in tokens for t in mine] + [m12, wd, wg, wu] + (list(carried) if chained else [])
    out = pl.pallas_call(
        functools.partial(groups_kernel, groups, pieces, chained),
        in_specs=[pl.BlockSpec(memory_space=pltpu.SMEM)] + [anywhere] * len(args),
        out_specs=[anywhere] * (2 + 2 * count),
        out_shape=[slots, slots] + [jax.ShapeDtypeStruct((2 * TOK, D), BF)] * (2 * count),
        scratch_shapes=[
            pltpu.VMEM((count, 4 * PACK, D), BF),
            pltpu.VMEM((count, 2, 4 * CAP, 2 * HID), F32),
            pltpu.VMEM((2, HID, D), BF),
            pltpu.VMEM((2, D, HID), BF),
            pltpu.VMEM((2, D, HID), BF),
            pltpu.VMEM((count, 2, 4 * CAP, D), BF),
            pltpu.VMEM((count, 2, 4 * CAP, 2 * HID), BF),
            pltpu.VMEM((count, 4 * TOK, D), BF),
            pltpu.VMEM((4, 2 * CAP, TOK), BF),
            pltpu.VMEM((4, 2 * CAP, D), BF),
            pltpu.SemaphoreType.DMA((lent + 3 + count,)),
            pltpu.SemaphoreType.DMA((4 * count,)),
        ],
        input_output_aliases={lent + 5: 0, lent + 6: 1} if chained else {},
        compiler_params=pltpu.CompilerParams(vmem_limit_bytes=VMEM_LIMIT),
        cost_estimate=pl.CostEstimate(
            flops=2_900_000_000 * count, bytes_accessed=6_000_000 + 9_000_000 * count, transcendentals=0
        ),
        name="groups_" + "".join(str(g) for g in groups),
    )(eid, *args)
    return out[0], out[1], out[2:]


def compress(local_grad, residual):
    carried = local_grad * loss_unscale + residual.astype(F32)
    magnitude = jnp.mean(jnp.abs(carried), axis=-1, keepdims=True) + epsilon
    compressed = (magnitude * jnp.tanh(carried * (1.0 / magnitude))).astype(BF)
    return compressed, (carried - compressed.astype(F32)).astype(BF)


def gate_up_kernel(spot, xt, gab, res_gate, res_up, keep, give, left_gate, left_up, held):
    core = spot[4]
    half = pl.program_id(1)
    grads = [jnp.dot(xt[0, u * 256 : (u + 1) * 256], gab[0], preferred_element_type=F32) for u in range(2)]
    for u in range(2):
        rows = slice(u * 256, (u + 1) * 256)
        at = spot[2 * half + u]
        for m, (res, left) in enumerate(((res_gate, left_gate), (res_up, left_up))):
            held[u, m], left[0, rows] = compress(grads[u][:, m * HID : (m + 1) * HID], res[0, rows])
            keep[at, m, 0] = held[u, m, pl.ds(pl.multiple_of(core * 128, 128), 128)]
            give[at, m, 0] = held[u, m, pl.ds(pl.multiple_of((1 - core) * 128, 128), 128)]


def gate_up_grads(spot, xt, gab, res_gate, res_up):
    tile = pl.BlockSpec((1, HID, HID), lambda e, t, s: (e, t, 0))
    res_shape = jax.ShapeDtypeStruct((2, D, HID), BF)
    blocks = jax.ShapeDtypeStruct((SIDE, 2, 2, 128, HID), BF)
    return pl.pallas_call(
        gate_up_kernel,
        grid_spec=pltpu.PrefetchScalarGridSpec(
            num_scalar_prefetch=1,
            grid=(2, 2),
            in_specs=[
                pl.BlockSpec((1, 512, 16 * CAP), lambda e, t, s: (e, t, 0)),
                pl.BlockSpec((1, 16 * CAP, 2 * HID), lambda e, t, s: (e, 0, 0)),
                tile,
                tile,
            ],
            out_specs=[pl.BlockSpec((SIDE, 2, 1, 128, HID), lambda e, t, s: (0, 0, e, 0, 0))] * 2 + [tile, tile],
            scratch_shapes=[pltpu.VMEM((2, 2, 256, HID), BF)],
        ),
        out_shape=[blocks, blocks, res_shape, res_shape],
        compiler_params=pltpu.CompilerParams(vmem_limit_bytes=VMEM_LIMIT),
        cost_estimate=pl.CostEstimate(flops=5_400_000_000, bytes_accessed=22_000_000, transcendentals=2_000_000),
        name="gate_up_grads",
    )(spot, xt, gab, res_gate, res_up)


def down_kernel(spot, ht, cot, res, keep, give, left):
    core = spot[4]
    grads = [jnp.dot(ht[0, u * 256 : (u + 1) * 256], cot[0], preferred_element_type=F32) for u in range(2)]
    for u in range(2):
        rows = slice(u * 256, (u + 1) * 256)
        compressed, left[0, rows] = compress(grads[u], res[0, rows])
        for own in range(2):

            @pl.when(core == own)
            def _():
                for x in range(SIDE):
                    keep[spot[x], 0, rows] = compressed[:, (2 * x + own) * 128 : (2 * x + own + 1) * 128]
                    give[spot[x], 0, rows] = compressed[:, (2 * x + 1 - own) * 128 : (2 * x + 2 - own) * 128]


def down_grads(spot, ht, cot, res):
    tile = pl.BlockSpec((1, HID, D), lambda e, s: (e, 0, 0))
    blocks = jax.ShapeDtypeStruct((SIDE, 2, HID, 128), BF)
    return pl.pallas_call(
        down_kernel,
        grid_spec=pltpu.PrefetchScalarGridSpec(
            num_scalar_prefetch=1,
            grid=(2,),
            in_specs=[
                pl.BlockSpec((1, HID, 16 * CAP), lambda e, s: (e, 0, 0)),
                pl.BlockSpec((1, 16 * CAP, D), lambda e, s: (e, 0, 0)),
                tile,
            ],
            out_specs=[pl.BlockSpec((SIDE, 1, HID, 128), lambda e, s: (0, e, 0, 0))] * 2 + [tile],
        ),
        out_shape=[blocks, blocks, jax.ShapeDtypeStruct((2, HID, D), BF)],
        compiler_params=pltpu.CompilerParams(vmem_limit_bytes=VMEM_LIMIT),
        cost_estimate=pl.CostEstimate(flops=2_700_000_000, bytes_accessed=14_000_000, transcendentals=1_000_000),
        name="down_grads",
    )(spot, ht, cot, res)


def total(*terms):
    out = terms[0].astype(F32)
    for term in terms[1:]:
        out = out + term.astype(F32)
    return out


def add(*terms):
    return total(*terms).astype(BF)


def mean_over_dp(keep, give):
    got = dp_hop(give, lambda x, c: (x, 1 - c))
    to_minus = dp_hop(add(keep[1], got[1]), lambda x, c: (x - 1, c))
    to_plus = dp_hop(add(keep[2], got[2]), lambda x, c: (x + 1, c))
    to_far = dp_hop(add(keep[3], got[3]), lambda x, c: (x + 2, c))
    return total(keep[0], got[0], to_minus, to_plus, to_far) / 8.0


def on_device(x_saved, d_out, routes, probs, w_gate, w_up, w_down, res_gate, res_up, res_down):
    place = lax.axis_index("expert")
    replica = lax.axis_index("dp")
    x, core = replica // 2, replica % 2
    first = jnp.where(core == 0, place // SIDE, place % SIDE)
    second = jnp.where(core == 0, place % SIDE, place // SIDE)
    offsets = jnp.array(OFFSETS, jnp.int32)
    perm = expert_index(
        core, ((first + offsets) % SIDE)[None, :], ((second + offsets) % SIDE)[:, None]
    ).reshape(-1).astype(jnp.int32)
    where_held = jnp.array([OFFSETS.index(o) for o in (0, 1, 2, -1)], jnp.int32)
    spot = jnp.concatenate([where_held[(jnp.arange(SIDE) - x) % SIDE], core[None]]).astype(jnp.int32)
    eid = (place * 2).astype(jnp.int32).reshape(1)

    own = pack(d_out, routes, probs)
    rest = jnp.concatenate([hop(own, 0, 1), hop(own, 0, -1), hop(own, 0, 2)], axis=0)
    own1, own2 = hop(own, 1, 1), hop(own, 1, -1)
    rest1, rest2 = hop(rest, 1, 1), hop(rest, 1, -1)
    group3 = (
        hop(jnp.concatenate([own1, rest1[:PACK]], axis=0), 1, 1),
        hop(rest2[PACK:], 1, -1),
    )

    terms = forward_terms(0, perm, x_saved[0], w_gate, w_up, None)
    xt, ht, m12 = forward_terms(1, perm, x_saved[0], w_gate, w_up, terms)

    run = functools.partial(groups_pass, eid=eid, m12=m12, wd=w_down, wg=w_gate, wu=w_up)
    cot, gab, (part0a, part0b) = run((0,), [(own, rest)], carried=None)
    cot, gab, (part1a, part1b, part2a, part2b) = run(
        (1, 2), [(own1, rest1), (own2, rest2)], carried=(cot, gab)
    )
    cot, gab, (part3a, part3b) = run((3,), [group3], carried=(cot, gab))

    direct_plus, direct_minus = hop(part2b, 1, 1), hop(part1a, 1, -1)
    over_plus, over_minus = hop(part3a, 1, 1), hop(part3b, 1, -1)
    late_plus, late_minus = hop(add(part2a, over_plus), 1, 1), hop(add(part1b, over_minus), 1, -1)

    def column(i):
        part = slice(i % 2 * TOK, (i % 2 + 1) * TOK)
        terms = (part0a, late_plus, direct_minus) if i < 2 else (part0b, direct_plus, late_minus)
        return total(*(t[part] for t in terms))

    d_tokens = add(
        column(0),
        hop(column(2).astype(BF), 0, 1),
        hop(column(1).astype(BF), 0, -1),
        hop(column(3).astype(BF), 0, 2),
    )

    keep, give, left_gate, left_up = gate_up_grads(spot, xt, gab, res_gate[0], res_up[0])
    mean = mean_over_dp(keep, give)
    keep, give, left_down = down_grads(spot, ht, cot, res_down[0])
    mean_down = mean_over_dp(keep, give)
    return (d_tokens, mean[0], mean[1], mean_down, left_gate[None], left_up[None], left_down[None])


def solution(mesh):
    in_specs = (
        P("dp", "expert", None, None),
        P(("dp", "expert"), None),
        P(("dp", "expert"), None),
        P(("dp", "expert"), None),
        P("expert", None, None),
        P("expert", None, None),
        P("expert", None, None),
        P("dp", "expert", None, None),
        P("dp", "expert", None, None),
        P("dp", "expert", None, None),
    )
    out_specs = (
        P(("dp", "expert"), None),
        P("expert", "dp", None),
        P("expert", "dp", None),
        P("expert", None, "dp"),
        P("dp", "expert", None, None),
        P("dp", "expert", None, None),
        P("dp", "expert", None, None),
    )
    return jax.shard_map(
        on_device, mesh=mesh, in_specs=in_specs, out_specs=out_specs, check_vma=False
    )
```

```python
import functools

import jax
import jax.numpy as jnp
from jax import lax
from jax.experimental import pallas as pl
from jax.experimental.pallas import tpu as pltpu
from jax.sharding import PartitionSpec as P

loss_unscale = 0.0625
epsilon = 1e-05

SIDE = 4
OFFSETS = (0, -1, 1, 2)
CAP = 80
TOK = 256
PACK = TOK + 16
D = 1024
HID = 512
BF = jnp.bfloat16
F32 = jnp.float32
VMEM_LIMIT = 56 * 2**20


def expert_index(core, first, second):
    return jnp.where(core == 0, first * SIDE + second, second * SIDE + first)


def pairs(axis, step):
    out = []
    for dp in range(8):
        core = dp % 2
        for z in range(SIDE):
            for y in range(SIDE):
                along_z = (axis == 0) == (core == 0)
                z2, y2 = ((z + step) % SIDE, y) if along_z else (z, (y + step) % SIDE)
                out.append((dp * 16 + z * SIDE + y, dp * 16 + z2 * SIDE + y2))
    return out


def hop(value, axis, step):
    return lax.ppermute(value, ("dp", "expert"), pairs(axis, step))


def dp_hop(value, move):
    return lax.ppermute(
        value, "dp", [(x * 2 + c, move(x, c)[0] % SIDE * 2 + move(x, c)[1]) for x in range(SIDE) for c in range(2)]
    )


def nt(left, right):
    return lax.dot_general(left, right, (((1,), (1,)), ((), ())), preferred_element_type=F32)


def pack_kernel(tokens, routes, probs, out):
    out[:TOK, :] = tokens[...]
    weights = probs[...]
    high = weights.astype(BF)
    left = weights - high.astype(F32)
    middle = left.astype(BF)
    low = (left - middle.astype(F32)).astype(BF)
    out[TOK : TOK + 8, :] = jnp.concatenate(
        [routes[...].astype(F32).astype(BF), high, middle, low], axis=1
    )
    out[TOK + 8 :, :] = jnp.zeros((8, D), BF)


def pack(tokens, routes, probs):
    return pl.pallas_call(
        pack_kernel,
        out_shape=jax.ShapeDtypeStruct((PACK, D), BF),
        cost_estimate=pl.CostEstimate(flops=0, bytes_accessed=1_100_000, transcendentals=0),
        name="pack",
    )(tokens, routes.T, probs.T)


def forward_kernel(chained, perm, *refs):
    xs, (wg, wu), refs = refs[:8], refs[8:10], refs[10 + (3 if chained else 0) :]
    xt, ht, m12, rows = refs
    for i in range(8):
        rows[i * CAP : (i + 1) * CAP, :] = xs[i][0, 0]
    half = 4 * CAP
    pre = []
    for h in range(2):
        saved = rows[h * half : (h + 1) * half, :]
        pre.append(
            (
                jnp.dot(saved, wg[0], preferred_element_type=F32),
                jnp.dot(saved, wu[0], preferred_element_type=F32),
            )
        )
    xt[0] = rows[...].T
    hidden = []
    for h, (gate, up) in enumerate(pre):
        logistic = jax.nn.sigmoid(gate)
        act = gate * logistic
        m12[0, h * half : (h + 1) * half, :HID] = up * (logistic * (1.0 + gate * (1.0 - logistic)))
        m12[0, h * half : (h + 1) * half, HID:] = act
        hidden.append((act * up).astype(BF))
    ht[0] = jnp.concatenate(hidden, axis=0).T


def forward_terms(e, perm, x, wg, wu, carried):
    blocks = x.reshape(2, 16, CAP, D)
    chained = carried is not None

    def block_at(i):
        return pl.BlockSpec((1, 1, CAP, D), lambda h, p: (e, p[8 * h + i], 0, 0))

    half = 8 * CAP
    return pl.pallas_call(
        functools.partial(forward_kernel, chained),
        grid_spec=pltpu.PrefetchScalarGridSpec(
            num_scalar_prefetch=1,
            grid=(2,),
            in_specs=[block_at(i) for i in range(8)]
            + [pl.BlockSpec((1, D, HID), lambda h, p: (e, 0, 0))] * 2
            + [pl.BlockSpec(memory_space=pl.ANY)] * (3 if chained else 0),
            out_specs=[
                pl.BlockSpec((1, D, half), lambda h, p: (e, 0, h)),
                pl.BlockSpec((1, HID, half), lambda h, p: (e, 0, h)),
                pl.BlockSpec((1, half, 2 * HID), lambda h, p: (e, h, 0)),
            ],
            scratch_shapes=[pltpu.VMEM((half, D), BF)],
        ),
        out_shape=[
            jax.ShapeDtypeStruct((2, D, 16 * CAP), BF),
            jax.ShapeDtypeStruct((2, HID, 16 * CAP), BF),
            jax.ShapeDtypeStruct((2, 16 * CAP, 2 * HID), F32),
        ],
        input_output_aliases={11 + i: i for i in range(3)} if chained else {},
        compiler_params=pltpu.CompilerParams(vmem_limit_bytes=VMEM_LIMIT),
        cost_estimate=pl.CostEstimate(flops=2_700_000_000, bytes_accessed=15_000_000, transcendentals=655_360),
        name="forward_terms",
    )(perm, *([blocks] * 8), wg, wu, *(carried or ()))


def groups_kernel(groups, pieces, chained, eid, *refs):
    count, lent = len(groups), sum(len(p) for p in pieces)
    tokens, refs = refs[:lent], refs[lent:]
    m12, wd, wg, wu = refs[:4]
    refs = refs[4 + (2 if chained else 0) :]
    cot, gab, partials, refs = refs[0], refs[1], refs[2 : 2 + 2 * count], refs[2 + 2 * count :]
    tok_v, m12_v, wd_v, wg_v, wu_v, cot_v, gab_v, part_v, onehot, rows, sem_in, sem_out = refs

    loads, token_loads, factor_loads, at = [], [], [], 0

    def load(source, target):
        loads.append(pltpu.make_async_copy(source, target, sem_in.at[len(loads)]))
        loads[-1].start()
        return loads[-1]

    weight_loads = None
    for n, group in enumerate(groups):
        offset, mine = 0, []
        for height in pieces[n]:
            mine.append(load(tokens[at], tok_v.at[n, pl.ds(offset, height)]))
            at, offset = at + 1, offset + height
        token_loads.append(mine)
        if n == 0:
            down_load = load(wd, wd_v)
        factor_loads.append(load(m12.at[:, pl.ds(group * 4 * CAP, 4 * CAP)], m12_v.at[n]))
        if n == 0:
            weight_loads = [load(wg, wg_v), load(wu, wu_v)]

    stores = []

    def store(source, target):
        stores.append(pltpu.make_async_copy(source, target, sem_out.at[len(stores)]))
        stores[-1].start()

    before = (
        lax.broadcasted_iota(jnp.int32, (TOK, TOK), 0) < lax.broadcasted_iota(jnp.int32, (TOK, TOK), 1)
    ).astype(BF)
    slot = lax.broadcasted_iota(jnp.int32, (CAP, TOK), 0).astype(F32)
    for n, group in enumerate(groups):
        for item in token_loads[n]:
            item.wait()
        named, weights = [], []
        for i in range(4):
            meta = tok_v[n, i * PACK + TOK : (i + 1) * PACK, :].astype(F32)[:8]
            routes = meta[:, :TOK]
            probs = meta[:, TOK : 2 * TOK] + meta[:, 2 * TOK : 3 * TOK] + meta[:, 3 * TOK :]
            for k in range(2):
                hit = routes == (eid[0] + k).astype(F32)
                named.append(jnp.sum(jnp.where(hit, 1.0, 0.0), axis=0, keepdims=True))
                weights.append(jnp.sum(jnp.where(hit, probs, 0.0), axis=0, keepdims=True))
        mask = jnp.concatenate(named, axis=0)
        rank = jnp.dot(mask.astype(BF), before, preferred_element_type=F32)
        key = jnp.where(mask > 0.5, rank, -1.0)
        for i in range(4):
            halves, scales = [], []
            for k in range(2):
                hit = slot == key[2 * i + k : 2 * i + k + 1, :]
                halves.append(jnp.where(hit, 1.0, 0.0).astype(BF))
                scales.append(jnp.sum(jnp.where(hit, weights[2 * i + k], 0.0), axis=1, keepdims=True))
            chosen = jnp.concatenate(halves, axis=0)
            onehot[i] = chosen
            taken = jnp.dot(chosen, tok_v[n, i * PACK : i * PACK + TOK, :], preferred_element_type=F32)
            scaled = (taken * jnp.concatenate(scales, axis=0)).astype(BF)
            cot_v[n, 0, i * CAP : (i + 1) * CAP, :] = scaled[:CAP]
            cot_v[n, 1, i * CAP : (i + 1) * CAP, :] = scaled[CAP:]
        place = pl.ds(group * 4 * CAP, 4 * CAP)
        store(cot_v.at[n], cot.at[:, place])
        if n == 0:
            down_load.wait()
        factor_loads[n].wait()
        for e in range(2):
            grad_hidden = nt(cot_v[n, e], wd_v[e])
            gab_v[n, e, :, :HID] = (grad_hidden * m12_v[n, e, :, :HID]).astype(BF)
            gab_v[n, e, :, HID:] = (grad_hidden * m12_v[n, e, :, HID:]).astype(BF)
        store(gab_v.at[n], gab.at[:, place])
        if n == 0:
            for item in weight_loads:
                item.wait()
        for e in range(2):
            row_grads = (nt(gab_v[n, e, :, :HID], wg_v[e]) + nt(gab_v[n, e, :, HID:], wu_v[e])).astype(BF)
            for i in range(4):
                rows[i, e * CAP : (e + 1) * CAP, :] = row_grads[i * CAP : (i + 1) * CAP]
        for i in range(4):
            part_v[n, i * TOK : (i + 1) * TOK, :] = lax.dot_general(
                onehot[i], rows[i], (((0,), (0,)), ((), ())), preferred_element_type=F32
            ).astype(BF)
            if i % 2 == 1:
                store(part_v.at[n, pl.ds((i - 1) * TOK, 2 * TOK)], partials[2 * n + i // 2])
    for item in stores:
        item.wait()


def groups_pass(groups, tokens, eid, m12, wd, wg, wu, carried):
    chained = carried is not None
    count = len(groups)
    pieces = [[t.shape[0] for t in mine] for mine in tokens]
    lent = sum(len(p) for p in pieces)
    anywhere = pl.BlockSpec(memory_space=pl.ANY)
    slots = jax.ShapeDtypeStruct((2, 16 * CAP, D), BF)
    args = [t for mine in tokens for t in mine] + [m12, wd, wg, wu] + (list(carried) if chained else [])
    out = pl.pallas_call(
        functools.partial(groups_kernel, groups, pieces, chained),
        in_specs=[pl.BlockSpec(memory_space=pltpu.SMEM)] + [anywhere] * len(args),
        out_specs=[anywhere] * (2 + 2 * count),
        out_shape=[slots, slots] + [jax.ShapeDtypeStruct((2 * TOK, D), BF)] * (2 * count),
        scratch_shapes=[
            pltpu.VMEM((count, 4 * PACK, D), BF),
            pltpu.VMEM((count, 2, 4 * CAP, 2 * HID), F32),
            pltpu.VMEM((2, HID, D), BF),
            pltpu.VMEM((2, D, HID), BF),
            pltpu.VMEM((2, D, HID), BF),
            pltpu.VMEM((count, 2, 4 * CAP, D), BF),
            pltpu.VMEM((count, 2, 4 * CAP, 2 * HID), BF),
            pltpu.VMEM((count, 4 * TOK, D), BF),
            pltpu.VMEM((4, 2 * CAP, TOK), BF),
            pltpu.VMEM((4, 2 * CAP, D), BF),
            pltpu.SemaphoreType.DMA((lent + 3 + count,)),
            pltpu.SemaphoreType.DMA((4 * count,)),
        ],
        input_output_aliases={lent + 5: 0, lent + 6: 1} if chained else {},
        compiler_params=pltpu.CompilerParams(vmem_limit_bytes=VMEM_LIMIT),
        cost_estimate=pl.CostEstimate(
            flops=2_900_000_000 * count, bytes_accessed=6_000_000 + 9_000_000 * count, transcendentals=0
        ),
        name="groups_" + "".join(str(g) for g in groups),
    )(eid, *args)
    return out[0], out[1], out[2:]


def compress(local_grad, residual):
    carried = local_grad * loss_unscale + residual.astype(F32)
    magnitude = jnp.mean(jnp.abs(carried), axis=-1, keepdims=True) + epsilon
    compressed = (magnitude * jnp.tanh(carried * (1.0 / magnitude))).astype(BF)
    return compressed, (carried - compressed.astype(F32)).astype(BF)


def gate_up_kernel(spot, xt, gab, res_gate, res_up, keep, give, left_gate, left_up, held):
    core = spot[4]
    half = pl.program_id(1)
    grads = [jnp.dot(xt[0, u * 256 : (u + 1) * 256], gab[0], preferred_element_type=F32) for u in range(2)]
    for u in range(2):
        rows = slice(u * 256, (u + 1) * 256)
        at = spot[2 * half + u]
        for m, (res, left) in enumerate(((res_gate, left_gate), (res_up, left_up))):
            held[u, m], left[0, rows] = compress(grads[u][:, m * HID : (m + 1) * HID], res[0, rows])
            keep[at, m, 0] = held[u, m, pl.ds(pl.multiple_of(core * 128, 128), 128)]
            give[at, m, 0] = held[u, m, pl.ds(pl.multiple_of((1 - core) * 128, 128), 128)]


def gate_up_grads(spot, xt, gab, res_gate, res_up):
    tile = pl.BlockSpec((1, HID, HID), lambda e, t, s: (e, t, 0))
    res_shape = jax.ShapeDtypeStruct((2, D, HID), BF)
    blocks = jax.ShapeDtypeStruct((SIDE, 2, 2, 128, HID), BF)
    return pl.pallas_call(
        gate_up_kernel,
        grid_spec=pltpu.PrefetchScalarGridSpec(
            num_scalar_prefetch=1,
            grid=(2, 2),
            in_specs=[
                pl.BlockSpec((1, 512, 16 * CAP), lambda e, t, s: (e, t, 0)),
                pl.BlockSpec((1, 16 * CAP, 2 * HID), lambda e, t, s: (e, 0, 0)),
                tile,
                tile,
            ],
            out_specs=[pl.BlockSpec((SIDE, 2, 1, 128, HID), lambda e, t, s: (0, 0, e, 0, 0))] * 2 + [tile, tile],
            scratch_shapes=[pltpu.VMEM((2, 2, 256, HID), BF)],
        ),
        out_shape=[blocks, blocks, res_shape, res_shape],
        compiler_params=pltpu.CompilerParams(vmem_limit_bytes=VMEM_LIMIT),
        cost_estimate=pl.CostEstimate(flops=5_400_000_000, bytes_accessed=22_000_000, transcendentals=2_000_000),
        name="gate_up_grads",
    )(spot, xt, gab, res_gate, res_up)


def down_kernel(spot, ht, cot, res, keep, give, left):
    core = spot[4]
    grads = [jnp.dot(ht[0, u * 256 : (u + 1) * 256], cot[0], preferred_element_type=F32) for u in range(2)]
    for u in range(2):
        rows = slice(u * 256, (u + 1) * 256)
        compressed, left[0, rows] = compress(grads[u], res[0, rows])
        for own in range(2):

            @pl.when(core == own)
            def _():
                for x in range(SIDE):
                    keep[spot[x], 0, rows] = compressed[:, (2 * x + own) * 128 : (2 * x + own + 1) * 128]
                    give[spot[x], 0, rows] = compressed[:, (2 * x + 1 - own) * 128 : (2 * x + 2 - own) * 128]


def down_grads(spot, ht, cot, res):
    tile = pl.BlockSpec((1, HID, D), lambda e, s: (e, 0, 0))
    blocks = jax.ShapeDtypeStruct((SIDE, 2, HID, 128), BF)
    return pl.pallas_call(
        down_kernel,
        grid_spec=pltpu.PrefetchScalarGridSpec(
            num_scalar_prefetch=1,
            grid=(2,),
            in_specs=[
                pl.BlockSpec((1, HID, 16 * CAP), lambda e, s: (e, 0, 0)),
                pl.BlockSpec((1, 16 * CAP, D), lambda e, s: (e, 0, 0)),
                tile,
            ],
            out_specs=[pl.BlockSpec((SIDE, 1, HID, 128), lambda e, s: (0, e, 0, 0))] * 2 + [tile],
        ),
        out_shape=[blocks, blocks, jax.ShapeDtypeStruct((2, HID, D), BF)],
        compiler_params=pltpu.CompilerParams(vmem_limit_bytes=VMEM_LIMIT),
        cost_estimate=pl.CostEstimate(flops=2_700_000_000, bytes_accessed=14_000_000, transcendentals=1_000_000),
        name="down_grads",
    )(spot, ht, cot, res)


def total(*terms):
    out = terms[0].astype(F32)
    for term in terms[1:]:
        out = out + term.astype(F32)
    return out


def add(*terms):
    return total(*terms).astype(BF)


def mean_over_dp(keep, give):
    got = dp_hop(give, lambda x, c: (x, 1 - c))
    to_minus = dp_hop(add(keep[1], got[1]), lambda x, c: (x - 1, c))
    to_plus = dp_hop(add(keep[2], got[2]), lambda x, c: (x + 1, c))
    to_far = dp_hop(add(keep[3], got[3]), lambda x, c: (x + 2, c))
    return total(keep[0], got[0], to_minus, to_plus, to_far) / 8.0


def on_device(x_saved, d_out, routes, probs, w_gate, w_up, w_down, res_gate, res_up, res_down):
    place = lax.axis_index("expert")
    replica = lax.axis_index("dp")
    x, core = replica // 2, replica % 2
    first = jnp.where(core == 0, place // SIDE, place % SIDE)
    second = jnp.where(core == 0, place % SIDE, place // SIDE)
    offsets = jnp.array(OFFSETS, jnp.int32)
    perm = expert_index(
        core, ((first + offsets) % SIDE)[None, :], ((second + offsets) % SIDE)[:, None]
    ).reshape(-1).astype(jnp.int32)
    where_held = jnp.array([OFFSETS.index(o) for o in (0, 1, 2, -1)], jnp.int32)
    spot = jnp.concatenate([where_held[(jnp.arange(SIDE) - x) % SIDE], core[None]]).astype(jnp.int32)
    eid = (place * 2).astype(jnp.int32).reshape(1)

    own = pack(d_out, routes, probs)
    near = (hop(own, 0, 1), hop(own, 0, -1), hop(own, 0, 2))
    terms = forward_terms(0, perm, x_saved[0], w_gate, w_up, None)
    near, terms = lax.optimization_barrier((near, terms))
    group0 = jnp.concatenate([own, *near], axis=0)
    group1, group2 = hop(group0, 1, 1), hop(group0, 1, -1)
    xt, ht, m12 = forward_terms(1, perm, x_saved[0], w_gate, w_up, terms)

    run = functools.partial(groups_pass, eid=eid, m12=m12, wd=w_down, wg=w_gate, wu=w_up)
    cot, gab, (part0a, part0b) = run((0,), [(group0,)], carried=None)
    group1, group2, cot = lax.optimization_barrier((group1, group2, cot))
    group3 = (hop(group1[: 2 * PACK], 1, 1), hop(group2[2 * PACK :], 1, -1))
    cot, gab, (part1a, part1b, part2a, part2b) = run(
        (1, 2), [(group1,), (group2,)], carried=(cot, gab)
    )
    cot, gab, (part3a, part3b) = run((3,), [group3], carried=(cot, gab))

    direct_plus, direct_minus = hop(part2b, 1, 1), hop(part1a, 1, -1)
    over_plus, over_minus = hop(part3a, 1, 1), hop(part3b, 1, -1)
    keep, give, left_gate, left_up = gate_up_grads(spot, xt, gab, res_gate[0], res_up[0])
    over_plus, over_minus, direct_plus, direct_minus, give = lax.optimization_barrier(
        (over_plus, over_minus, direct_plus, direct_minus, give)
    )
    mean = mean_over_dp(keep, give)
    late_plus, late_minus = hop(add(part2a, over_plus), 1, 1), hop(add(part1b, over_minus), 1, -1)
    keep, give, left_down = down_grads(spot, ht, cot, res_down[0])
    late_plus, late_minus, give = lax.optimization_barrier((late_plus, late_minus, give))
    mean_down = mean_over_dp(keep, give)

    def column(i):
        part = slice(i % 2 * TOK, (i % 2 + 1) * TOK)
        terms = (part0a, late_plus, direct_minus) if i < 2 else (part0b, direct_plus, late_minus)
        return total(*(t[part] for t in terms))

    d_tokens = add(
        column(0),
        hop(column(2).astype(BF), 0, 1),
        hop(column(1).astype(BF), 0, -1),
        hop(column(3).astype(BF), 0, 2),
    )
    return (d_tokens, mean[0], mean[1], mean_down, left_gate[None], left_up[None], left_down[None])


def solution(mesh):
    in_specs = (
        P("dp", "expert", None, None),
        P(("dp", "expert"), None),
        P(("dp", "expert"), None),
        P(("dp", "expert"), None),
        P("expert", None, None),
        P("expert", None, None),
        P("expert", None, None),
        P("dp", "expert", None, None),
        P("dp", "expert", None, None),
        P("dp", "expert", None, None),
    )
    out_specs = (
        P(("dp", "expert"), None),
        P("expert", "dp", None),
        P("expert", "dp", None),
        P("expert", None, "dp"),
        P("dp", "expert", None, None),
        P("dp", "expert", None, None),
        P("dp", "expert", None, None),
    )
    return jax.shard_map(
        on_device, mesh=mesh, in_specs=in_specs, out_specs=out_specs, check_vma=False
    )
```

```python
import functools

import jax
import jax.numpy as jnp
from jax import lax
from jax.experimental import pallas as pl
from jax.experimental.pallas import tpu as pltpu
from jax.sharding import PartitionSpec as P

loss_unscale = 0.0625
epsilon = 1e-05

SIDE = 4
OFFSETS = (0, -1, 1, 2)
CAP = 80
TOK = 256
PACK = TOK + 16
D = 1024
HID = 512
BF = jnp.bfloat16
F32 = jnp.float32
VMEM_LIMIT = 56 * 2**20


def expert_index(core, first, second):
    return jnp.where(core == 0, first * SIDE + second, second * SIDE + first)


def pairs(axis, step):
    out = []
    for dp in range(8):
        core = dp % 2
        for z in range(SIDE):
            for y in range(SIDE):
                along_z = (axis == 0) == (core == 0)
                z2, y2 = ((z + step) % SIDE, y) if along_z else (z, (y + step) % SIDE)
                out.append((dp * 16 + z * SIDE + y, dp * 16 + z2 * SIDE + y2))
    return out


def hop(value, axis, step):
    return lax.ppermute(value, ("dp", "expert"), pairs(axis, step))


def dp_hop(value, move):
    return lax.ppermute(
        value, "dp", [(x * 2 + c, move(x, c)[0] % SIDE * 2 + move(x, c)[1]) for x in range(SIDE) for c in range(2)]
    )


def nt(left, right):
    return lax.dot_general(left, right, (((1,), (1,)), ((), ())), preferred_element_type=F32)


def pack_kernel(tokens, routes, probs, out):
    out[:TOK, :] = tokens[...]
    weights = probs[...]
    high = weights.astype(BF)
    left = weights - high.astype(F32)
    middle = left.astype(BF)
    low = (left - middle.astype(F32)).astype(BF)
    out[TOK : TOK + 8, :] = jnp.concatenate(
        [routes[...].astype(F32).astype(BF), high, middle, low], axis=1
    )
    out[TOK + 8 :, :] = jnp.zeros((8, D), BF)


def pack(tokens, routes, probs):
    return pl.pallas_call(
        pack_kernel,
        out_shape=jax.ShapeDtypeStruct((PACK, D), BF),
        cost_estimate=pl.CostEstimate(flops=0, bytes_accessed=1_100_000, transcendentals=0),
        name="pack",
    )(tokens, routes.T, probs.T)


def forward_kernel(chained, perm, *refs):
    xs, (wg, wu), refs = refs[:8], refs[8:10], refs[10 + (3 if chained else 0) :]
    xt, ht, m12, rows = refs
    for i in range(8):
        rows[i * CAP : (i + 1) * CAP, :] = xs[i][0, 0]
    half = 4 * CAP
    pre = []
    for h in range(2):
        saved = rows[h * half : (h + 1) * half, :]
        pre.append(
            (
                jnp.dot(saved, wg[0], preferred_element_type=F32),
                jnp.dot(saved, wu[0], preferred_element_type=F32),
            )
        )
    xt[0] = rows[...].T
    hidden = []
    for h, (gate, up) in enumerate(pre):
        logistic = jax.nn.sigmoid(gate)
        act = gate * logistic
        m12[0, h * half : (h + 1) * half, :HID] = up * (logistic * (1.0 + gate * (1.0 - logistic)))
        m12[0, h * half : (h + 1) * half, HID:] = act
        hidden.append((act * up).astype(BF))
    ht[0] = jnp.concatenate(hidden, axis=0).T


def forward_terms(e, perm, x, wg, wu, carried):
    blocks = x.reshape(2, 16, CAP, D)
    chained = carried is not None

    def block_at(i):
        return pl.BlockSpec((1, 1, CAP, D), lambda h, p: (e, p[8 * h + i], 0, 0))

    half = 8 * CAP
    return pl.pallas_call(
        functools.partial(forward_kernel, chained),
        grid_spec=pltpu.PrefetchScalarGridSpec(
            num_scalar_prefetch=1,
            grid=(2,),
            in_specs=[block_at(i) for i in range(8)]
            + [pl.BlockSpec((1, D, HID), lambda h, p: (e, 0, 0))] * 2
            + [pl.BlockSpec(memory_space=pl.ANY)] * (3 if chained else 0),
            out_specs=[
                pl.BlockSpec((1, D, half), lambda h, p: (e, 0, h)),
                pl.BlockSpec((1, HID, half), lambda h, p: (e, 0, h)),
                pl.BlockSpec((1, half, 2 * HID), lambda h, p: (e, h, 0)),
            ],
            scratch_shapes=[pltpu.VMEM((half, D), BF)],
        ),
        out_shape=[
            jax.ShapeDtypeStruct((2, D, 16 * CAP), BF),
            jax.ShapeDtypeStruct((2, HID, 16 * CAP), BF),
            jax.ShapeDtypeStruct((2, 16 * CAP, 2 * HID), F32),
        ],
        input_output_aliases={11 + i: i for i in range(3)} if chained else {},
        compiler_params=pltpu.CompilerParams(vmem_limit_bytes=VMEM_LIMIT),
        cost_estimate=pl.CostEstimate(flops=2_700_000_000, bytes_accessed=15_000_000, transcendentals=655_360),
        name="forward_terms",
    )(perm, *([blocks] * 8), wg, wu, *(carried or ()))


def dispatch_kernel(targets, eids, *refs):
    blocks, (cots, hots) = refs[:4], (refs[4 : 4 + len(targets)], refs[4 + len(targets) :])
    before = (
        lax.broadcasted_iota(jnp.int32, (TOK, TOK), 0) < lax.broadcasted_iota(jnp.int32, (TOK, TOK), 1)
    ).astype(BF)
    slot = lax.broadcasted_iota(jnp.int32, (CAP, TOK), 0).astype(F32)
    named, weights = [], []
    for i in range(4):
        meta = blocks[i][TOK:, :].astype(F32)[:8]
        routes = meta[:, :TOK]
        probs = meta[:, TOK : 2 * TOK] + meta[:, 2 * TOK : 3 * TOK] + meta[:, 3 * TOK :]
        for target in targets:
            for e in range(2):
                hit = routes == (eids[target] + e).astype(F32)
                named.append(jnp.sum(jnp.where(hit, 1.0, 0.0), axis=0, keepdims=True))
                weights.append(jnp.sum(jnp.where(hit, probs, 0.0), axis=0, keepdims=True))
    mask = jnp.concatenate(named, axis=0)
    rank = jnp.dot(mask.astype(BF), before, preferred_element_type=F32)
    key = jnp.where(mask > 0.5, rank, -1.0)
    per = 2 * len(targets)
    for i in range(4):
        halves, scales = [], []
        for k in range(per):
            hit = slot == key[per * i + k : per * i + k + 1, :]
            halves.append(jnp.where(hit, 1.0, 0.0).astype(BF))
            scales.append(jnp.sum(jnp.where(hit, weights[per * i + k], 0.0), axis=1, keepdims=True))
        chosen = jnp.concatenate(halves, axis=0)
        taken = jnp.dot(chosen, blocks[i][:TOK, :], preferred_element_type=F32)
        scaled = (taken * jnp.concatenate(scales, axis=0)).astype(BF)
        for k in range(per):
            cots[k // 2][k % 2, i * CAP : (i + 1) * CAP, :] = scaled[k * CAP : (k + 1) * CAP]
            hots[k // 2][i, k % 2 * CAP : (k % 2 + 1) * CAP, :] = halves[k]


def dispatch(targets, eids, blocks):
    whole = pl.BlockSpec(memory_space=pltpu.VMEM)
    count = len(targets)
    out = pl.pallas_call(
        functools.partial(dispatch_kernel, targets),
        in_specs=[pl.BlockSpec(memory_space=pltpu.SMEM)] + [whole] * 4,
        out_specs=[whole] * (2 * count),
        out_shape=[jax.ShapeDtypeStruct((2, 4 * CAP, D), BF)] * count
        + [jax.ShapeDtypeStruct((4, 2 * CAP, TOK), BF)] * count,
        compiler_params=pltpu.CompilerParams(vmem_limit_bytes=VMEM_LIMIT),
        cost_estimate=pl.CostEstimate(flops=400_000_000 * count, bytes_accessed=6_000_000, transcendentals=0),
        name="dispatch_" + "".join(str(t) for t in targets),
    )(eids, *blocks)
    return out[:count], out[count:]


def groups_kernel(groups, chained, *refs):
    count = len(groups)
    arrived, m12, wd, wg, wu = refs[:count], *refs[count : count + 4]
    refs = refs[count + 4 + (2 if chained else 0) :]
    cot, gab, outs, refs = refs[0], refs[1], refs[2 : 2 + count], refs[2 + count :]
    m12_v, wd_v, wg_v, wu_v, cot_v, gab_v, rows_v, sem_in, sem_out = refs
    loads, stores, cot_loads, factor_loads = [], [], [], []

    def load(source, target):
        loads.append(pltpu.make_async_copy(source, target, sem_in.at[len(loads)]))
        loads[-1].start()
        return loads[-1]

    def store(source, target):
        stores.append(pltpu.make_async_copy(source, target, sem_out.at[len(stores)]))
        stores[-1].start()

    down_loads, weight_loads = [], []
    for n, group in enumerate(groups):
        cot_loads.append([load(arrived[n].at[e], cot_v.at[n, e]) for e in range(2)])
        if n == 0:
            down_loads = [load(wd.at[e], wd_v.at[e]) for e in range(2)]
        factor_loads.append(
            [load(m12.at[e, pl.ds(group * 4 * CAP, 4 * CAP)], m12_v.at[n, e]) for e in range(2)]
        )
        if n == 0:
            weight_loads = [[load(wg.at[e], wg_v.at[e]), load(wu.at[e], wu_v.at[e])] for e in range(2)]
    for n, group in enumerate(groups):
        place = pl.ds(group * 4 * CAP, 4 * CAP)
        for e in range(2):
            cot_loads[n][e].wait()
            store(cot_v.at[n, e], cot.at[e, place])
            if n == 0:
                down_loads[e].wait()
            grad_hidden = nt(cot_v[n, e], wd_v[e])
            factor_loads[n][e].wait()
            gab_v[n, e, :, :HID] = (grad_hidden * m12_v[n, e, :, :HID]).astype(BF)
            gab_v[n, e, :, HID:] = (grad_hidden * m12_v[n, e, :, HID:]).astype(BF)
            store(gab_v.at[n, e], gab.at[e, place])
        for e in range(2):
            if n == 0:
                for item in weight_loads[e]:
                    item.wait()
            rows_v[n, e] = (nt(gab_v[n, e, :, :HID], wg_v[e]) + nt(gab_v[n, e, :, HID:], wu_v[e])).astype(BF)
            store(rows_v.at[n, e], outs[n].at[e])
    for item in stores:
        item.wait()


def groups_pass(groups, arrived, m12, wd, wg, wu, carried):
    chained = carried is not None
    count = len(groups)
    anywhere = pl.BlockSpec(memory_space=pl.ANY)
    slots = jax.ShapeDtypeStruct((2, 16 * CAP, D), BF)
    args = [*arrived, m12, wd, wg, wu] + (list(carried) if chained else [])
    out = pl.pallas_call(
        functools.partial(groups_kernel, groups, chained),
        in_specs=[anywhere] * len(args),
        out_specs=[anywhere] * (2 + count),
        out_shape=[slots, slots] + [jax.ShapeDtypeStruct((2, 4 * CAP, D), BF)] * count,
        scratch_shapes=[
            pltpu.VMEM((count, 2, 4 * CAP, 2 * HID), F32),
            pltpu.VMEM((2, HID, D), BF),
            pltpu.VMEM((2, D, HID), BF),
            pltpu.VMEM((2, D, HID), BF),
            pltpu.VMEM((count, 2, 4 * CAP, D), BF),
            pltpu.VMEM((count, 2, 4 * CAP, 2 * HID), BF),
            pltpu.VMEM((count, 2, 4 * CAP, D), BF),
            pltpu.SemaphoreType.DMA((6 + 4 * count,)),
            pltpu.SemaphoreType.DMA((6 * count,)),
        ],
        input_output_aliases={count + 4: 0, count + 5: 1} if chained else {},
        compiler_params=pltpu.CompilerParams(vmem_limit_bytes=VMEM_LIMIT),
        cost_estimate=pl.CostEstimate(
            flops=2_100_000_000 * count, bytes_accessed=6_000_000 + 9_000_000 * count, transcendentals=0
        ),
        name="groups_" + "".join(str(g) for g in groups),
    )(*args)
    return out[0], out[1], out[2:]


def combine_kernel(*refs):
    rows, hots, outs, (rows_v, hots_v, sem_rows, sem_hots) = refs[:4], refs[4:8], refs[8:12], refs[12:]
    loads = []
    for i in range(4):
        mine = []
        for k in range(4):
            mine.append(
                pltpu.make_async_copy(
                    hots[k].at[i], hots_v.at[i, pl.ds(k * 2 * CAP, 2 * CAP)], sem_hots.at[4 * i + k]
                )
            )
            for e in range(2):
                mine.append(
                    pltpu.make_async_copy(
                        rows[k].at[e, pl.ds(i * CAP, CAP)],
                        rows_v.at[i, pl.ds((2 * k + e) * CAP, CAP)],
                        sem_rows.at[8 * i + 2 * k + e],
                    )
                )
        for item in mine:
            item.start()
        loads.append(mine)
    for i in range(4):
        for item in loads[i]:
            item.wait()
        outs[i][...] = lax.dot_general(
            hots_v[i], rows_v[i], (((0,), (0,)), ((), ())), preferred_element_type=F32
        ).astype(BF)


def combine(rows, hots):
    anywhere = pl.BlockSpec(memory_space=pl.ANY)
    return pl.pallas_call(
        combine_kernel,
        in_specs=[anywhere] * 8,
        out_specs=[pl.BlockSpec(memory_space=pltpu.VMEM)] * 4,
        out_shape=[jax.ShapeDtypeStruct((TOK, D), BF)] * 4,
        scratch_shapes=[
            pltpu.VMEM((4, 8 * CAP, D), BF),
            pltpu.VMEM((4, 8 * CAP, TOK), BF),
            pltpu.SemaphoreType.DMA((32,)),
            pltpu.SemaphoreType.DMA((16,)),
        ],
        compiler_params=pltpu.CompilerParams(vmem_limit_bytes=VMEM_LIMIT),
        cost_estimate=pl.CostEstimate(flops=1_400_000_000, bytes_accessed=9_000_000, transcendentals=0),
        name="combine",
    )(*rows, *hots)


def compress(local_grad, residual):
    carried = local_grad * loss_unscale + residual.astype(F32)
    magnitude = jnp.mean(jnp.abs(carried), axis=-1, keepdims=True) + epsilon
    compressed = (magnitude * jnp.tanh(carried * (1.0 / magnitude))).astype(BF)
    return compressed, (carried - compressed.astype(F32)).astype(BF)


def gate_up_kernel(spot, xt, gab, res_gate, res_up, keep, give_gate, give_up, left_gate, left_up, held):
    core = spot[8]
    half = pl.program_id(1)
    grads = [jnp.dot(xt[0, u * 256 : (u + 1) * 256], gab[0], preferred_element_type=F32) for u in range(2)]
    for u in range(2):
        rows = slice(u * 256, (u + 1) * 256)
        kept_at, given_at = spot[2 * half + u], spot[SIDE + 2 * half + u]
        for m, (res, left) in enumerate(((res_gate, left_gate), (res_up, left_up))):
            held[u, m], left[0, rows] = compress(grads[u][:, m * HID : (m + 1) * HID], res[0, rows])
            keep[kept_at, m, 0] = held[u, m, pl.ds(pl.multiple_of(core * 128, 128), 128)]
            give = (give_gate, give_up)[m]
            give[given_at, 0] = held[u, m, pl.ds(pl.multiple_of((1 - core) * 128, 128), 128)]


def gate_up_grads(spot, xt, gab, res_gate, res_up):
    tile = pl.BlockSpec((1, HID, HID), lambda e, t, s: (e, t, 0))
    res_shape = jax.ShapeDtypeStruct((2, D, HID), BF)
    keep_shape = jax.ShapeDtypeStruct((SIDE, 2, 2, 128, HID), BF)
    give_shape = jax.ShapeDtypeStruct((SIDE, 2, 128, HID), BF)
    return pl.pallas_call(
        gate_up_kernel,
        grid_spec=pltpu.PrefetchScalarGridSpec(
            num_scalar_prefetch=1,
            grid=(2, 2),
            in_specs=[
                pl.BlockSpec((1, 512, 16 * CAP), lambda e, t, s: (e, t, 0)),
                pl.BlockSpec((1, 16 * CAP, 2 * HID), lambda e, t, s: (e, 0, 0)),
                tile,
                tile,
            ],
            out_specs=[pl.BlockSpec((SIDE, 2, 1, 128, HID), lambda e, t, s: (0, 0, e, 0, 0))]
            + [pl.BlockSpec((SIDE, 1, 128, HID), lambda e, t, s: (0, e, 0, 0))] * 2
            + [tile, tile],
            scratch_shapes=[pltpu.VMEM((2, 2, 256, HID), BF)],
        ),
        out_shape=[keep_shape, give_shape, give_shape, res_shape, res_shape],
        compiler_params=pltpu.CompilerParams(vmem_limit_bytes=VMEM_LIMIT),
        cost_estimate=pl.CostEstimate(flops=5_400_000_000, bytes_accessed=22_000_000, transcendentals=2_000_000),
        name="gate_up_grads",
    )(spot, xt, gab, res_gate, res_up)


def down_kernel(spot, ht, cot, res, keep, give, left):
    core = spot[8]
    grads = [jnp.dot(ht[0, u * 256 : (u + 1) * 256], cot[0], preferred_element_type=F32) for u in range(2)]
    for u in range(2):
        rows = slice(u * 256, (u + 1) * 256)
        compressed, left[0, rows] = compress(grads[u], res[0, rows])
        for own in range(2):

            @pl.when(core == own)
            def _():
                for x in range(SIDE):
                    keep[spot[x], 0, rows] = compressed[:, (2 * x + own) * 128 : (2 * x + own + 1) * 128]
                    give[spot[SIDE + x], 0, rows] = compressed[:, (2 * x + 1 - own) * 128 : (2 * x + 2 - own) * 128]


def down_grads(spot, ht, cot, res):
    tile = pl.BlockSpec((1, HID, D), lambda e, s: (e, 0, 0))
    blocks = jax.ShapeDtypeStruct((SIDE, 2, HID, 128), BF)
    return pl.pallas_call(
        down_kernel,
        grid_spec=pltpu.PrefetchScalarGridSpec(
            num_scalar_prefetch=1,
            grid=(2,),
            in_specs=[
                pl.BlockSpec((1, HID, 16 * CAP), lambda e, s: (e, 0, 0)),
                pl.BlockSpec((1, 16 * CAP, D), lambda e, s: (e, 0, 0)),
                tile,
            ],
            out_specs=[pl.BlockSpec((SIDE, 1, HID, 128), lambda e, s: (0, e, 0, 0))] * 2 + [tile],
        ),
        out_shape=[blocks, blocks, jax.ShapeDtypeStruct((2, HID, D), BF)],
        compiler_params=pltpu.CompilerParams(vmem_limit_bytes=VMEM_LIMIT),
        cost_estimate=pl.CostEstimate(flops=2_700_000_000, bytes_accessed=14_000_000, transcendentals=1_000_000),
        name="down_grads",
    )(spot, ht, cot, res)


def total(*terms):
    out = terms[0].astype(F32)
    for term in terms[1:]:
        out = out + term.astype(F32)
    return out


def add(*terms):
    return total(*terms).astype(BF)


def partner(stage, x, core):
    return x ^ (1 if stage == core else 3)


def mean_over_dp(keep, got, beside):
    first = dp_hop(add(keep[2:], got[2:]), lambda x, c: (partner(0, x, c), c))
    first, _ = lax.optimization_barrier((first, beside))
    second = dp_hop(add(keep[1], got[1], first[1]), lambda x, c: (partner(1, x, c), c))
    return total(keep[0], got[0], first[0], second) / 8.0


def on_device(x_saved, d_out, routes, probs, w_gate, w_up, w_down, res_gate, res_up, res_down):
    place = lax.axis_index("expert")
    replica = lax.axis_index("dp")
    x, core = replica // 2, replica % 2
    first = jnp.where(core == 0, place // SIDE, place % SIDE)
    second = jnp.where(core == 0, place % SIDE, place // SIDE)
    offsets = jnp.array(OFFSETS, jnp.int32)
    perm = expert_index(
        core, ((first + offsets) % SIDE)[None, :], ((second + offsets) % SIDE)[:, None]
    ).reshape(-1).astype(jnp.int32)
    apart = jnp.arange(SIDE, dtype=jnp.int32) ^ x
    orders = [apart_at[apart] for apart_at in (jnp.array([0, 2, 3, 1]), jnp.array([0, 1, 3, 2]))]
    spot = jnp.concatenate(
        [jnp.where(core == 0, orders[0], orders[1]), jnp.where(core == 0, orders[1], orders[0]), core[None]]
    ).astype(jnp.int32)
    eids = (expert_index(core, first, (second + offsets) % SIDE) * 2).astype(jnp.int32)

    own = pack(d_out, routes, probs)
    near = (hop(own, 0, 1), hop(own, 0, -1), hop(own, 0, 2))
    terms = forward_terms(0, perm, x_saved[0], w_gate, w_up, None)
    near, terms = lax.optimization_barrier((near, terms))
    (to_minus, to_plus), (hot1, hot2) = dispatch((1, 2), eids, (own, *near))
    group1, group2 = hop(to_plus, 1, 1), hop(to_minus, 1, -1)
    (group0, to_far), (hot0, hot3) = dispatch((0, 3), eids, (own, *near))
    group3 = hop(to_far, 1, 2)
    xt, ht, m12 = forward_terms(1, perm, x_saved[0], w_gate, w_up, terms)

    run = functools.partial(groups_pass, m12=m12, wd=w_down, wg=w_gate, wu=w_up)
    cot, gab, (rows0,) = run((0,), [group0], carried=None)
    group1, group2, cot = lax.optimization_barrier((group1, group2, cot))
    cot, gab, (rows1, rows2) = run((1, 2), [group1, group2], carried=(cot, gab))
    cot, gab, (rows3,) = run((3,), [group3], carried=(cot, gab))
    rows = (rows0, hop(rows2, 1, 1), hop(rows1, 1, -1), hop(rows3, 1, 2))

    keep, give_gate, give_up, left_gate, left_up = gate_up_grads(spot, xt, gab, res_gate[0], res_up[0])
    got_gate, got_up = (dp_hop(g, lambda x, c: (x, 1 - c)) for g in (give_gate, give_up))
    near_rows, ht, left_gate = lax.optimization_barrier((rows[1:3], ht, left_gate))
    keep_down, give_down, left_down = down_grads(spot, ht, cot, res_down[0])
    rows = (rows[0], *near_rows, rows[3])
    rows, got_gate, got_up, give_down = lax.optimization_barrier((rows, got_gate, got_up, give_down))
    got_down = dp_hop(give_down, lambda x, c: (x, 1 - c))
    mine, before, behind, across = combine(rows, (hot0, hot1, hot2, hot3))
    mean = mean_over_dp(keep, jnp.stack([got_gate, got_up], axis=1), mine)
    mean_down = mean_over_dp(keep_down, got_down, mine)
    terms = (mine, hop(behind, 0, 1), hop(before, 0, -1), hop(across, 0, 2))
    terms, mean, mean_down = lax.optimization_barrier((terms, mean, mean_down))
    d_tokens = add(*terms)
    return (d_tokens, mean[0], mean[1], mean_down, left_gate[None], left_up[None], left_down[None])


def solution(mesh):
    in_specs = (
        P("dp", "expert", None, None),
        P(("dp", "expert"), None),
        P(("dp", "expert"), None),
        P(("dp", "expert"), None),
        P("expert", None, None),
        P("expert", None, None),
        P("expert", None, None),
        P("dp", "expert", None, None),
        P("dp", "expert", None, None),
        P("dp", "expert", None, None),
    )
    out_specs = (
        P(("dp", "expert"), None),
        P("expert", "dp", None),
        P("expert", "dp", None),
        P("expert", None, "dp"),
        P("dp", "expert", None, None),
        P("dp", "expert", None, None),
        P("dp", "expert", None, None),
    )
    return jax.shard_map(
        on_device, mesh=mesh, in_specs=in_specs, out_specs=out_specs, check_vma=False
    )
```

```python
import functools

import jax
import jax.numpy as jnp
from jax import lax
from jax.experimental import pallas as pl
from jax.experimental.pallas import tpu as pltpu
from jax.sharding import PartitionSpec as P

loss_unscale = 0.0625
epsilon = 1e-05

SIDE = 4
OFFSETS = (0, -1, 1, 2)
CAP = 80
TOK = 256
PACK = TOK + 16
D = 1024
HID = 512
BF = jnp.bfloat16
F32 = jnp.float32
VMEM_LIMIT = 56 * 2**20


def place_of(here):
    core = here[0] & 1
    z, y = here[1] // SIDE, here[1] & (SIDE - 1)
    return here[0] // 2, core, jnp.where(core == 0, z, y), jnp.where(core == 0, y, z)


def expert_at(here, first_off, second_off):
    _, core, first, second = place_of(here)
    first, second = (first + first_off + SIDE) & (SIDE - 1), (second + second_off + SIDE) & (SIDE - 1)
    return jnp.where(core == 0, first * SIDE + second, second * SIDE + first)


def block_place(owner, x, core):
    apart = owner ^ x
    return jnp.where(apart == 0, 0, jnp.where(apart == 1, 2 - core, jnp.where(apart == 2, 3, 1 + core)))


def pairs(axis, step):
    out = []
    for dp in range(8):
        core = dp % 2
        for z in range(SIDE):
            for y in range(SIDE):
                along_z = (axis == 0) == (core == 0)
                z2, y2 = ((z + step) % SIDE, y) if along_z else (z, (y + step) % SIDE)
                out.append((dp * 16 + z * SIDE + y, dp * 16 + z2 * SIDE + y2))
    return out


def hop(value, axis, step):
    return lax.ppermute(value, ("dp", "expert"), pairs(axis, step))


def dp_hop(value, move):
    return lax.ppermute(
        value, "dp", [(x * 2 + c, move(x, c)[0] % SIDE * 2 + move(x, c)[1]) for x in range(SIDE) for c in range(2)]
    )


def nt(left, right):
    return lax.dot_general(left, right, (((1,), (1,)), ((), ())), preferred_element_type=F32)


def pack_kernel(tokens, routes, probs, out):
    out[:TOK, :] = tokens[...]
    weights = probs[...]
    high = weights.astype(BF)
    left = weights - high.astype(F32)
    middle = left.astype(BF)
    low = (left - middle.astype(F32)).astype(BF)
    out[TOK : TOK + 8, :] = jnp.concatenate(
        [routes[...].astype(F32).astype(BF), high, middle, low], axis=1
    )
    out[TOK + 8 :, :] = jnp.zeros((8, D), BF)


def pack(tokens, routes, probs):
    return pl.pallas_call(
        pack_kernel,
        out_shape=jax.ShapeDtypeStruct((PACK, D), BF),
        cost_estimate=pl.CostEstimate(flops=0, bytes_accessed=1_100_000, transcendentals=0),
        name="pack",
    )(tokens, routes.T, probs.T)


def forward_kernel(chained, here, *refs):
    xs, (wg, wu), refs = refs[:8], refs[8:10], refs[10 + (3 if chained else 0) :]
    xt, ht, m12, rows = refs
    for i in range(8):
        rows[i * CAP : (i + 1) * CAP, :] = xs[i][0, 0]
    half = 4 * CAP
    pre = []
    for h in range(2):
        saved = rows[h * half : (h + 1) * half, :]
        pre.append(
            (
                jnp.dot(saved, wg[0], preferred_element_type=F32),
                jnp.dot(saved, wu[0], preferred_element_type=F32),
            )
        )
    xt[0] = rows[...].T
    hidden = []
    for h, (gate, up) in enumerate(pre):
        logistic = jax.nn.sigmoid(gate)
        act = gate * logistic
        m12[0, h * half : (h + 1) * half, :HID] = up * (logistic * (1.0 + gate * (1.0 - logistic)))
        m12[0, h * half : (h + 1) * half, HID:] = act
        hidden.append((act * up).astype(BF))
    ht[0] = jnp.concatenate(hidden, axis=0).T


def forward_terms(e, here, x, wg, wu, carried):
    blocks = x.reshape(2, 16, CAP, D)
    chained = carried is not None

    def block_at(i):
        def at(h, here):
            return e, expert_at(here, OFFSETS[i % 4], h if i < 4 else 3 * h - 1), 0, 0

        return pl.BlockSpec((1, 1, CAP, D), at)

    half = 8 * CAP
    return pl.pallas_call(
        functools.partial(forward_kernel, chained),
        grid_spec=pltpu.PrefetchScalarGridSpec(
            num_scalar_prefetch=1,
            grid=(2,),
            in_specs=[block_at(i) for i in range(8)]
            + [pl.BlockSpec((1, D, HID), lambda h, p: (e, 0, 0))] * 2
            + [pl.BlockSpec(memory_space=pl.ANY)] * (3 if chained else 0),
            out_specs=[
                pl.BlockSpec((1, D, half), lambda h, p: (e, 0, h)),
                pl.BlockSpec((1, HID, half), lambda h, p: (e, 0, h)),
                pl.BlockSpec((1, half, 2 * HID), lambda h, p: (e, h, 0)),
            ],
            scratch_shapes=[pltpu.VMEM((half, D), BF)],
        ),
        out_shape=[
            jax.ShapeDtypeStruct((2, D, 16 * CAP), BF),
            jax.ShapeDtypeStruct((2, HID, 16 * CAP), BF),
            jax.ShapeDtypeStruct((2, 16 * CAP, 2 * HID), F32),
        ],
        input_output_aliases={11 + i: i for i in range(3)} if chained else {},
        compiler_params=pltpu.CompilerParams(vmem_limit_bytes=VMEM_LIMIT),
        cost_estimate=pl.CostEstimate(flops=2_700_000_000, bytes_accessed=15_000_000, transcendentals=655_360),
        name="forward_terms",
    )(here, *([blocks] * 8), wg, wu, *(carried or ()))


def dispatch_kernel(targets, layout, here, *refs):
    blocks, outs, hots = refs[:4], refs[4 : 4 + len(layout)], refs[4 + len(layout) :]
    before = (
        lax.broadcasted_iota(jnp.int32, (TOK, TOK), 0) < lax.broadcasted_iota(jnp.int32, (TOK, TOK), 1)
    ).astype(BF)
    slot = lax.broadcasted_iota(jnp.int32, (CAP, TOK), 0).astype(F32)
    names = [(2 * expert_at(here, 0, OFFSETS[t]) + e).astype(F32) for t in targets for e in range(2)]
    named, weights = [], []
    for i in range(4):
        meta = blocks[i][TOK:, :].astype(F32)[:8]
        routes = meta[:, :TOK]
        probs = meta[:, TOK : 2 * TOK] + meta[:, 2 * TOK : 3 * TOK] + meta[:, 3 * TOK :]
        for name in names:
            hit = routes == name
            named.append(jnp.sum(jnp.where(hit, 1.0, 0.0), axis=0, keepdims=True))
            weights.append(jnp.sum(jnp.where(hit, probs, 0.0), axis=0, keepdims=True))
    mask = jnp.concatenate(named, axis=0)
    rank = jnp.dot(mask.astype(BF), before, preferred_element_type=F32)
    key = jnp.where(mask > 0.5, rank, -1.0)
    per = len(names)
    for i in range(4):
        halves, scales = [], []
        for k in range(per):
            hit = slot == key[per * i + k : per * i + k + 1, :]
            halves.append(jnp.where(hit, 1.0, 0.0).astype(BF))
            scales.append(jnp.sum(jnp.where(hit, weights[per * i + k], 0.0), axis=1, keepdims=True))
            hots[k // 2][i, k % 2 * CAP : (k % 2 + 1) * CAP, :] = halves[k]
        chosen = jnp.concatenate(halves, axis=0)
        taken = jnp.dot(chosen, blocks[i][:TOK, :], preferred_element_type=F32)
        scaled = (taken * jnp.concatenate(scales, axis=0)).astype(BF)
        for out, held in zip(outs, layout):
            for n, (target, e) in enumerate(held):
                k = 2 * targets.index(target) + e
                out[n, i * CAP : (i + 1) * CAP, :] = scaled[k * CAP : (k + 1) * CAP]


def dispatch(targets, layout, here, blocks):
    whole = pl.BlockSpec(memory_space=pltpu.VMEM)
    out = pl.pallas_call(
        functools.partial(dispatch_kernel, targets, layout),
        in_specs=[pl.BlockSpec(memory_space=pltpu.SMEM)] + [whole] * 4,
        out_specs=[whole] * (len(layout) + len(targets)),
        out_shape=[jax.ShapeDtypeStruct((len(held), 4 * CAP, D), BF) for held in layout]
        + [jax.ShapeDtypeStruct((4, 2 * CAP, TOK), BF)] * len(targets),
        compiler_params=pltpu.CompilerParams(vmem_limit_bytes=VMEM_LIMIT),
        cost_estimate=pl.CostEstimate(
            flops=400_000_000 * len(targets), bytes_accessed=6_000_000, transcendentals=0
        ),
        name="dispatch_" + "".join(str(t) for t in targets),
    )(here, *blocks)
    return out[: len(layout)], out[len(layout) :]


def halves_of(refs, split):
    out = []
    for two in split:
        out.append([refs[0], refs[1]] if two else [refs[0].at[0], refs[0].at[1]])
        refs = refs[2 if two else 1 :]
    return out


def groups_kernel(groups, split, chained, *refs):
    count = len(groups)
    lent = count + sum(split)
    arrived = halves_of(refs[:lent], split)
    m12, wd, wg, wu = refs[lent : lent + 4]
    refs = refs[lent + 4 + (2 if chained else 0) :]
    cot, gab, outs, refs = refs[0], refs[1], halves_of(refs[2 : 2 + lent], split), refs[2 + lent :]
    m12_v, wd_v, wg_v, wu_v, cot_v, gab_v, rows_v, sem_in, sem_out = refs
    loads, stores, cot_loads, factor_loads = [], [], [], []

    def load(source, target):
        loads.append(pltpu.make_async_copy(source, target, sem_in.at[len(loads)]))
        loads[-1].start()
        return loads[-1]

    def store(source, target):
        stores.append(pltpu.make_async_copy(source, target, sem_out.at[len(stores)]))
        stores[-1].start()

    down_loads, weight_loads = [], []
    for n, group in enumerate(groups):
        cot_loads.append([load(arrived[n][e], cot_v.at[n, e]) for e in range(2)])
        if n == 0:
            down_loads = [load(wd.at[e], wd_v.at[e]) for e in range(2)]
        factor_loads.append(
            [load(m12.at[e, pl.ds(group * 4 * CAP, 4 * CAP)], m12_v.at[n, e]) for e in range(2)]
        )
        if n == 0:
            weight_loads = [[load(wg.at[e], wg_v.at[e]), load(wu.at[e], wu_v.at[e])] for e in range(2)]
    for n, group in enumerate(groups):
        place = pl.ds(group * 4 * CAP, 4 * CAP)
        for e in range(2):
            cot_loads[n][e].wait()
            store(cot_v.at[n, e], cot.at[e, place])
            if n == 0:
                down_loads[e].wait()
            grad_hidden = nt(cot_v[n, e], wd_v[e])
            factor_loads[n][e].wait()
            gab_v[n, e, :, :HID] = (grad_hidden * m12_v[n, e, :, :HID]).astype(BF)
            gab_v[n, e, :, HID:] = (grad_hidden * m12_v[n, e, :, HID:]).astype(BF)
            store(gab_v.at[n, e], gab.at[e, place])
        for e in range(2):
            if n == 0:
                for item in weight_loads[e]:
                    item.wait()
            rows_v[n, e] = (nt(gab_v[n, e, :, :HID], wg_v[e]) + nt(gab_v[n, e, :, HID:], wu_v[e])).astype(BF)
            store(rows_v.at[n, e], outs[n][e])
    for item in stores:
        item.wait()


def groups_pass(groups, arrived, m12, wd, wg, wu, carried):
    chained = carried is not None
    count = len(groups)
    anywhere = pl.BlockSpec(memory_space=pl.ANY)
    slots = jax.ShapeDtypeStruct((2, 16 * CAP, D), BF)
    split = [isinstance(a, tuple) for a in arrived]
    lent = count + sum(split)
    args = [a for two, a in zip(split, arrived) for a in (a if two else (a,))]
    args += [m12, wd, wg, wu] + (list(carried) if chained else [])
    row_shapes = []
    for two in split:
        shape = (4 * CAP, D) if two else (2, 4 * CAP, D)
        row_shapes += [jax.ShapeDtypeStruct(shape, BF)] * (2 if two else 1)
    out = pl.pallas_call(
        functools.partial(groups_kernel, groups, split, chained),
        in_specs=[anywhere] * len(args),
        out_specs=[anywhere] * (2 + lent),
        out_shape=[slots, slots] + row_shapes,
        scratch_shapes=[
            pltpu.VMEM((count, 2, 4 * CAP, 2 * HID), F32),
            pltpu.VMEM((2, HID, D), BF),
            pltpu.VMEM((2, D, HID), BF),
            pltpu.VMEM((2, D, HID), BF),
            pltpu.VMEM((count, 2, 4 * CAP, D), BF),
            pltpu.VMEM((count, 2, 4 * CAP, 2 * HID), BF),
            pltpu.VMEM((count, 2, 4 * CAP, D), BF),
            pltpu.SemaphoreType.DMA((6 + 4 * count,)),
            pltpu.SemaphoreType.DMA((6 * count,)),
        ],
        input_output_aliases={lent + 4: 0, lent + 5: 1} if chained else {},
        compiler_params=pltpu.CompilerParams(vmem_limit_bytes=VMEM_LIMIT),
        cost_estimate=pl.CostEstimate(
            flops=2_100_000_000 * count, bytes_accessed=6_000_000 + 9_000_000 * count, transcendentals=0
        ),
        name="groups_" + "".join(str(g) for g in groups),
    )(*args)
    return out[0], out[1], out[2:]


def combine_kernel(*refs):
    rows, hots, outs, (rows_v, hots_v, sem_rows, sem_hots) = refs[:5], refs[5:9], refs[9:13], refs[13:]
    rows = halves_of(rows, (False, False, False, True))
    loads = []
    for i in range(4):
        mine = []
        for k in range(4):
            mine.append(
                pltpu.make_async_copy(
                    hots[k].at[i], hots_v.at[i, pl.ds(k * 2 * CAP, 2 * CAP)], sem_hots.at[4 * i + k]
                )
            )
            for e in range(2):
                mine.append(
                    pltpu.make_async_copy(
                        rows[k][e].at[pl.ds(i * CAP, CAP)],
                        rows_v.at[i, pl.ds((2 * k + e) * CAP, CAP)],
                        sem_rows.at[8 * i + 2 * k + e],
                    )
                )
        for item in mine:
            item.start()
        loads.append(mine)
    for i in range(4):
        for item in loads[i]:
            item.wait()
        outs[i][...] = lax.dot_general(
            hots_v[i], rows_v[i], (((0,), (0,)), ((), ())), preferred_element_type=F32
        ).astype(BF)


def combine(rows, hots):
    anywhere = pl.BlockSpec(memory_space=pl.ANY)
    return pl.pallas_call(
        combine_kernel,
        in_specs=[anywhere] * 9,
        out_specs=[pl.BlockSpec(memory_space=pltpu.VMEM)] * 4,
        out_shape=[jax.ShapeDtypeStruct((TOK, D), BF)] * 4,
        scratch_shapes=[
            pltpu.VMEM((4, 8 * CAP, D), BF),
            pltpu.VMEM((4, 8 * CAP, TOK), BF),
            pltpu.SemaphoreType.DMA((32,)),
            pltpu.SemaphoreType.DMA((16,)),
        ],
        compiler_params=pltpu.CompilerParams(vmem_limit_bytes=VMEM_LIMIT),
        cost_estimate=pl.CostEstimate(flops=1_400_000_000, bytes_accessed=9_000_000, transcendentals=0),
        name="combine",
    )(*rows, *hots)


def compress(local_grad, residual):
    carried = local_grad * loss_unscale + residual.astype(F32)
    magnitude = jnp.mean(jnp.abs(carried), axis=-1, keepdims=True) + epsilon
    compressed = (magnitude * jnp.tanh(carried * (1.0 / magnitude))).astype(BF)
    return compressed, (carried - compressed.astype(F32)).astype(BF)


def gate_up_kernel(here, xt, gab, res_gate, res_up, keep, give_gate, give_up, left_gate, left_up, held):
    x, core, _, _ = place_of(here)
    half = pl.program_id(1)
    grads = [jnp.dot(xt[0, u * 256 : (u + 1) * 256], gab[0], preferred_element_type=F32) for u in range(2)]
    for u in range(2):
        rows = slice(u * 256, (u + 1) * 256)
        kept_at = block_place(2 * half + u, x, core)
        given_at = block_place(2 * half + u, x, 1 - core)
        for m, (res, left) in enumerate(((res_gate, left_gate), (res_up, left_up))):
            held[u, m], left[0, rows] = compress(grads[u][:, m * HID : (m + 1) * HID], res[0, rows])
            keep[kept_at, m, 0] = held[u, m, pl.ds(pl.multiple_of(core * 128, 128), 128)]
            give = (give_gate, give_up)[m]
            give[given_at, 0] = held[u, m, pl.ds(pl.multiple_of((1 - core) * 128, 128), 128)]


def gate_up_grads(here, xt, gab, res_gate, res_up):
    tile = pl.BlockSpec((1, HID, HID), lambda e, t, s: (e, t, 0))
    res_shape = jax.ShapeDtypeStruct((2, D, HID), BF)
    keep_shape = jax.ShapeDtypeStruct((SIDE, 2, 2, 128, HID), BF)
    give_shape = jax.ShapeDtypeStruct((SIDE, 2, 128, HID), BF)
    return pl.pallas_call(
        gate_up_kernel,
        grid_spec=pltpu.PrefetchScalarGridSpec(
            num_scalar_prefetch=1,
            grid=(2, 2),
            in_specs=[
                pl.BlockSpec((1, 512, 16 * CAP), lambda e, t, s: (e, t, 0)),
                pl.BlockSpec((1, 16 * CAP, 2 * HID), lambda e, t, s: (e, 0, 0)),
                tile,
                tile,
            ],
            out_specs=[pl.BlockSpec((SIDE, 2, 1, 128, HID), lambda e, t, s: (0, 0, e, 0, 0))]
            + [pl.BlockSpec((SIDE, 1, 128, HID), lambda e, t, s: (0, e, 0, 0))] * 2
            + [tile, tile],
            scratch_shapes=[pltpu.VMEM((2, 2, 256, HID), BF)],
        ),
        out_shape=[keep_shape, give_shape, give_shape, res_shape, res_shape],
        compiler_params=pltpu.CompilerParams(vmem_limit_bytes=VMEM_LIMIT),
        cost_estimate=pl.CostEstimate(flops=5_400_000_000, bytes_accessed=22_000_000, transcendentals=2_000_000),
        name="gate_up_grads",
    )(here, xt, gab, res_gate, res_up)


def down_kernel(here, ht, cot, res, keep, give, left):
    x, core, _, _ = place_of(here)
    grads = [jnp.dot(ht[0, u * 256 : (u + 1) * 256], cot[0], preferred_element_type=F32) for u in range(2)]
    for u in range(2):
        rows = slice(u * 256, (u + 1) * 256)
        compressed, left[0, rows] = compress(grads[u], res[0, rows])
        for own in range(2):

            @pl.when(core == own)
            def _():
                for owner in range(SIDE):
                    at = 2 * owner + own
                    keep[block_place(owner, x, own), 0, rows] = compressed[:, at * 128 : (at + 1) * 128]
                    at = 2 * owner + 1 - own
                    give[block_place(owner, x, 1 - own), 0, rows] = compressed[:, at * 128 : (at + 1) * 128]


def down_grads(here, ht, cot, res):
    tile = pl.BlockSpec((1, HID, D), lambda e, s: (e, 0, 0))
    blocks = jax.ShapeDtypeStruct((SIDE, 2, HID, 128), BF)
    return pl.pallas_call(
        down_kernel,
        grid_spec=pltpu.PrefetchScalarGridSpec(
            num_scalar_prefetch=1,
            grid=(2,),
            in_specs=[
                pl.BlockSpec((1, HID, 16 * CAP), lambda e, s: (e, 0, 0)),
                pl.BlockSpec((1, 16 * CAP, D), lambda e, s: (e, 0, 0)),
                tile,
            ],
            out_specs=[pl.BlockSpec((SIDE, 1, HID, 128), lambda e, s: (0, e, 0, 0))] * 2 + [tile],
        ),
        out_shape=[blocks, blocks, jax.ShapeDtypeStruct((2, HID, D), BF)],
        compiler_params=pltpu.CompilerParams(vmem_limit_bytes=VMEM_LIMIT),
        cost_estimate=pl.CostEstimate(flops=2_700_000_000, bytes_accessed=14_000_000, transcendentals=1_000_000),
        name="down_grads",
    )(here, ht, cot, res)


def total(*terms):
    out = terms[0].astype(F32)
    for term in terms[1:]:
        out = out + term.astype(F32)
    return out


def add(*terms):
    return total(*terms).astype(BF)


def partner(stage, x, core):
    return x ^ (1 if stage == core else 3)


def mean_over_dp(keep, got, beside):
    first = dp_hop(add(keep[2:], got[2:]), lambda x, c: (partner(0, x, c), c))
    first, _ = lax.optimization_barrier((first, beside))
    second = dp_hop(add(keep[1], got[1], first[1]), lambda x, c: (partner(1, x, c), c))
    return total(keep[0], got[0], first[0], second) / 8.0


def on_device(x_saved, d_out, routes, probs, w_gate, w_up, w_down, res_gate, res_up, res_down):
    here = jnp.stack([lax.axis_index("dp"), lax.axis_index("expert")]).astype(jnp.int32)

    own = pack(d_out, routes, probs)
    near = (hop(own, 0, 1), hop(own, 0, -1), hop(own, 0, 2))
    terms = forward_terms(0, here, x_saved[0], w_gate, w_up, None)
    near, terms = lax.optimization_barrier((near, terms))
    layout = (((2, 0), (2, 1), (3, 0)), ((1, 0), (1, 1), (3, 1)))
    (to_plus, to_minus), (hot1, hot2, hot3) = dispatch((1, 2, 3), layout, here, (own, *near))
    group1, group2 = hop(to_plus, 1, 1), hop(to_minus, 1, -1)
    (group0,), (hot0,) = dispatch((0,), (((0, 0), (0, 1)),), here, (own, *near))
    xt, ht, m12 = forward_terms(1, here, x_saved[0], w_gate, w_up, terms)

    run = functools.partial(groups_pass, m12=m12, wd=w_down, wg=w_gate, wu=w_up)
    cot, gab, (rows0,) = run((0,), [group0], carried=None)
    group1, group2, cot = lax.optimization_barrier((group1, group2, cot))
    group3 = (hop(group1[2], 1, 1), hop(group2[2], 1, -1))
    cot, gab, (rows1, rows2) = run((1, 2), [group1, group2], carried=(cot, gab))
    near_rows = (hop(rows2[:2], 1, 1), hop(rows1[:2], 1, -1))
    cot, gab, (rows3a, rows3b) = run((3,), [group3], carried=(cot, gab))
    half_way = (hop(rows3a, 1, 1), hop(rows3b, 1, -1))

    keep, give_gate, give_up, left_gate, left_up = gate_up_grads(here, xt, gab, res_gate[0], res_up[0])
    got_gate, got_up = (dp_hop(g, lambda x, c: (x, 1 - c)) for g in (give_gate, give_up))
    near_rows, half_way, ht, left_gate = lax.optimization_barrier((near_rows, half_way, ht, left_gate))
    far_rows = (hop(half_way[0], 1, 1), hop(half_way[1], 1, -1))
    keep_down, give_down, left_down = down_grads(here, ht, cot, res_down[0])
    near_rows, far_rows, got_gate, got_up, give_down = lax.optimization_barrier(
        (near_rows, far_rows, got_gate, got_up, give_down)
    )
    got_down = dp_hop(give_down, lambda x, c: (x, 1 - c))

    mine, before, behind, across = combine((rows0, *near_rows, *far_rows), (hot0, hot1, hot2, hot3))
    terms = (mine, hop(behind, 0, 1), hop(before, 0, -1), hop(across, 0, 2))
    mean = mean_over_dp(keep, jnp.stack([got_gate, got_up], axis=1), mine)
    mean_down = mean_over_dp(keep_down, got_down, terms)
    terms, mean, mean_down = lax.optimization_barrier((terms, mean, mean_down))
    d_tokens = add(*terms)
    return (d_tokens, mean[0], mean[1], mean_down, left_gate[None], left_up[None], left_down[None])


def solution(mesh):
    in_specs = (
        P("dp", "expert", None, None),
        P(("dp", "expert"), None),
        P(("dp", "expert"), None),
        P(("dp", "expert"), None),
        P("expert", None, None),
        P("expert", None, None),
        P("expert", None, None),
        P("dp", "expert", None, None),
        P("dp", "expert", None, None),
        P("dp", "expert", None, None),
    )
    out_specs = (
        P(("dp", "expert"), None),
        P("expert", "dp", None),
        P("expert", "dp", None),
        P("expert", None, "dp"),
        P("dp", "expert", None, None),
        P("dp", "expert", None, None),
        P("dp", "expert", None, None),
    )
    return jax.shard_map(
        on_device, mesh=mesh, in_specs=in_specs, out_specs=out_specs, check_vma=False
    )
```

```python
import functools

import jax
import jax.numpy as jnp
from jax import lax
from jax.experimental import pallas as pl
from jax.experimental.pallas import tpu as pltpu
from jax.sharding import PartitionSpec as P

loss_unscale = 0.0625
epsilon = 1e-05

SIDE = 4
OFFSETS = (0, -1, 1, 2)
CAP = 80
TOK = 256
PACK = TOK + 16
D = 1024
HID = 512
BF = jnp.bfloat16
F32 = jnp.float32
VMEM_LIMIT = 30 * 2**20


def place_of(here):
    core = here[0] & 1
    z, y = here[1] // SIDE, here[1] & (SIDE - 1)
    return here[0] // 2, core, jnp.where(core == 0, z, y), jnp.where(core == 0, y, z)


def expert_at(here, first_off, second_off):
    _, core, first, second = place_of(here)
    first, second = (first + first_off + SIDE) & (SIDE - 1), (second + second_off + SIDE) & (SIDE - 1)
    return jnp.where(core == 0, first * SIDE + second, second * SIDE + first)


def block_place(owner, x, core):
    apart = owner ^ x
    return jnp.where(apart == 0, 0, jnp.where(apart == 1, 2 - core, jnp.where(apart == 2, 3, 1 + core)))


def pairs(axis, step):
    out = []
    for dp in range(8):
        core = dp % 2
        for z in range(SIDE):
            for y in range(SIDE):
                along_z = (axis == 0) == (core == 0)
                z2, y2 = ((z + step) % SIDE, y) if along_z else (z, (y + step) % SIDE)
                out.append((dp * 16 + z * SIDE + y, dp * 16 + z2 * SIDE + y2))
    return out


def hop(value, axis, step):
    return lax.ppermute(value, ("dp", "expert"), pairs(axis, step))


def dp_hop(value, move):
    return lax.ppermute(
        value, "dp", [(x * 2 + c, move(x, c)[0] % SIDE * 2 + move(x, c)[1]) for x in range(SIDE) for c in range(2)]
    )


def nt(left, right):
    return lax.dot_general(left, right, (((1,), (1,)), ((), ())), preferred_element_type=F32)


def pack_kernel(tokens, routes, probs, out):
    out[:TOK, :] = tokens[...]
    weights = probs[...]
    high = weights.astype(BF)
    left = weights - high.astype(F32)
    middle = left.astype(BF)
    low = (left - middle.astype(F32)).astype(BF)
    out[TOK : TOK + 8, :] = jnp.concatenate(
        [routes[...].astype(F32).astype(BF), high, middle, low], axis=1
    )
    out[TOK + 8 :, :] = jnp.zeros((8, D), BF)


def pack(tokens, routes, probs):
    return pl.pallas_call(
        pack_kernel,
        out_shape=jax.ShapeDtypeStruct((PACK, D), BF),
        cost_estimate=pl.CostEstimate(flops=0, bytes_accessed=1_100_000, transcendentals=0),
        name="pack",
    )(tokens, routes.T, probs.T)


def forward_kernel(chained, here, *refs):
    xs, (wg, wu), refs = refs[:8], refs[8:10], refs[10 + (3 if chained else 0) :]
    xt, ht, m12, rows = refs
    for i in range(8):
        rows[i * CAP : (i + 1) * CAP, :] = xs[i][0, 0]
    half = 4 * CAP
    pre = []
    for h in range(2):
        saved = rows[h * half : (h + 1) * half, :]
        pre.append(
            (
                jnp.dot(saved, wg[0], preferred_element_type=F32),
                jnp.dot(saved, wu[0], preferred_element_type=F32),
            )
        )
    xt[0] = rows[...].T
    hidden = []
    for h, (gate, up) in enumerate(pre):
        logistic = jax.nn.sigmoid(gate)
        act = gate * logistic
        m12[0, h * half : (h + 1) * half, :HID] = up * (logistic * (1.0 + gate * (1.0 - logistic)))
        m12[0, h * half : (h + 1) * half, HID:] = act
        hidden.append((act * up).astype(BF))
    ht[0] = jnp.concatenate(hidden, axis=0).T


def forward_terms(e, here, x, wg, wu, carried):
    blocks = x.reshape(2, 16, CAP, D)
    chained = carried is not None

    def block_at(i):
        def at(h, here):
            return e, expert_at(here, OFFSETS[i % 4], h if i < 4 else 3 * h - 1), 0, 0

        return pl.BlockSpec((1, 1, CAP, D), at)

    half = 8 * CAP
    return pl.pallas_call(
        functools.partial(forward_kernel, chained),
        grid_spec=pltpu.PrefetchScalarGridSpec(
            num_scalar_prefetch=1,
            grid=(2,),
            in_specs=[block_at(i) for i in range(8)]
            + [pl.BlockSpec((1, D, HID), lambda h, p: (e, 0, 0))] * 2
            + [pl.BlockSpec(memory_space=pl.ANY)] * (3 if chained else 0),
            out_specs=[
                pl.BlockSpec((1, D, half), lambda h, p: (e, 0, h)),
                pl.BlockSpec((1, HID, half), lambda h, p: (e, 0, h)),
                pl.BlockSpec((1, half, 2 * HID), lambda h, p: (e, h, 0)),
            ],
            scratch_shapes=[pltpu.VMEM((half, D), BF)],
        ),
        out_shape=[
            jax.ShapeDtypeStruct((2, D, 16 * CAP), BF),
            jax.ShapeDtypeStruct((2, HID, 16 * CAP), BF),
            jax.ShapeDtypeStruct((2, 16 * CAP, 2 * HID), F32),
        ],
        input_output_aliases={11 + i: i for i in range(3)} if chained else {},
        compiler_params=pltpu.CompilerParams(vmem_limit_bytes=VMEM_LIMIT),
        cost_estimate=pl.CostEstimate(flops=2_700_000_000, bytes_accessed=15_000_000, transcendentals=655_360),
        name="forward_terms",
    )(here, *([blocks] * 8), wg, wu, *(carried or ()))


def dispatch_kernel(targets, layout, here, *refs):
    blocks, outs, hots = refs[:4], refs[4 : 4 + len(layout)], refs[4 + len(layout) :]
    before = (
        lax.broadcasted_iota(jnp.int32, (TOK, TOK), 0) < lax.broadcasted_iota(jnp.int32, (TOK, TOK), 1)
    ).astype(BF)
    slot = lax.broadcasted_iota(jnp.int32, (CAP, TOK), 0).astype(F32)
    names = [(2 * expert_at(here, 0, OFFSETS[t]) + e).astype(F32) for t in targets for e in range(2)]
    named, weights = [], []
    for i in range(4):
        meta = blocks[i][TOK:, :].astype(F32)[:8]
        routes = meta[:, :TOK]
        probs = meta[:, TOK : 2 * TOK] + meta[:, 2 * TOK : 3 * TOK] + meta[:, 3 * TOK :]
        for name in names:
            hit = routes == name
            named.append(jnp.sum(jnp.where(hit, 1.0, 0.0), axis=0, keepdims=True))
            weights.append(jnp.sum(jnp.where(hit, probs, 0.0), axis=0, keepdims=True))
    mask = jnp.concatenate(named, axis=0)
    rank = jnp.dot(mask.astype(BF), before, preferred_element_type=F32)
    key = jnp.where(mask > 0.5, rank, -1.0)
    per = len(names)
    for i in range(4):
        halves, scales = [], []
        for k in range(per):
            hit = slot == key[per * i + k : per * i + k + 1, :]
            halves.append(jnp.where(hit, 1.0, 0.0).astype(BF))
            scales.append(jnp.sum(jnp.where(hit, weights[per * i + k], 0.0), axis=1, keepdims=True))
            hots[k // 2][i, k % 2 * CAP : (k % 2 + 1) * CAP, :] = halves[k]
        chosen = jnp.concatenate(halves, axis=0)
        taken = jnp.dot(chosen, blocks[i][:TOK, :], preferred_element_type=F32)
        scaled = (taken * jnp.concatenate(scales, axis=0)).astype(BF)
        for out, held in zip(outs, layout):
            for n, (target, e) in enumerate(held):
                k = 2 * targets.index(target) + e
                out[n, i * CAP : (i + 1) * CAP, :] = scaled[k * CAP : (k + 1) * CAP]


def dispatch(targets, layout, here, blocks):
    whole = pl.BlockSpec(memory_space=pltpu.VMEM)
    out = pl.pallas_call(
        functools.partial(dispatch_kernel, targets, layout),
        in_specs=[pl.BlockSpec(memory_space=pltpu.SMEM)] + [whole] * 4,
        out_specs=[whole] * (len(layout) + len(targets)),
        out_shape=[jax.ShapeDtypeStruct((len(held), 4 * CAP, D), BF) for held in layout]
        + [jax.ShapeDtypeStruct((4, 2 * CAP, TOK), BF)] * len(targets),
        compiler_params=pltpu.CompilerParams(vmem_limit_bytes=VMEM_LIMIT),
        cost_estimate=pl.CostEstimate(
            flops=400_000_000 * len(targets), bytes_accessed=6_000_000, transcendentals=0
        ),
        name="dispatch_" + "".join(str(t) for t in targets),
    )(here, *blocks)
    return out[: len(layout)], out[len(layout) :]


class Copies:
    def __init__(self, semaphores):
        self.semaphores, self.started = semaphores, []

    def start(self, source, target):
        copy = pltpu.make_async_copy(source, target, self.semaphores.at[len(self.started)])
        copy.start()
        self.started.append(copy)
        return copy

    def wait(self):
        for copy in self.started:
            copy.wait()


def halves_of(refs, split):
    out = []
    for two in split:
        out.append([refs[0], refs[1]] if two else [refs[0].at[0], refs[0].at[1]])
        refs = refs[2 if two else 1 :]
    return out


def groups_kernel(groups, split, chained, *refs):
    count = len(groups)
    lent = count + sum(split)
    arrived = halves_of(refs[:lent], split)
    m12, wd, wg, wu = refs[lent : lent + 4]
    refs = refs[lent + 4 + (1 if chained else 0) :]
    gab, outs, refs = refs[0], halves_of(refs[1 : 1 + lent], split), refs[1 + lent :]
    m12_v, wd_v, wg_v, wu_v, cot_v, gab_v, rows_v, sem_in, sem_out = refs
    loads, stores, cot_loads, factor_loads = Copies(sem_in), Copies(sem_out), [], []
    load, store = loads.start, stores.start

    down_loads, weight_loads = [], []
    for n, group in enumerate(groups):
        cot_loads.append([load(arrived[n][e], cot_v.at[n, e]) for e in range(2)])
        if n == 0:
            down_loads = [load(wd.at[e], wd_v.at[e]) for e in range(2)]
        factor_loads.append(
            [load(m12.at[e, pl.ds(group * 4 * CAP, 4 * CAP)], m12_v.at[n, e]) for e in range(2)]
        )
        if n == 0:
            weight_loads = [[load(wg.at[e], wg_v.at[e]), load(wu.at[e], wu_v.at[e])] for e in range(2)]
    for n, group in enumerate(groups):
        place = pl.ds(group * 4 * CAP, 4 * CAP)
        for e in range(2):
            cot_loads[n][e].wait()
            if n == 0:
                down_loads[e].wait()
            grad_hidden = nt(cot_v[n, e], wd_v[e])
            factor_loads[n][e].wait()
            gab_v[n, e, :, :HID] = (grad_hidden * m12_v[n, e, :, :HID]).astype(BF)
            gab_v[n, e, :, HID:] = (grad_hidden * m12_v[n, e, :, HID:]).astype(BF)
            store(gab_v.at[n, e], gab.at[e, place])
        for e in range(2):
            if n == 0:
                for item in weight_loads[e]:
                    item.wait()
            rows_v[n, e] = (nt(gab_v[n, e, :, :HID], wg_v[e]) + nt(gab_v[n, e, :, HID:], wu_v[e])).astype(BF)
            store(rows_v.at[n, e], outs[n][e])
    stores.wait()


def groups_pass(groups, arrived, m12, wd, wg, wu, carried):
    chained = carried is not None
    count = len(groups)
    anywhere = pl.BlockSpec(memory_space=pl.ANY)
    slots = jax.ShapeDtypeStruct((2, 16 * CAP, D), BF)
    split = [isinstance(a, tuple) for a in arrived]
    lent = count + sum(split)
    args = [a for two, a in zip(split, arrived) for a in (a if two else (a,))]
    args += [m12, wd, wg, wu] + ([carried] if chained else [])
    row_shapes = []
    for two in split:
        shape = (4 * CAP, D) if two else (2, 4 * CAP, D)
        row_shapes += [jax.ShapeDtypeStruct(shape, BF)] * (2 if two else 1)
    out = pl.pallas_call(
        functools.partial(groups_kernel, groups, split, chained),
        in_specs=[anywhere] * len(args),
        out_specs=[anywhere] * (1 + lent),
        out_shape=[slots] + row_shapes,
        scratch_shapes=[
            pltpu.VMEM((count, 2, 4 * CAP, 2 * HID), F32),
            pltpu.VMEM((2, HID, D), BF),
            pltpu.VMEM((2, D, HID), BF),
            pltpu.VMEM((2, D, HID), BF),
            pltpu.VMEM((count, 2, 4 * CAP, D), BF),
            pltpu.VMEM((count, 2, 4 * CAP, 2 * HID), BF),
            pltpu.VMEM((count, 2, 4 * CAP, D), BF),
            pltpu.SemaphoreType.DMA((6 + 4 * count,)),
            pltpu.SemaphoreType.DMA((4 * count,)),
        ],
        input_output_aliases={lent + 4: 0} if chained else {},
        compiler_params=pltpu.CompilerParams(vmem_limit_bytes=VMEM_LIMIT),
        cost_estimate=pl.CostEstimate(
            flops=2_100_000_000 * count, bytes_accessed=6_000_000 + 9_000_000 * count, transcendentals=0
        ),
        name="groups_" + "".join(str(g) for g in groups),
    )(*args)
    return out[0], out[1:]


def combine_kernel(*refs):
    rows, hots, outs, (rows_v, hots_v, sem_rows, sem_hots) = refs[:5], refs[5:9], refs[9:13], refs[13:]
    rows = halves_of(rows, (False, False, False, True))
    loads = []
    for i in range(4):
        mine = []
        for k in range(4):
            mine.append(
                pltpu.make_async_copy(
                    hots[k].at[i], hots_v.at[i, pl.ds(k * 2 * CAP, 2 * CAP)], sem_hots.at[4 * i + k]
                )
            )
            for e in range(2):
                mine.append(
                    pltpu.make_async_copy(
                        rows[k][e].at[pl.ds(i * CAP, CAP)],
                        rows_v.at[i, pl.ds((2 * k + e) * CAP, CAP)],
                        sem_rows.at[8 * i + 2 * k + e],
                    )
                )
        for item in mine:
            item.start()
        loads.append(mine)
    for i in range(4):
        for item in loads[i]:
            item.wait()
        outs[i][...] = lax.dot_general(
            hots_v[i], rows_v[i], (((0,), (0,)), ((), ())), preferred_element_type=F32
        ).astype(BF)


def combine(rows, hots):
    anywhere = pl.BlockSpec(memory_space=pl.ANY)
    return pl.pallas_call(
        combine_kernel,
        in_specs=[anywhere] * 9,
        out_specs=[pl.BlockSpec(memory_space=pltpu.VMEM)] * 4,
        out_shape=[jax.ShapeDtypeStruct((TOK, D), BF)] * 4,
        scratch_shapes=[
            pltpu.VMEM((4, 8 * CAP, D), BF),
            pltpu.VMEM((4, 8 * CAP, TOK), BF),
            pltpu.SemaphoreType.DMA((32,)),
            pltpu.SemaphoreType.DMA((16,)),
        ],
        compiler_params=pltpu.CompilerParams(vmem_limit_bytes=VMEM_LIMIT),
        cost_estimate=pl.CostEstimate(flops=1_400_000_000, bytes_accessed=9_000_000, transcendentals=0),
        name="combine",
    )(*rows, *hots)


def compress(local_grad, residual):
    carried = local_grad * loss_unscale + residual.astype(F32)
    magnitude = jnp.mean(jnp.abs(carried), axis=-1, keepdims=True) + epsilon
    compressed = (magnitude * jnp.tanh(carried * (1.0 / magnitude))).astype(BF)
    return compressed, (carried - compressed.astype(F32)).astype(BF)


def gate_up_kernel(here, xt, gab, res_gate, res_up, keep, give_gate, give_up, left_gate, left_up, *scratch):
    xt_v, gab_v, res_v, left_v, keep_v, give_v, held, sem_in, sem_out = scratch
    x, core, _, _ = place_of(here)
    loads, stores, waits = Copies(sem_in), Copies(sem_out), {}
    half = D // 2
    for e in range(2):
        waits[e, 0] = [
            loads.start(xt.at[e, pl.ds(0, half)], xt_v.at[e, pl.ds(0, half)]),
            loads.start(gab.at[e], gab_v.at[e]),
            loads.start(res_gate.at[e], res_v.at[e, 0]),
            loads.start(res_up.at[e], res_v.at[e, 1]),
        ]
        waits[e, 2] = [loads.start(xt.at[e, pl.ds(half, half)], xt_v.at[e, pl.ds(half, half)])]
    for e in range(2):
        for t in range(SIDE):
            for item in waits.get((e, t), ()):
                item.wait()
            rows = pl.ds(t * 256, 256)
            grads = jnp.dot(xt_v[e, rows], gab_v[e], preferred_element_type=F32)
            kept_at, given_at = block_place(t, x, core), block_place(t, x, 1 - core)
            for m, left in enumerate((left_gate, left_up)):
                held[m], left_v[e, m, rows] = compress(grads[:, m * HID : (m + 1) * HID], res_v[e, m, rows])
                keep_v[kept_at, m, e] = held[m, pl.ds(pl.multiple_of(core * 128, 128), 128)]
                give_v[given_at, m, e] = held[m, pl.ds(pl.multiple_of((1 - core) * 128, 128), 128)]
                stores.start(left_v.at[e, m, rows], left.at[e, rows])
        for m, give in enumerate((give_gate, give_up)):
            stores.start(give_v.at[:, m, e], give.at[:, e])
        stores.start(keep_v.at[:, :, e], keep.at[:, :, e])
    stores.wait()


def gate_up_grads(here, xt, gab, res_gate, res_up):
    anywhere = pl.BlockSpec(memory_space=pl.ANY)
    res_shape = jax.ShapeDtypeStruct((2, D, HID), BF)
    give_shape = jax.ShapeDtypeStruct((SIDE, 2, 128, HID), BF)
    return pl.pallas_call(
        gate_up_kernel,
        in_specs=[pl.BlockSpec(memory_space=pltpu.SMEM)] + [anywhere] * 4,
        out_specs=[anywhere] * 5,
        out_shape=[
            jax.ShapeDtypeStruct((SIDE, 2, 2, 128, HID), BF), give_shape, give_shape, res_shape, res_shape
        ],
        scratch_shapes=[
            pltpu.VMEM((2, D, 16 * CAP), BF),
            pltpu.VMEM((2, 16 * CAP, 2 * HID), BF),
            pltpu.VMEM((2, 2, D, HID), BF),
            pltpu.VMEM((2, 2, D, HID), BF),
            pltpu.VMEM((SIDE, 2, 2, 128, HID), BF),
            pltpu.VMEM((SIDE, 2, 2, 128, HID), BF),
            pltpu.VMEM((2, 256, HID), BF),
            pltpu.SemaphoreType.DMA((10,)),
            pltpu.SemaphoreType.DMA((22,)),
        ],
        compiler_params=pltpu.CompilerParams(vmem_limit_bytes=VMEM_LIMIT),
        cost_estimate=pl.CostEstimate(flops=5_400_000_000, bytes_accessed=22_000_000, transcendentals=2_000_000),
        name="gate_up_grads",
    )(here, xt, gab, res_gate, res_up)


def down_kernel(split, here, ht, res, *refs):
    lent = 4 + sum(split)
    arrived, (keep, give, left) = halves_of(refs[:lent], split), refs[lent : lent + 3]
    ht_v, cot_v, res_v, left_v, sent_v, sem_in, sem_out = refs[lent + 3 :]
    x, core, _, _ = place_of(here)
    loads, stores, waits = Copies(sem_in), Copies(sem_out), {}
    for e in range(2):
        waits[e] = [loads.start(ht.at[e], ht_v.at[e])]
        waits[e] += [
            loads.start(arrived[g][e], cot_v.at[e, pl.ds(g * 4 * CAP, 4 * CAP)]) for g in range(4)
        ]
        waits[e] += [loads.start(res.at[e], res_v.at[e])]
    for e in range(2):
        for item in waits[e]:
            item.wait()
        for t in range(2):
            rows = pl.ds(t * 256, 256)
            grads = jnp.dot(ht_v[e, rows], cot_v[e], preferred_element_type=F32)
            compressed, left_v[e, rows] = compress(grads, res_v[e, rows])
            stores.start(left_v.at[e, rows], left.at[e, rows])
            for owner in range(SIDE):
                for c in range(2):
                    at = 2 * owner + c
                    sent_v[core ^ c, block_place(owner, x, c), e, rows] = compressed[:, at * 128 : (at + 1) * 128]
        stores.start(sent_v.at[0, :, e], keep.at[:, e])
        stores.start(sent_v.at[1, :, e], give.at[:, e])
    stores.wait()


def down_grads(here, ht, arrived, res):
    anywhere = pl.BlockSpec(memory_space=pl.ANY)
    blocks = jax.ShapeDtypeStruct((SIDE, 2, HID, 128), BF)
    split = [isinstance(a, tuple) for a in arrived]
    pieces = [a for two, one in zip(split, arrived) for a in (one if two else (one,))]
    return pl.pallas_call(
        functools.partial(down_kernel, split),
        in_specs=[pl.BlockSpec(memory_space=pltpu.SMEM)] + [anywhere] * (2 + len(pieces)),
        out_specs=[anywhere] * 3,
        out_shape=[blocks, blocks, jax.ShapeDtypeStruct((2, HID, D), BF)],
        scratch_shapes=[
            pltpu.VMEM((2, HID, 16 * CAP), BF),
            pltpu.VMEM((2, 16 * CAP, D), BF),
            pltpu.VMEM((2, HID, D), BF),
            pltpu.VMEM((2, HID, D), BF),
            pltpu.VMEM((2, SIDE, 2, HID, 128), BF),
            pltpu.SemaphoreType.DMA((12,)),
            pltpu.SemaphoreType.DMA((8,)),
        ],
        compiler_params=pltpu.CompilerParams(vmem_limit_bytes=VMEM_LIMIT),
        cost_estimate=pl.CostEstimate(flops=2_700_000_000, bytes_accessed=14_000_000, transcendentals=1_000_000),
        name="down_grads",
    )(here, ht, res, *pieces)


def total(*terms):
    out = terms[0].astype(F32)
    for term in terms[1:]:
        out = out + term.astype(F32)
    return out


def add(*terms):
    return total(*terms).astype(BF)


def partner(stage, x, core):
    return x ^ (1 if stage == core else 3)


def mean_over_dp(keep, got, beside):
    first = dp_hop(add(keep[2:], got[2:]), lambda x, c: (partner(0, x, c), c))
    first, _ = lax.optimization_barrier((first, beside))
    second = dp_hop(add(keep[1], got[1], first[1]), lambda x, c: (partner(1, x, c), c))
    return total(keep[0], got[0], first[0], second) / 8.0


def on_device(x_saved, d_out, routes, probs, w_gate, w_up, w_down, res_gate, res_up, res_down):
    here = jnp.stack([lax.axis_index("dp"), lax.axis_index("expert")]).astype(jnp.int32)

    own = pack(d_out, routes, probs)
    near = (hop(own, 0, 1), hop(own, 0, -1), hop(own, 0, 2))
    terms = forward_terms(0, here, x_saved[0], w_gate, w_up, None)
    near, terms = lax.optimization_barrier((near, terms))
    layout = (((2, 0), (2, 1), (3, 0)), ((1, 0), (1, 1), (3, 1)))
    (to_plus, to_minus), (hot1, hot2, hot3) = dispatch((1, 2, 3), layout, here, (own, *near))
    group1, group2 = hop(to_plus, 1, 1), hop(to_minus, 1, -1)
    (group0,), (hot0,) = dispatch((0,), (((0, 0), (0, 1)),), here, (own, *near))
    xt, ht, m12 = forward_terms(1, here, x_saved[0], w_gate, w_up, terms)

    run = functools.partial(groups_pass, m12=m12, wd=w_down, wg=w_gate, wu=w_up)
    gab, (rows0,) = run((0,), [group0], carried=None)
    group1, group2, gab = lax.optimization_barrier((group1, group2, gab))
    group3 = (hop(group1[2], 1, 1), hop(group2[2], 1, -1))
    gab, (rows1, rows2) = run((1, 2), [group1, group2], carried=gab)
    near_rows = (hop(rows2[:2], 1, 1), hop(rows1[:2], 1, -1))
    gab, (rows3a, rows3b) = run((3,), [group3], carried=gab)
    half_way = (hop(rows3a, 1, 1), hop(rows3b, 1, -1))

    keep, give_gate, give_up, left_gate, left_up = gate_up_grads(here, xt, gab, res_gate[0], res_up[0])
    near_rows, give_gate, give_up = lax.optimization_barrier((near_rows, give_gate, give_up))
    got_gate, got_up = (dp_hop(g, lambda x, c: (x, 1 - c)) for g in (give_gate, give_up))
    half_way, got_gate, got_up, ht = lax.optimization_barrier((half_way, got_gate, got_up, ht))
    far_rows = (hop(half_way[0], 1, 1), hop(half_way[1], 1, -1))
    keep_down, give_down, left_down = down_grads(here, ht, (group0, group1, group2, group3), res_down[0])
    far_rows, give_down = lax.optimization_barrier((far_rows, give_down))
    got_down = dp_hop(give_down, lambda x, c: (x, 1 - c))

    mine, before, behind, across = combine((rows0, *near_rows, *far_rows), (hot0, hot1, hot2, hot3))
    terms = (mine, hop(behind, 0, 1), hop(before, 0, -1), hop(across, 0, 2))
    mean = mean_over_dp(keep, jnp.stack([got_gate, got_up], axis=1), mine)
    mean_down = mean_over_dp(keep_down, got_down, terms)
    terms, mean, mean_down = lax.optimization_barrier((terms, mean, mean_down))
    d_tokens = add(*terms)
    return (d_tokens, mean[0], mean[1], mean_down, left_gate[None], left_up[None], left_down[None])


def solution(mesh):
    in_specs = (
        P("dp", "expert", None, None),
        P(("dp", "expert"), None),
        P(("dp", "expert"), None),
        P(("dp", "expert"), None),
        P("expert", None, None),
        P("expert", None, None),
        P("expert", None, None),
        P("dp", "expert", None, None),
        P("dp", "expert", None, None),
        P("dp", "expert", None, None),
    )
    out_specs = (
        P(("dp", "expert"), None),
        P("expert", "dp", None),
        P("expert", "dp", None),
        P("expert", None, "dp"),
        P("dp", "expert", None, None),
        P("dp", "expert", None, None),
        P("dp", "expert", None, None),
    )
    return jax.shard_map(
        on_device, mesh=mesh, in_specs=in_specs, out_specs=out_specs, check_vma=False
    )
```

```python
import functools

import jax
import jax.numpy as jnp
from jax import lax
from jax.experimental import pallas as pl
from jax.experimental.pallas import tpu as pltpu
from jax.sharding import PartitionSpec as P

loss_unscale = 0.0625
epsilon = 1e-05

SIDE = 4
OFFSETS = (0, -1, 1, 2)
CAP = 80
TOK = 256
PACK = TOK + 16
D = 1024
HID = 512
BF = jnp.bfloat16
F32 = jnp.float32
VMEM_LIMIT = 56 * 2**20


def place_of(here):
    core = here[0] & 1
    z, y = here[1] // SIDE, here[1] & (SIDE - 1)
    return here[0] // 2, core, jnp.where(core == 0, z, y), jnp.where(core == 0, y, z)


def expert_at(here, first_off, second_off):
    _, core, first, second = place_of(here)
    first, second = (first + first_off + SIDE) & (SIDE - 1), (second + second_off + SIDE) & (SIDE - 1)
    return jnp.where(core == 0, first * SIDE + second, second * SIDE + first)


def block_place(owner, x, core):
    apart = owner ^ x
    return jnp.where(apart == 0, 0, jnp.where(apart == 1, 2 - core, jnp.where(apart == 2, 3, 1 + core)))


def pairs(axis, step):
    out = []
    for dp in range(8):
        core = dp % 2
        for z in range(SIDE):
            for y in range(SIDE):
                along_z = (axis == 0) == (core == 0)
                z2, y2 = ((z + step) % SIDE, y) if along_z else (z, (y + step) % SIDE)
                out.append((dp * 16 + z * SIDE + y, dp * 16 + z2 * SIDE + y2))
    return out


def hop(value, axis, step):
    return lax.ppermute(value, ("dp", "expert"), pairs(axis, step))


def dp_hop(value, move):
    return lax.ppermute(
        value, "dp", [(x * 2 + c, move(x, c)[0] % SIDE * 2 + move(x, c)[1]) for x in range(SIDE) for c in range(2)]
    )


def nt(left, right):
    return lax.dot_general(left, right, (((1,), (1,)), ((), ())), preferred_element_type=F32)


def pack_kernel(tokens, routes, probs, out):
    out[:TOK, :] = tokens[...]
    weights = probs[...]
    high = weights.astype(BF)
    left = weights - high.astype(F32)
    middle = left.astype(BF)
    low = (left - middle.astype(F32)).astype(BF)
    out[TOK : TOK + 8, :] = jnp.concatenate(
        [routes[...].astype(F32).astype(BF), high, middle, low], axis=1
    )
    out[TOK + 8 :, :] = jnp.zeros((8, D), BF)


def pack(tokens, routes, probs):
    return pl.pallas_call(
        pack_kernel,
        out_shape=jax.ShapeDtypeStruct((PACK, D), BF),
        cost_estimate=pl.CostEstimate(flops=0, bytes_accessed=1_100_000, transcendentals=0),
        name="pack",
    )(tokens, routes.T, probs.T)


def forward_kernel(chained, here, *refs):
    xs, (wg, wu), refs = refs[:8], refs[8:10], refs[10 + (3 if chained else 0) :]
    xt, ht, m12, rows = refs
    for i in range(8):
        rows[i * CAP : (i + 1) * CAP, :] = xs[i][0, 0]
    half = 4 * CAP
    pre = []
    for h in range(2):
        saved = rows[h * half : (h + 1) * half, :]
        pre.append(
            (
                jnp.dot(saved, wg[0], preferred_element_type=F32),
                jnp.dot(saved, wu[0], preferred_element_type=F32),
            )
        )
    xt[0] = rows[...].T
    hidden = []
    for h, (gate, up) in enumerate(pre):
        logistic = jax.nn.sigmoid(gate)
        act = gate * logistic
        m12[0, h * half : (h + 1) * half, :HID] = (up * (logistic * (1.0 + gate * (1.0 - logistic)))).astype(BF)
        m12[0, h * half : (h + 1) * half, HID:] = act.astype(BF)
        hidden.append((act * up).astype(BF))
    ht[0] = jnp.concatenate(hidden, axis=0).T


def forward_terms(e, here, x, wg, wu, carried):
    blocks = x.reshape(2, 16, CAP, D)
    chained = carried is not None

    def block_at(i):
        def at(h, here):
            return e, expert_at(here, OFFSETS[i % 4], h if i < 4 else 3 * h - 1), 0, 0

        return pl.BlockSpec((1, 1, CAP, D), at)

    half = 8 * CAP
    return pl.pallas_call(
        functools.partial(forward_kernel, chained),
        grid_spec=pltpu.PrefetchScalarGridSpec(
            num_scalar_prefetch=1,
            grid=(2,),
            in_specs=[block_at(i) for i in range(8)]
            + [pl.BlockSpec((1, D, HID), lambda h, p: (e, 0, 0))] * 2
            + [pl.BlockSpec(memory_space=pl.ANY)] * (3 if chained else 0),
            out_specs=[
                pl.BlockSpec((1, D, half), lambda h, p: (e, 0, h)),
                pl.BlockSpec((1, HID, half), lambda h, p: (e, 0, h)),
                pl.BlockSpec((1, half, 2 * HID), lambda h, p: (e, h, 0)),
            ],
            scratch_shapes=[pltpu.VMEM((half, D), BF)],
        ),
        out_shape=[
            jax.ShapeDtypeStruct((2, D, 16 * CAP), BF),
            jax.ShapeDtypeStruct((2, HID, 16 * CAP), BF),
            jax.ShapeDtypeStruct((2, 16 * CAP, 2 * HID), BF),
        ],
        input_output_aliases={11 + i: i for i in range(3)} if chained else {},
        compiler_params=pltpu.CompilerParams(vmem_limit_bytes=VMEM_LIMIT),
        cost_estimate=pl.CostEstimate(flops=2_700_000_000, bytes_accessed=15_000_000, transcendentals=655_360),
        name="forward_terms",
    )(here, *([blocks] * 8), wg, wu, *(carried or ()))


def dispatch_kernel(targets, layout, here, *refs):
    blocks, outs, hots = refs[:4], refs[4 : 4 + len(layout)], refs[4 + len(layout) :]
    before = (
        lax.broadcasted_iota(jnp.int32, (TOK, TOK), 0) < lax.broadcasted_iota(jnp.int32, (TOK, TOK), 1)
    ).astype(BF)
    slot = lax.broadcasted_iota(jnp.int32, (CAP, TOK), 0).astype(F32)
    names = [(2 * expert_at(here, 0, OFFSETS[t]) + e).astype(F32) for t in targets for e in range(2)]
    named, weights = [], []
    for i in range(4):
        meta = blocks[i][TOK:, :].astype(F32)[:8]
        routes = meta[:, :TOK]
        probs = meta[:, TOK : 2 * TOK] + meta[:, 2 * TOK : 3 * TOK] + meta[:, 3 * TOK :]
        for name in names:
            hit = routes == name
            named.append(jnp.sum(jnp.where(hit, 1.0, 0.0), axis=0, keepdims=True))
            weights.append(jnp.sum(jnp.where(hit, probs, 0.0), axis=0, keepdims=True))
    mask = jnp.concatenate(named, axis=0)
    rank = jnp.dot(mask.astype(BF), before, preferred_element_type=F32)
    key = jnp.where(mask > 0.5, rank, -1.0)
    per = len(names)
    for i in range(4):
        halves, scales = [], []
        for k in range(per):
            hit = slot == key[per * i + k : per * i + k + 1, :]
            halves.append(jnp.where(hit, 1.0, 0.0).astype(BF))
            scales.append(jnp.sum(jnp.where(hit, weights[per * i + k], 0.0), axis=1, keepdims=True))
            hots[k // 2][i, k % 2 * CAP : (k % 2 + 1) * CAP, :] = halves[k]
        chosen = jnp.concatenate(halves, axis=0)
        taken = jnp.dot(chosen, blocks[i][:TOK, :], preferred_element_type=F32)
        scaled = (taken * jnp.concatenate(scales, axis=0)).astype(BF)
        for out, held in zip(outs, layout):
            for n, (target, e) in enumerate(held):
                k = 2 * targets.index(target) + e
                out[n, i * CAP : (i + 1) * CAP, :] = scaled[k * CAP : (k + 1) * CAP]


def dispatch(targets, layout, here, blocks):
    whole = pl.BlockSpec(memory_space=pltpu.VMEM)
    out = pl.pallas_call(
        functools.partial(dispatch_kernel, targets, layout),
        in_specs=[pl.BlockSpec(memory_space=pltpu.SMEM)] + [whole] * 4,
        out_specs=[whole] * (len(layout) + len(targets)),
        out_shape=[jax.ShapeDtypeStruct((len(held), 4 * CAP, D), BF) for held in layout]
        + [jax.ShapeDtypeStruct((4, 2 * CAP, TOK), BF)] * len(targets),
        compiler_params=pltpu.CompilerParams(vmem_limit_bytes=VMEM_LIMIT),
        cost_estimate=pl.CostEstimate(
            flops=400_000_000 * len(targets), bytes_accessed=6_000_000, transcendentals=0
        ),
        name="dispatch_" + "".join(str(t) for t in targets),
    )(here, *blocks)
    return out[: len(layout)], out[len(layout) :]


class Copies:
    def __init__(self, semaphores):
        self.semaphores, self.started = semaphores, []

    def start(self, source, target):
        copy = pltpu.make_async_copy(source, target, self.semaphores.at[len(self.started)])
        copy.start()
        self.started.append(copy)
        return copy

    def wait(self):
        for copy in self.started:
            copy.wait()


def halves_of(refs, split):
    out = []
    for two in split:
        out.append([refs[0], refs[1]] if two else [refs[0].at[0], refs[0].at[1]])
        refs = refs[2 if two else 1 :]
    return out


def groups_kernel(groups, split, chained, *refs):
    count = len(groups)
    lent = count + sum(split)
    arrived = halves_of(refs[:lent], split)
    m12, wd, wg, wu = refs[lent : lent + 4]
    refs = refs[lent + 4 + (1 if chained else 0) :]
    gab, outs, refs = refs[0], halves_of(refs[1 : 1 + lent], split), refs[1 + lent :]
    m12_v, wd_v, wg_v, wu_v, cot_v, gab_v, rows_v, sem_in, sem_out = refs
    loads, stores, cot_loads, factor_loads = Copies(sem_in), Copies(sem_out), [], []
    load, store = loads.start, stores.start

    down_loads, weight_loads = [], []
    for n, group in enumerate(groups):
        cot_loads.append([load(arrived[n][e], cot_v.at[n, e]) for e in range(2)])
        if n == 0:
            down_loads = [load(wd.at[e], wd_v.at[e]) for e in range(2)]
        factor_loads.append(
            [load(m12.at[e, pl.ds(group * 4 * CAP, 4 * CAP)], m12_v.at[n, e]) for e in range(2)]
        )
        if n == 0:
            weight_loads = [[load(wg.at[e], wg_v.at[e]), load(wu.at[e], wu_v.at[e])] for e in range(2)]
    for n, group in enumerate(groups):
        place = pl.ds(group * 4 * CAP, 4 * CAP)
        for e in range(2):
            cot_loads[n][e].wait()
            if n == 0:
                down_loads[e].wait()
            grad_hidden = nt(cot_v[n, e], wd_v[e])
            factor_loads[n][e].wait()
            gab_v[n, e, :, :HID] = (grad_hidden * m12_v[n, e, :, :HID].astype(F32)).astype(BF)
            gab_v[n, e, :, HID:] = (grad_hidden * m12_v[n, e, :, HID:].astype(F32)).astype(BF)
            store(gab_v.at[n, e], gab.at[e, place])
        for e in range(2):
            if n == 0:
                for item in weight_loads[e]:
                    item.wait()
            rows_v[n, e] = (nt(gab_v[n, e, :, :HID], wg_v[e]) + nt(gab_v[n, e, :, HID:], wu_v[e])).astype(BF)
            store(rows_v.at[n, e], outs[n][e])
    stores.wait()


def groups_pass(groups, arrived, m12, wd, wg, wu, carried):
    chained = carried is not None
    count = len(groups)
    anywhere = pl.BlockSpec(memory_space=pl.ANY)
    slots = jax.ShapeDtypeStruct((2, 16 * CAP, D), BF)
    split = [isinstance(a, tuple) for a in arrived]
    lent = count + sum(split)
    args = [a for two, a in zip(split, arrived) for a in (a if two else (a,))]
    args += [m12, wd, wg, wu] + ([carried] if chained else [])
    row_shapes = []
    for two in split:
        shape = (4 * CAP, D) if two else (2, 4 * CAP, D)
        row_shapes += [jax.ShapeDtypeStruct(shape, BF)] * (2 if two else 1)
    out = pl.pallas_call(
        functools.partial(groups_kernel, groups, split, chained),
        in_specs=[anywhere] * len(args),
        out_specs=[anywhere] * (1 + lent),
        out_shape=[slots] + row_shapes,
        scratch_shapes=[
            pltpu.VMEM((count, 2, 4 * CAP, 2 * HID), BF),
            pltpu.VMEM((2, HID, D), BF),
            pltpu.VMEM((2, D, HID), BF),
            pltpu.VMEM((2, D, HID), BF),
            pltpu.VMEM((count, 2, 4 * CAP, D), BF),
            pltpu.VMEM((count, 2, 4 * CAP, 2 * HID), BF),
            pltpu.VMEM((count, 2, 4 * CAP, D), BF),
            pltpu.SemaphoreType.DMA((6 + 4 * count,)),
            pltpu.SemaphoreType.DMA((4 * count,)),
        ],
        input_output_aliases={lent + 4: 0} if chained else {},
        compiler_params=pltpu.CompilerParams(vmem_limit_bytes=VMEM_LIMIT),
        cost_estimate=pl.CostEstimate(
            flops=2_100_000_000 * count, bytes_accessed=6_000_000 + 9_000_000 * count, transcendentals=0
        ),
        name="groups_" + "".join(str(g) for g in groups),
    )(*args)
    return out[0], out[1:]


def combine_kernel(*refs):
    rows, hots, outs, (rows_v, hots_v, sem_rows, sem_hots) = refs[:5], refs[5:9], refs[9:13], refs[13:]
    rows = halves_of(rows, (False, False, False, True))
    loads = []
    for i in range(4):
        mine = []
        for k in range(4):
            mine.append(
                pltpu.make_async_copy(
                    hots[k].at[i], hots_v.at[i, pl.ds(k * 2 * CAP, 2 * CAP)], sem_hots.at[4 * i + k]
                )
            )
            for e in range(2):
                mine.append(
                    pltpu.make_async_copy(
                        rows[k][e].at[pl.ds(i * CAP, CAP)],
                        rows_v.at[i, pl.ds((2 * k + e) * CAP, CAP)],
                        sem_rows.at[8 * i + 2 * k + e],
                    )
                )
        for item in mine:
            item.start()
        loads.append(mine)
    for i in range(4):
        for item in loads[i]:
            item.wait()
        outs[i][...] = lax.dot_general(
            hots_v[i], rows_v[i], (((0,), (0,)), ((), ())), preferred_element_type=F32
        ).astype(BF)


def combine(rows, hots):
    anywhere = pl.BlockSpec(memory_space=pl.ANY)
    return pl.pallas_call(
        combine_kernel,
        in_specs=[anywhere] * 9,
        out_specs=[pl.BlockSpec(memory_space=pltpu.VMEM)] * 4,
        out_shape=[jax.ShapeDtypeStruct((TOK, D), BF)] * 4,
        scratch_shapes=[
            pltpu.VMEM((4, 8 * CAP, D), BF),
            pltpu.VMEM((4, 8 * CAP, TOK), BF),
            pltpu.SemaphoreType.DMA((32,)),
            pltpu.SemaphoreType.DMA((16,)),
        ],
        compiler_params=pltpu.CompilerParams(vmem_limit_bytes=VMEM_LIMIT),
        cost_estimate=pl.CostEstimate(flops=1_400_000_000, bytes_accessed=9_000_000, transcendentals=0),
        name="combine",
    )(*rows, *hots)


def compress(local_grad, residual):
    carried = local_grad * loss_unscale + residual.astype(F32)
    magnitude = jnp.mean(jnp.abs(carried), axis=-1, keepdims=True) + epsilon
    compressed = (magnitude * jnp.tanh(carried * (1.0 / magnitude))).astype(BF)
    return compressed, (carried - compressed.astype(F32)).astype(BF)


def gate_up_kernel(here, xt, gab, res_gate, res_up, keep, give_gate, give_up, left_gate, left_up, *scratch):
    xt_v, gab_v, res_v, left_v, keep_v, give_v, held, sem_in, sem_out = scratch
    x, core, _, _ = place_of(here)
    loads, stores, waits = Copies(sem_in), Copies(sem_out), {}
    half = D // 2
    for e in range(2):
        waits[e, 0] = [
            loads.start(xt.at[e, pl.ds(0, half)], xt_v.at[e, pl.ds(0, half)]),
            loads.start(gab.at[e], gab_v.at[e]),
            loads.start(res_gate.at[e], res_v.at[e, 0]),
            loads.start(res_up.at[e], res_v.at[e, 1]),
        ]
        waits[e, 2] = [loads.start(xt.at[e, pl.ds(half, half)], xt_v.at[e, pl.ds(half, half)])]
    for e in range(2):
        for t in range(SIDE):
            for item in waits.get((e, t), ()):
                item.wait()
            rows = pl.ds(t * 256, 256)
            grads = jnp.dot(xt_v[e, rows], gab_v[e], preferred_element_type=F32)
            kept_at, given_at = block_place(t, x, core), block_place(t, x, 1 - core)
            for m, left in enumerate((left_gate, left_up)):
                held[m], left_v[e, m, rows] = compress(grads[:, m * HID : (m + 1) * HID], res_v[e, m, rows])
                keep_v[kept_at, m, e] = held[m, pl.ds(pl.multiple_of(core * 128, 128), 128)]
                give_v[given_at, m, e] = held[m, pl.ds(pl.multiple_of((1 - core) * 128, 128), 128)]
                stores.start(left_v.at[e, m, rows], left.at[e, rows])
        for m, give in enumerate((give_gate, give_up)):
            stores.start(give_v.at[:, m, e], give.at[:, e])
        stores.start(keep_v.at[:, :, e], keep.at[:, :, e])
    stores.wait()


def gate_up_grads(here, xt, gab, res_gate, res_up):
    anywhere = pl.BlockSpec(memory_space=pl.ANY)
    res_shape = jax.ShapeDtypeStruct((2, D, HID), BF)
    give_shape = jax.ShapeDtypeStruct((SIDE, 2, 128, HID), BF)
    return pl.pallas_call(
        gate_up_kernel,
        in_specs=[pl.BlockSpec(memory_space=pltpu.SMEM)] + [anywhere] * 4,
        out_specs=[anywhere] * 5,
        out_shape=[
            jax.ShapeDtypeStruct((SIDE, 2, 2, 128, HID), BF), give_shape, give_shape, res_shape, res_shape
        ],
        scratch_shapes=[
            pltpu.VMEM((2, D, 16 * CAP), BF),
            pltpu.VMEM((2, 16 * CAP, 2 * HID), BF),
            pltpu.VMEM((2, 2, D, HID), BF),
            pltpu.VMEM((2, 2, D, HID), BF),
            pltpu.VMEM((SIDE, 2, 2, 128, HID), BF),
            pltpu.VMEM((SIDE, 2, 2, 128, HID), BF),
            pltpu.VMEM((2, 256, HID), BF),
            pltpu.SemaphoreType.DMA((10,)),
            pltpu.SemaphoreType.DMA((22,)),
        ],
        compiler_params=pltpu.CompilerParams(vmem_limit_bytes=VMEM_LIMIT),
        cost_estimate=pl.CostEstimate(flops=5_400_000_000, bytes_accessed=22_000_000, transcendentals=2_000_000),
        name="gate_up_grads",
    )(here, xt, gab, res_gate, res_up)


def down_kernel(split, here, ht, res, *refs):
    lent = 4 + sum(split)
    arrived, (keep, give, left) = halves_of(refs[:lent], split), refs[lent : lent + 3]
    ht_v, cot_v, res_v, left_v, sent_v, sem_in, sem_out = refs[lent + 3 :]
    x, core, _, _ = place_of(here)
    loads, stores, waits = Copies(sem_in), Copies(sem_out), {}
    for e in range(2):
        waits[e] = [loads.start(ht.at[e], ht_v.at[e])]
        waits[e] += [
            loads.start(arrived[g][e], cot_v.at[e, pl.ds(g * 4 * CAP, 4 * CAP)]) for g in range(4)
        ]
        waits[e] += [loads.start(res.at[e], res_v.at[e])]
    for e in range(2):
        for item in waits[e]:
            item.wait()
        for t in range(2):
            rows = pl.ds(t * 256, 256)
            grads = jnp.dot(ht_v[e, rows], cot_v[e], preferred_element_type=F32)
            compressed, left_v[e, rows] = compress(grads, res_v[e, rows])
            stores.start(left_v.at[e, rows], left.at[e, rows])
            for owner in range(SIDE):
                for c in range(2):
                    at = 2 * owner + c
                    sent_v[core ^ c, block_place(owner, x, c), e, rows] = compressed[:, at * 128 : (at + 1) * 128]
        stores.start(sent_v.at[0, :, e], keep.at[:, e])
        stores.start(sent_v.at[1, :, e], give.at[:, e])
    stores.wait()


def down_grads(here, ht, arrived, res):
    anywhere = pl.BlockSpec(memory_space=pl.ANY)
    blocks = jax.ShapeDtypeStruct((SIDE, 2, HID, 128), BF)
    split = [isinstance(a, tuple) for a in arrived]
    pieces = [a for two, one in zip(split, arrived) for a in (one if two else (one,))]
    return pl.pallas_call(
        functools.partial(down_kernel, split),
        in_specs=[pl.BlockSpec(memory_space=pltpu.SMEM)] + [anywhere] * (2 + len(pieces)),
        out_specs=[anywhere] * 3,
        out_shape=[blocks, blocks, jax.ShapeDtypeStruct((2, HID, D), BF)],
        scratch_shapes=[
            pltpu.VMEM((2, HID, 16 * CAP), BF),
            pltpu.VMEM((2, 16 * CAP, D), BF),
            pltpu.VMEM((2, HID, D), BF),
            pltpu.VMEM((2, HID, D), BF),
            pltpu.VMEM((2, SIDE, 2, HID, 128), BF),
            pltpu.SemaphoreType.DMA((12,)),
            pltpu.SemaphoreType.DMA((8,)),
        ],
        compiler_params=pltpu.CompilerParams(vmem_limit_bytes=VMEM_LIMIT),
        cost_estimate=pl.CostEstimate(flops=2_700_000_000, bytes_accessed=14_000_000, transcendentals=1_000_000),
        name="down_grads",
    )(here, ht, res, *pieces)


def total(*terms):
    out = terms[0].astype(F32)
    for term in terms[1:]:
        out = out + term.astype(F32)
    return out


def add(*terms):
    return total(*terms).astype(BF)


def partner(stage, x, core):
    return x ^ (1 if stage == core else 3)


def halve(keep, got, passed, beside):
    first = dp_hop(passed, lambda x, c: (partner(0, x, c), c))
    first, _ = lax.optimization_barrier((first, beside))
    second = dp_hop(add(keep[1], got[1], first[1]), lambda x, c: (partner(1, x, c), c))
    return first, second


def on_device(x_saved, d_out, routes, probs, w_gate, w_up, w_down, res_gate, res_up, res_down):
    here = jnp.stack([lax.axis_index("dp"), lax.axis_index("expert")]).astype(jnp.int32)

    own = pack(d_out, routes, probs)
    near = (hop(own, 0, 1), hop(own, 0, -1), hop(own, 0, 2))
    terms = forward_terms(0, here, x_saved[0], w_gate, w_up, None)
    near, terms = lax.optimization_barrier((near, terms))
    layout = (((2, 0), (2, 1)), ((1, 0), (1, 1)), ((3, 0),), ((3, 1),))
    (to_plus, to_minus, far_plus, far_minus), (hot1, hot2, hot3) = dispatch((1, 2, 3), layout, here, (own, *near))
    far_plus, far_minus = hop(far_plus[0], 1, 1), hop(far_minus[0], 1, -1)
    group1, group2 = hop(to_plus, 1, 1), hop(to_minus, 1, -1)
    (group0,), (hot0,) = dispatch((0,), (((0, 0), (0, 1)),), here, (own, *near))
    xt, ht, m12 = forward_terms(1, here, x_saved[0], w_gate, w_up, terms)

    run = functools.partial(groups_pass, m12=m12, wd=w_down, wg=w_gate, wu=w_up)
    gab, (rows0,) = run((0,), [group0], carried=None)
    far_plus, far_minus, gab = lax.optimization_barrier((far_plus, far_minus, gab))
    group3 = (hop(far_plus, 1, 1), hop(far_minus, 1, -1))
    gab, (rows1, rows2) = run((1, 2), [group1, group2], carried=gab)
    near_rows = (hop(rows2, 1, 1), hop(rows1, 1, -1))
    gab, (rows3a, rows3b) = run((3,), [group3], carried=gab)
    half_way = (hop(rows3a, 1, 1), hop(rows3b, 1, -1))

    keep, give_gate, give_up, left_gate, left_up = gate_up_grads(here, xt, gab, res_gate[0], res_up[0])
    near_rows, half_way, give_gate, give_up = lax.optimization_barrier((near_rows, half_way, give_gate, give_up))
    got_gate, got_up = (dp_hop(g, lambda x, c: (x, 1 - c)) for g in (give_gate, give_up))
    far_rows = (hop(half_way[0], 1, 1), hop(half_way[1], 1, -1))
    keep_down, give_down, left_down = down_grads(here, ht, (group0, group1, group2, group3), res_down[0])
    far_rows, got_gate, got_up, give_down = lax.optimization_barrier((far_rows, got_gate, got_up, give_down))
    got_down = dp_hop(give_down, lambda x, c: (x, 1 - c))
    got = jnp.stack([got_gate, got_up], axis=1)
    passed, passed_down = add(keep[2:], got[2:]), add(keep_down[2:], got_down[2:])

    far_rows, passed, passed_down = lax.optimization_barrier((far_rows, passed, passed_down))
    mine, before, behind, across = combine((rows0, *near_rows, *far_rows), (hot0, hot1, hot2, hot3))
    terms = (mine, hop(behind, 0, 1), hop(before, 0, -1), hop(across, 0, 2))
    first_in, second_in = halve(keep, got, passed, mine)
    first_down, second_down = halve(keep_down, got_down, passed_down, mine)
    d_tokens, second_in, second_down = lax.optimization_barrier((add(*terms), second_in, second_down))
    mean = total(keep[0], got[0], first_in[0], second_in) / 8.0
    mean_down = total(keep_down[0], got_down[0], first_down[0], second_down) / 8.0
    return (d_tokens, mean[0], mean[1], mean_down, left_gate[None], left_up[None], left_down[None])


def solution(mesh):
    in_specs = (
        P("dp", "expert", None, None),
        P(("dp", "expert"), None),
        P(("dp", "expert"), None),
        P(("dp", "expert"), None),
        P("expert", None, None),
        P("expert", None, None),
        P("expert", None, None),
        P("dp", "expert", None, None),
        P("dp", "expert", None, None),
        P("dp", "expert", None, None),
    )
    out_specs = (
        P(("dp", "expert"), None),
        P("expert", "dp", None),
        P("expert", "dp", None),
        P("expert", None, "dp"),
        P("dp", "expert", None, None),
        P("dp", "expert", None, None),
        P("dp", "expert", None, None),
    )
    return jax.shard_map(
        on_device, mesh=mesh, in_specs=in_specs, out_specs=out_specs, check_vma=False
    )
```

```python
import functools

import jax
import jax.numpy as jnp
from jax import lax
from jax.experimental import pallas as pl
from jax.experimental.pallas import tpu as pltpu
from jax.sharding import PartitionSpec as P

loss_unscale = 0.0625
epsilon = 1e-05

SIDE = 4
OFFSETS = (0, -1, 1, 2)
CAP = 80
TOK = 256
PACK = TOK + 16
D = 1024
HID = 512
BF = jnp.bfloat16
F32 = jnp.float32
VMEM_LIMIT = 61 * 2**20


def place_of(here):
    core = here[0] & 1
    z, y = here[1] // SIDE, here[1] & (SIDE - 1)
    return here[0] // 2, core, jnp.where(core == 0, z, y), jnp.where(core == 0, y, z)


def expert_at(here, first_off, second_off):
    _, core, first, second = place_of(here)
    first, second = (first + first_off + SIDE) & (SIDE - 1), (second + second_off + SIDE) & (SIDE - 1)
    return jnp.where(core == 0, first * SIDE + second, second * SIDE + first)


def block_place(owner, x, core):
    apart = owner ^ x
    return jnp.where(apart == 0, 0, jnp.where(apart == 1, 2 - core, jnp.where(apart == 2, 3, 1 + core)))


def pairs(axis, step):
    out = []
    for dp in range(8):
        core = dp % 2
        for z in range(SIDE):
            for y in range(SIDE):
                along_z = (axis == 0) == (core == 0)
                z2, y2 = ((z + step) % SIDE, y) if along_z else (z, (y + step) % SIDE)
                out.append((dp * 16 + z * SIDE + y, dp * 16 + z2 * SIDE + y2))
    return out


def hop(value, axis, step):
    return lax.ppermute(value, ("dp", "expert"), pairs(axis, step))


def dp_hop(value, move):
    return lax.ppermute(
        value, "dp", [(x * 2 + c, move(x, c)[0] % SIDE * 2 + move(x, c)[1]) for x in range(SIDE) for c in range(2)]
    )


def nt(left, right):
    return lax.dot_general(left, right, (((1,), (1,)), ((), ())), preferred_element_type=F32)


def pack_kernel(tokens, routes, probs, out):
    out[:TOK, :] = tokens[...]
    weights = probs[...]
    high = weights.astype(BF)
    left = weights - high.astype(F32)
    middle = left.astype(BF)
    low = (left - middle.astype(F32)).astype(BF)
    out[TOK : TOK + 8, :] = jnp.concatenate(
        [routes[...].astype(F32).astype(BF), high, middle, low], axis=1
    )
    out[TOK + 8 :, :] = jnp.zeros((8, D), BF)


def pack(tokens, routes, probs):
    return pl.pallas_call(
        pack_kernel,
        out_shape=jax.ShapeDtypeStruct((PACK, D), BF),
        cost_estimate=pl.CostEstimate(flops=0, bytes_accessed=1_100_000, transcendentals=0),
        name="pack",
    )(tokens, routes.T, probs.T)


def forward_kernel(chained, here, *refs):
    xs, (wg, wu), refs = refs[:8], refs[8:10], refs[10 + (3 if chained else 0) :]
    xt, ht, m12, rows = refs
    for i in range(8):
        rows[i * CAP : (i + 1) * CAP, :] = xs[i][0, 0]
    half = 4 * CAP
    pre = []
    for h in range(2):
        saved = rows[h * half : (h + 1) * half, :]
        pre.append(
            (
                jnp.dot(saved, wg[0], preferred_element_type=F32),
                jnp.dot(saved, wu[0], preferred_element_type=F32),
            )
        )
    xt[0] = rows[...].T
    hidden = []
    for h, (gate, up) in enumerate(pre):
        logistic = jax.nn.sigmoid(gate)
        act = gate * logistic
        m12[0, h * half : (h + 1) * half, :HID] = (up * (logistic * (1.0 + gate * (1.0 - logistic)))).astype(BF)
        m12[0, h * half : (h + 1) * half, HID:] = act.astype(BF)
        hidden.append((act * up).astype(BF))
    ht[0] = jnp.concatenate(hidden, axis=0).T


def forward_terms(e, here, x, wg, wu, carried):
    blocks = x.reshape(2, 16, CAP, D)
    chained = carried is not None

    def block_at(i):
        def at(h, here):
            return e, expert_at(here, OFFSETS[i % 4], h if i < 4 else 3 * h - 1), 0, 0

        return pl.BlockSpec((1, 1, CAP, D), at)

    half = 8 * CAP
    return pl.pallas_call(
        functools.partial(forward_kernel, chained),
        grid_spec=pltpu.PrefetchScalarGridSpec(
            num_scalar_prefetch=1,
            grid=(2,),
            in_specs=[block_at(i) for i in range(8)]
            + [pl.BlockSpec((1, D, HID), lambda h, p: (e, 0, 0))] * 2
            + [pl.BlockSpec(memory_space=pl.ANY)] * (3 if chained else 0),
            out_specs=[
                pl.BlockSpec((1, D, half), lambda h, p: (e, 0, h)),
                pl.BlockSpec((1, HID, half), lambda h, p: (e, 0, h)),
                pl.BlockSpec((1, half, 2 * HID), lambda h, p: (e, h, 0)),
            ],
            scratch_shapes=[pltpu.VMEM((half, D), BF)],
        ),
        out_shape=[
            jax.ShapeDtypeStruct((2, D, 16 * CAP), BF),
            jax.ShapeDtypeStruct((2, HID, 16 * CAP), BF),
            jax.ShapeDtypeStruct((2, 16 * CAP, 2 * HID), BF),
        ],
        input_output_aliases={11 + i: i for i in range(3)} if chained else {},
        compiler_params=pltpu.CompilerParams(vmem_limit_bytes=VMEM_LIMIT),
        cost_estimate=pl.CostEstimate(flops=2_700_000_000, bytes_accessed=15_000_000, transcendentals=655_360),
        name="forward_terms",
    )(here, *([blocks] * 8), wg, wu, *(carried or ()))


def dispatch_kernel(targets, layout, here, *refs):
    blocks, outs, hots = refs[:4], refs[4 : 4 + len(layout)], refs[4 + len(layout) :]
    before = (
        lax.broadcasted_iota(jnp.int32, (TOK, TOK), 0) < lax.broadcasted_iota(jnp.int32, (TOK, TOK), 1)
    ).astype(BF)
    slot = lax.broadcasted_iota(jnp.int32, (CAP, TOK), 0).astype(F32)
    names = [(2 * expert_at(here, 0, OFFSETS[t]) + e).astype(F32) for t in targets for e in range(2)]
    named, weights = [], []
    for i in range(4):
        meta = blocks[i][TOK:, :].astype(F32)[:8]
        routes = meta[:, :TOK]
        probs = meta[:, TOK : 2 * TOK] + meta[:, 2 * TOK : 3 * TOK] + meta[:, 3 * TOK :]
        for name in names:
            hit = routes == name
            named.append(jnp.sum(jnp.where(hit, 1.0, 0.0), axis=0, keepdims=True))
            weights.append(jnp.sum(jnp.where(hit, probs, 0.0), axis=0, keepdims=True))
    mask = jnp.concatenate(named, axis=0)
    rank = jnp.dot(mask.astype(BF), before, preferred_element_type=F32)
    key = jnp.where(mask > 0.5, rank, -1.0)
    per = len(names)
    for i in range(4):
        halves, scales = [], []
        for k in range(per):
            hit = slot == key[per * i + k : per * i + k + 1, :]
            halves.append(jnp.where(hit, 1.0, 0.0).astype(BF))
            scales.append(jnp.sum(jnp.where(hit, weights[per * i + k], 0.0), axis=1, keepdims=True))
            hots[k // 2][i, k % 2 * CAP : (k % 2 + 1) * CAP, :] = halves[k]
        chosen = jnp.concatenate(halves, axis=0)
        taken = jnp.dot(chosen, blocks[i][:TOK, :], preferred_element_type=F32)
        scaled = (taken * jnp.concatenate(scales, axis=0)).astype(BF)
        for out, held in zip(outs, layout):
            for n, (target, e) in enumerate(held):
                k = 2 * targets.index(target) + e
                out[n, i * CAP : (i + 1) * CAP, :] = scaled[k * CAP : (k + 1) * CAP]


def dispatch(targets, layout, here, blocks):
    whole = pl.BlockSpec(memory_space=pltpu.VMEM)
    out = pl.pallas_call(
        functools.partial(dispatch_kernel, targets, layout),
        in_specs=[pl.BlockSpec(memory_space=pltpu.SMEM)] + [whole] * 4,
        out_specs=[whole] * (len(layout) + len(targets)),
        out_shape=[jax.ShapeDtypeStruct((len(held), 4 * CAP, D), BF) for held in layout]
        + [jax.ShapeDtypeStruct((4, 2 * CAP, TOK), BF)] * len(targets),
        compiler_params=pltpu.CompilerParams(vmem_limit_bytes=VMEM_LIMIT),
        cost_estimate=pl.CostEstimate(
            flops=400_000_000 * len(targets), bytes_accessed=6_000_000, transcendentals=0
        ),
        name="dispatch_" + "".join(str(t) for t in targets),
    )(here, *blocks)
    return out[: len(layout)], out[len(layout) :]


class Copies:
    def __init__(self, semaphores):
        self.semaphores, self.started = semaphores, []

    def start(self, source, target):
        copy = pltpu.make_async_copy(source, target, self.semaphores.at[len(self.started)])
        copy.start()
        self.started.append(copy)
        return copy

    def wait(self):
        for copy in self.started:
            copy.wait()


def halves_of(refs, split):
    out = []
    for two in split:
        out.append([refs[0], refs[1]] if two else [refs[0].at[0], refs[0].at[1]])
        refs = refs[2 if two else 1 :]
    return out


def groups_kernel(groups, split, chained, *refs):
    count = len(groups)
    lent = count + sum(split)
    arrived = halves_of(refs[:lent], split)
    m12, wd, wg, wu = refs[lent : lent + 4]
    refs = refs[lent + 4 + (1 if chained else 0) :]
    gab, outs, refs = refs[0], halves_of(refs[1 : 1 + lent], split), refs[1 + lent :]
    m12_v, wd_v, wg_v, wu_v, cot_v, gab_v, rows_v, sem_in, sem_out = refs
    loads, stores, cot_loads, factor_loads = Copies(sem_in), Copies(sem_out), [], []
    load, store = loads.start, stores.start

    down_loads, weight_loads = [], []
    for n, group in enumerate(groups):
        cot_loads.append([load(arrived[n][e], cot_v.at[n, e]) for e in range(2)])
        if n == 0:
            down_loads = [load(wd.at[e], wd_v.at[e]) for e in range(2)]
        factor_loads.append(
            [load(m12.at[e, pl.ds(group * 4 * CAP, 4 * CAP)], m12_v.at[n, e]) for e in range(2)]
        )
        if n == 0:
            weight_loads = [[load(wg.at[e], wg_v.at[e]), load(wu.at[e], wu_v.at[e])] for e in range(2)]
    for n, group in enumerate(groups):
        place = pl.ds(group * 4 * CAP, 4 * CAP)
        for e in range(2):
            cot_loads[n][e].wait()
            if n == 0:
                down_loads[e].wait()
            grad_hidden = nt(cot_v[n, e], wd_v[e])
            factor_loads[n][e].wait()
            gab_v[n, e, :, :HID] = (grad_hidden * m12_v[n, e, :, :HID].astype(F32)).astype(BF)
            gab_v[n, e, :, HID:] = (grad_hidden * m12_v[n, e, :, HID:].astype(F32)).astype(BF)
            store(gab_v.at[n, e], gab.at[e, place])
        for e in range(2):
            if n == 0:
                for item in weight_loads[e]:
                    item.wait()
            rows_v[n, e] = (nt(gab_v[n, e, :, :HID], wg_v[e]) + nt(gab_v[n, e, :, HID:], wu_v[e])).astype(BF)
            store(rows_v.at[n, e], outs[n][e])
    stores.wait()


def groups_pass(groups, arrived, m12, wd, wg, wu, carried):
    chained = carried is not None
    count = len(groups)
    anywhere = pl.BlockSpec(memory_space=pl.ANY)
    slots = jax.ShapeDtypeStruct((2, 16 * CAP, D), BF)
    split = [isinstance(a, tuple) for a in arrived]
    lent = count + sum(split)
    args = [a for two, a in zip(split, arrived) for a in (a if two else (a,))]
    args += [m12, wd, wg, wu] + ([carried] if chained else [])
    row_shapes = []
    for two in split:
        shape = (4 * CAP, D) if two else (2, 4 * CAP, D)
        row_shapes += [jax.ShapeDtypeStruct(shape, BF)] * (2 if two else 1)
    out = pl.pallas_call(
        functools.partial(groups_kernel, groups, split, chained),
        in_specs=[anywhere] * len(args),
        out_specs=[anywhere] * (1 + lent),
        out_shape=[slots] + row_shapes,
        scratch_shapes=[
            pltpu.VMEM((count, 2, 4 * CAP, 2 * HID), BF),
            pltpu.VMEM((2, HID, D), BF),
            pltpu.VMEM((2, D, HID), BF),
            pltpu.VMEM((2, D, HID), BF),
            pltpu.VMEM((count, 2, 4 * CAP, D), BF),
            pltpu.VMEM((count, 2, 4 * CAP, 2 * HID), BF),
            pltpu.VMEM((count, 2, 4 * CAP, D), BF),
            pltpu.SemaphoreType.DMA((6 + 4 * count,)),
            pltpu.SemaphoreType.DMA((4 * count,)),
        ],
        input_output_aliases={lent + 4: 0} if chained else {},
        compiler_params=pltpu.CompilerParams(vmem_limit_bytes=VMEM_LIMIT),
        cost_estimate=pl.CostEstimate(
            flops=2_100_000_000 * count, bytes_accessed=6_000_000 + 9_000_000 * count, transcendentals=0
        ),
        name="groups_" + "".join(str(g) for g in groups),
    )(*args)
    return out[0], out[1:]


def combine_kernel(*refs):
    rows, hots, outs, (rows_v, hots_v, sem_rows, sem_hots) = refs[:5], refs[5:9], refs[9:13], refs[13:]
    rows = halves_of(rows, (False, False, False, True))
    loads = []
    for i in range(4):
        mine = []
        for k in range(4):
            mine.append(
                pltpu.make_async_copy(
                    hots[k].at[i], hots_v.at[i, pl.ds(k * 2 * CAP, 2 * CAP)], sem_hots.at[4 * i + k]
                )
            )
            for e in range(2):
                mine.append(
                    pltpu.make_async_copy(
                        rows[k][e].at[pl.ds(i * CAP, CAP)],
                        rows_v.at[i, pl.ds((2 * k + e) * CAP, CAP)],
                        sem_rows.at[8 * i + 2 * k + e],
                    )
                )
        for item in mine:
            item.start()
        loads.append(mine)
    for i in range(4):
        for item in loads[i]:
            item.wait()
        outs[i][...] = lax.dot_general(
            hots_v[i], rows_v[i], (((0,), (0,)), ((), ())), preferred_element_type=F32
        ).astype(BF)


def combine(rows, hots):
    anywhere = pl.BlockSpec(memory_space=pl.ANY)
    return pl.pallas_call(
        combine_kernel,
        in_specs=[anywhere] * 9,
        out_specs=[pl.BlockSpec(memory_space=pltpu.VMEM)] * 4,
        out_shape=[jax.ShapeDtypeStruct((TOK, D), BF)] * 4,
        scratch_shapes=[
            pltpu.VMEM((4, 8 * CAP, D), BF),
            pltpu.VMEM((4, 8 * CAP, TOK), BF),
            pltpu.SemaphoreType.DMA((32,)),
            pltpu.SemaphoreType.DMA((16,)),
        ],
        compiler_params=pltpu.CompilerParams(vmem_limit_bytes=VMEM_LIMIT),
        cost_estimate=pl.CostEstimate(flops=1_400_000_000, bytes_accessed=9_000_000, transcendentals=0),
        name="combine",
    )(*rows, *hots)


def compress(local_grad, residual):
    carried = local_grad * loss_unscale + residual.astype(F32)
    magnitude = jnp.mean(jnp.abs(carried), axis=-1, keepdims=True) + epsilon
    compressed = (magnitude * jnp.tanh(carried * (1.0 / magnitude))).astype(BF)
    return compressed, (carried - compressed.astype(F32)).astype(BF)


def gate_up_kernel(here, xt, gab, res_gate, res_up, keep, give_gate, give_up, left_gate, left_up, held):
    x, core, _, _ = place_of(here)
    half = pl.program_id(1)
    grads = [jnp.dot(xt[0, u * 256 : (u + 1) * 256], gab[0], preferred_element_type=F32) for u in range(2)]
    for u in range(2):
        rows = slice(u * 256, (u + 1) * 256)
        kept_at = block_place(2 * half + u, x, core)
        given_at = block_place(2 * half + u, x, 1 - core)
        for m, (res, left) in enumerate(((res_gate, left_gate), (res_up, left_up))):
            held[u, m], left[0, rows] = compress(grads[u][:, m * HID : (m + 1) * HID], res[0, rows])
            keep[m, kept_at, 0] = held[u, m, pl.ds(pl.multiple_of(core * 128, 128), 128)]
            give = (give_gate, give_up)[m]
            give[given_at, 0] = held[u, m, pl.ds(pl.multiple_of((1 - core) * 128, 128), 128)]


def gate_up_grads(here, xt, gab, res_gate, res_up):
    tile = pl.BlockSpec((1, HID, HID), lambda e, t, s: (e, t, 0))
    res_shape = jax.ShapeDtypeStruct((2, D, HID), BF)
    keep_shape = jax.ShapeDtypeStruct((2, SIDE, 2, 128, HID), BF)
    give_shape = jax.ShapeDtypeStruct((SIDE, 2, 128, HID), BF)
    return pl.pallas_call(
        gate_up_kernel,
        grid_spec=pltpu.PrefetchScalarGridSpec(
            num_scalar_prefetch=1,
            grid=(2, 2),
            in_specs=[
                pl.BlockSpec((1, 512, 16 * CAP), lambda e, t, s: (e, t, 0)),
                pl.BlockSpec((1, 16 * CAP, 2 * HID), lambda e, t, s: (e, 0, 0)),
                tile,
                tile,
            ],
            out_specs=[pl.BlockSpec((2, SIDE, 1, 128, HID), lambda e, t, s: (0, 0, e, 0, 0))]
            + [pl.BlockSpec((SIDE, 1, 128, HID), lambda e, t, s: (0, e, 0, 0))] * 2
            + [tile, tile],
            scratch_shapes=[pltpu.VMEM((2, 2, 256, HID), BF)],
        ),
        out_shape=[keep_shape, give_shape, give_shape, res_shape, res_shape],
        compiler_params=pltpu.CompilerParams(vmem_limit_bytes=VMEM_LIMIT),
        cost_estimate=pl.CostEstimate(flops=5_400_000_000, bytes_accessed=22_000_000, transcendentals=2_000_000),
        name="gate_up_grads",
    )(here, xt, gab, res_gate, res_up)


def down_kernel(e, chained, here, ht, res, *refs):
    arrived, refs = refs[:4], refs[4 + (3 if chained else 0) :]
    keep, give, left, ht_v, cot_v, res_v, left_v, sent_v, sem_in, sem_out = refs
    x, core, _, _ = place_of(here)
    loads, stores = Copies(sem_in), Copies(sem_out)
    loads.start(ht.at[e], ht_v)
    for g in range(4):
        source = arrived[g] if len(arrived[g].shape) == 2 else arrived[g].at[e]
        loads.start(source, cot_v.at[pl.ds(g * 4 * CAP, 4 * CAP)])
    loads.start(res.at[e], res_v)
    loads.wait()
    for t in range(2):
        rows = pl.ds(t * 256, 256)
        grads = jnp.dot(ht_v[rows], cot_v[...], preferred_element_type=F32)
        compressed, left_v[rows] = compress(grads, res_v[rows])
        stores.start(left_v.at[rows], left.at[e, rows])
        for owner in range(SIDE):
            for c in range(2):
                at = 2 * owner + c
                sent_v[core ^ c, block_place(owner, x, c), rows] = compressed[:, at * 128 : (at + 1) * 128]
    stores.start(sent_v.at[0], keep.at[:, e])
    stores.start(sent_v.at[1], give.at[:, e])
    stores.wait()


def down_grads(e, here, ht, arrived, res, carried):
    anywhere = pl.BlockSpec(memory_space=pl.ANY)
    blocks = jax.ShapeDtypeStruct((SIDE, 2, HID, 128), BF)
    chained = carried is not None
    pieces = [a[e] if isinstance(a, tuple) else a for a in arrived] + (list(carried) if chained else [])
    return pl.pallas_call(
        functools.partial(down_kernel, e, chained),
        in_specs=[pl.BlockSpec(memory_space=pltpu.SMEM)] + [anywhere] * (2 + len(pieces)),
        out_specs=[anywhere] * 3,
        out_shape=[blocks, blocks, jax.ShapeDtypeStruct((2, HID, D), BF)],
        scratch_shapes=[
            pltpu.VMEM((HID, 16 * CAP), BF),
            pltpu.VMEM((16 * CAP, D), BF),
            pltpu.VMEM((HID, D), BF),
            pltpu.VMEM((HID, D), BF),
            pltpu.VMEM((2, SIDE, HID, 128), BF),
            pltpu.SemaphoreType.DMA((6,)),
            pltpu.SemaphoreType.DMA((4,)),
        ],
        input_output_aliases={7 + i: i for i in range(3)} if chained else {},
        compiler_params=pltpu.CompilerParams(vmem_limit_bytes=VMEM_LIMIT),
        cost_estimate=pl.CostEstimate(flops=1_400_000_000, bytes_accessed=7_000_000, transcendentals=500_000),
        name="down_grads",
    )(here, ht, res, *pieces)


def total(*terms):
    out = terms[0].astype(F32)
    for term in terms[1:]:
        out = out + term.astype(F32)
    return out


def add(*terms):
    return total(*terms).astype(BF)


def partner(stage, x, core):
    return x ^ (1 if stage == core else 3)


def halve(passed, nearer, beside):
    first = dp_hop(passed, lambda x, c: (partner(0, x, c), c))
    first, _ = lax.optimization_barrier((first, beside))
    return first, dp_hop(add(*nearer(first)), lambda x, c: (partner(1, x, c), c))


def on_device(x_saved, d_out, routes, probs, w_gate, w_up, w_down, res_gate, res_up, res_down):
    here = jnp.stack([lax.axis_index("dp"), lax.axis_index("expert")]).astype(jnp.int32)

    own = pack(d_out, routes, probs)
    near = (hop(own, 0, 1), hop(own, 0, -1), hop(own, 0, 2))
    terms = forward_terms(0, here, x_saved[0], w_gate, w_up, None)
    near, terms = lax.optimization_barrier((near, terms))
    layout = (((2, 0), (2, 1)), ((1, 0), (1, 1)), ((3, 0),), ((3, 1),))
    (to_plus, to_minus, far_plus, far_minus), (hot1, hot2, hot3) = dispatch((1, 2, 3), layout, here, (own, *near))
    far_plus, far_minus = hop(far_plus[0], 1, 1), hop(far_minus[0], 1, -1)
    group1, group2 = hop(to_plus, 1, 1), hop(to_minus, 1, -1)
    (group0,), (hot0,) = dispatch((0,), (((0, 0), (0, 1)),), here, (own, *near))
    xt, ht, m12 = forward_terms(1, here, x_saved[0], w_gate, w_up, terms)

    run = functools.partial(groups_pass, m12=m12, wd=w_down, wg=w_gate, wu=w_up)
    gab, (rows0,) = run((0,), [group0], carried=None)
    far_plus, far_minus, gab = lax.optimization_barrier((far_plus, far_minus, gab))
    group3 = (hop(far_plus, 1, 1), hop(far_minus, 1, -1))
    gab, (rows1, rows2) = run((1, 2), [group1, group2], carried=gab)
    near_rows = (hop(rows2, 1, 1), hop(rows1, 1, -1))
    gab, (rows3a, rows3b) = run((3,), [group3], carried=gab)
    half_way = (hop(rows3a, 1, 1), hop(rows3b, 1, -1))

    keep, give_gate, give_up, left_gate, left_up = gate_up_grads(here, xt, gab, res_gate[0], res_up[0])
    near_rows, half_way, give_gate, give_up = lax.optimization_barrier((near_rows, half_way, give_gate, give_up))
    got_gate, got_up = (dp_hop(g, lambda x, c: (x, 1 - c)) for g in (give_gate, give_up))
    far_rows = (hop(half_way[0], 1, 1), hop(half_way[1], 1, -1))
    down = functools.partial(
        down_grads, here=here, ht=ht, arrived=(group0, group1, group2, group3), res=res_down[0]
    )
    carried = down(0, carried=None)
    got_gate, got_up, carried = lax.optimization_barrier((got_gate, got_up, carried))
    got = jnp.stack([got_gate, got_up])
    passed = add(keep[:, 2:], got[:, 2:])
    keep_down, give_down, left_down = down(1, carried=carried)
    far_rows, give_down = lax.optimization_barrier((far_rows, give_down))
    got_down = dp_hop(give_down, lambda x, c: (x, 1 - c))
    passed_down = add(keep_down[2:], got_down[2:])

    far_rows, passed_down = lax.optimization_barrier((far_rows, passed_down))
    mine, before, behind, across = combine((rows0, *near_rows, *far_rows), (hot0, hot1, hot2, hot3))
    terms = (mine, hop(behind, 0, 1), hop(before, 0, -1), hop(across, 0, 2))
    first_in, second_in = halve(passed, lambda first: (keep[:, 1], got[:, 1], first[:, 1]), mine)
    first_down, second_down = halve(
        passed_down, lambda first: (keep_down[1], got_down[1], first[1]), mine
    )
    d_tokens, second_in, second_down = lax.optimization_barrier((add(*terms), second_in, second_down))
    mean = [total(keep[m, 0], got[m, 0], first_in[m, 0], second_in[m]) / 8.0 for m in range(2)]
    mean_down = total(keep_down[0], got_down[0], first_down[0], second_down) / 8.0
    return (d_tokens, mean[0], mean[1], mean_down, left_gate[None], left_up[None], left_down[None])


def solution(mesh):
    in_specs = (
        P("dp", "expert", None, None),
        P(("dp", "expert"), None),
        P(("dp", "expert"), None),
        P(("dp", "expert"), None),
        P("expert", None, None),
        P("expert", None, None),
        P("expert", None, None),
        P("dp", "expert", None, None),
        P("dp", "expert", None, None),
        P("dp", "expert", None, None),
    )
    out_specs = (
        P(("dp", "expert"), None),
        P("expert", "dp", None),
        P("expert", "dp", None),
        P("expert", None, "dp"),
        P("dp", "expert", None, None),
        P("dp", "expert", None, None),
        P("dp", "expert", None, None),
    )
    return jax.shard_map(
        on_device, mesh=mesh, in_specs=in_specs, out_specs=out_specs, check_vma=False
    )
```

```python
import functools

import jax
import jax.numpy as jnp
from jax import lax
from jax.experimental import pallas as pl
from jax.experimental.pallas import tpu as pltpu
from jax.sharding import PartitionSpec as P

loss_unscale = 0.0625
epsilon = 1e-05

SIDE = 4
OFFSETS = (0, -1, 1, 2)
CAP = 80
TOK = 256
PACK = TOK + 16
D = 1024
HID = 512
BF = jnp.bfloat16
F32 = jnp.float32
VMEM_LIMIT = 56 * 2**20
GROUPS_VMEM_LIMIT = 63 * 2**20


def place_of(here):
    core = here[0] & 1
    z, y = here[1] // SIDE, here[1] & (SIDE - 1)
    return here[0] // 2, core, jnp.where(core == 0, z, y), jnp.where(core == 0, y, z)


def expert_at(here, first_off, second_off):
    _, core, first, second = place_of(here)
    first, second = (first + first_off + SIDE) & (SIDE - 1), (second + second_off + SIDE) & (SIDE - 1)
    return jnp.where(core == 0, first * SIDE + second, second * SIDE + first)


def block_place(owner, x, core):
    apart = owner ^ x
    return jnp.where(apart == 0, 0, jnp.where(apart == 1, 2 - core, jnp.where(apart == 2, 3, 1 + core)))


def pairs(axis, step):
    out = []
    for dp in range(8):
        core = dp % 2
        for z in range(SIDE):
            for y in range(SIDE):
                along_z = (axis == 0) == (core == 0)
                z2, y2 = ((z + step) % SIDE, y) if along_z else (z, (y + step) % SIDE)
                out.append((dp * 16 + z * SIDE + y, dp * 16 + z2 * SIDE + y2))
    return out


def hop(value, axis, step):
    return lax.ppermute(value, ("dp", "expert"), pairs(axis, step))


def dp_hop(value, move):
    return lax.ppermute(
        value, "dp", [(x * 2 + c, move(x, c)[0] % SIDE * 2 + move(x, c)[1]) for x in range(SIDE) for c in range(2)]
    )


def nt(left, right):
    return lax.dot_general(left, right, (((1,), (1,)), ((), ())), preferred_element_type=F32)


def pack_kernel(tokens, routes, probs, out):
    out[:TOK, :] = tokens[...]
    weights = probs[...]
    high = weights.astype(BF)
    left = weights - high.astype(F32)
    middle = left.astype(BF)
    low = (left - middle.astype(F32)).astype(BF)
    out[TOK : TOK + 8, :] = jnp.concatenate(
        [routes[...].astype(F32).astype(BF), high, middle, low], axis=1
    )
    out[TOK + 8 :, :] = jnp.zeros((8, D), BF)


def pack(tokens, routes, probs):
    return pl.pallas_call(
        pack_kernel,
        out_shape=jax.ShapeDtypeStruct((PACK, D), BF),
        cost_estimate=pl.CostEstimate(flops=0, bytes_accessed=1_100_000, transcendentals=0),
        name="pack",
    )(tokens, routes.T, probs.T)


def forward_kernel(chained, here, *refs):
    xs, (wg, wu), refs = refs[:8], refs[8:10], refs[10 + (3 if chained else 0) :]
    xt, ht, m12, rows = refs
    for i in range(8):
        rows[i * CAP : (i + 1) * CAP, :] = xs[i][0, 0]
    half = 4 * CAP
    pre = []
    for h in range(2):
        saved = rows[h * half : (h + 1) * half, :]
        pre.append(
            (
                jnp.dot(saved, wg[0], preferred_element_type=F32),
                jnp.dot(saved, wu[0], preferred_element_type=F32),
            )
        )
    xt[0] = rows[...].T
    hidden = []
    for h, (gate, up) in enumerate(pre):
        logistic = jax.nn.sigmoid(gate)
        act = gate * logistic
        m12[0, h * half : (h + 1) * half, :HID] = (up * (logistic * (1.0 + gate * (1.0 - logistic)))).astype(BF)
        m12[0, h * half : (h + 1) * half, HID:] = act.astype(BF)
        hidden.append((act * up).astype(BF))
    ht[0] = jnp.concatenate(hidden, axis=0).T


def forward_terms(e, here, x, wg, wu, carried):
    blocks = x.reshape(2, 16, CAP, D)
    chained = carried is not None

    def block_at(i):
        def at(h, here):
            return e, expert_at(here, OFFSETS[i % 4], h if i < 4 else 3 * h - 1), 0, 0

        return pl.BlockSpec((1, 1, CAP, D), at)

    half = 8 * CAP
    return pl.pallas_call(
        functools.partial(forward_kernel, chained),
        grid_spec=pltpu.PrefetchScalarGridSpec(
            num_scalar_prefetch=1,
            grid=(2,),
            in_specs=[block_at(i) for i in range(8)]
            + [pl.BlockSpec((1, D, HID), lambda h, p: (e, 0, 0))] * 2
            + [pl.BlockSpec(memory_space=pl.ANY)] * (3 if chained else 0),
            out_specs=[
                pl.BlockSpec((1, D, half), lambda h, p: (e, 0, h)),
                pl.BlockSpec((1, HID, half), lambda h, p: (e, 0, h)),
                pl.BlockSpec((1, half, 2 * HID), lambda h, p: (e, h, 0)),
            ],
            scratch_shapes=[pltpu.VMEM((half, D), BF)],
        ),
        out_shape=[
            jax.ShapeDtypeStruct((2, D, 16 * CAP), BF),
            jax.ShapeDtypeStruct((2, HID, 16 * CAP), BF),
            jax.ShapeDtypeStruct((2, 16 * CAP, 2 * HID), BF),
        ],
        input_output_aliases={11 + i: i for i in range(3)} if chained else {},
        compiler_params=pltpu.CompilerParams(vmem_limit_bytes=VMEM_LIMIT),
        cost_estimate=pl.CostEstimate(flops=2_700_000_000, bytes_accessed=15_000_000, transcendentals=655_360),
        name="forward_terms",
    )(here, *([blocks] * 8), wg, wu, *(carried or ()))


def dispatch_kernel(targets, layout, here, *refs):
    blocks, outs, hots = refs[:4], refs[4 : 4 + len(layout)], refs[4 + len(layout) :]
    before = (
        lax.broadcasted_iota(jnp.int32, (TOK, TOK), 0) < lax.broadcasted_iota(jnp.int32, (TOK, TOK), 1)
    ).astype(BF)
    slot = lax.broadcasted_iota(jnp.int32, (CAP, TOK), 0).astype(F32)
    names = [(2 * expert_at(here, 0, OFFSETS[t]) + e).astype(F32) for t in targets for e in range(2)]
    named, weights = [], []
    for i in range(4):
        meta = blocks[i][TOK:, :].astype(F32)[:8]
        routes = meta[:, :TOK]
        probs = meta[:, TOK : 2 * TOK] + meta[:, 2 * TOK : 3 * TOK] + meta[:, 3 * TOK :]
        for name in names:
            hit = routes == name
            named.append(jnp.sum(jnp.where(hit, 1.0, 0.0), axis=0, keepdims=True))
            weights.append(jnp.sum(jnp.where(hit, probs, 0.0), axis=0, keepdims=True))
    mask = jnp.concatenate(named, axis=0)
    rank = jnp.dot(mask.astype(BF), before, preferred_element_type=F32)
    key = jnp.where(mask > 0.5, rank, -1.0)
    per = len(names)
    for i in range(4):
        halves, scales = [], []
        for k in range(per):
            hit = slot == key[per * i + k : per * i + k + 1, :]
            halves.append(jnp.where(hit, 1.0, 0.0).astype(BF))
            scales.append(jnp.sum(jnp.where(hit, weights[per * i + k], 0.0), axis=1, keepdims=True))
            hots[k // 2][i, k % 2 * CAP : (k % 2 + 1) * CAP, :] = halves[k]
        chosen = jnp.concatenate(halves, axis=0)
        taken = jnp.dot(chosen, blocks[i][:TOK, :], preferred_element_type=F32)
        scaled = (taken * jnp.concatenate(scales, axis=0)).astype(BF)
        for out, held in zip(outs, layout):
            for n, (target, e) in enumerate(held):
                k = 2 * targets.index(target) + e
                out[n, i * CAP : (i + 1) * CAP, :] = scaled[k * CAP : (k + 1) * CAP]


def dispatch(targets, layout, here, blocks):
    whole = pl.BlockSpec(memory_space=pltpu.VMEM)
    out = pl.pallas_call(
        functools.partial(dispatch_kernel, targets, layout),
        in_specs=[pl.BlockSpec(memory_space=pltpu.SMEM)] + [whole] * 4,
        out_specs=[whole] * (len(layout) + len(targets)),
        out_shape=[jax.ShapeDtypeStruct((len(held), 4 * CAP, D), BF) for held in layout]
        + [jax.ShapeDtypeStruct((4, 2 * CAP, TOK), BF)] * len(targets),
        compiler_params=pltpu.CompilerParams(vmem_limit_bytes=VMEM_LIMIT),
        cost_estimate=pl.CostEstimate(
            flops=400_000_000 * len(targets), bytes_accessed=6_000_000, transcendentals=0
        ),
        name="dispatch_" + "".join(str(t) for t in targets),
    )(here, *blocks)
    return out[: len(layout)], out[len(layout) :]


class Copies:
    def __init__(self, semaphores):
        self.semaphores, self.started = semaphores, []

    def start(self, source, target):
        copy = pltpu.make_async_copy(source, target, self.semaphores.at[len(self.started)])
        copy.start()
        self.started.append(copy)
        return copy

    def wait(self):
        for copy in self.started:
            copy.wait()


def halves_of(refs, split):
    out = []
    for two in split:
        out.append([refs[0], refs[1]] if two else [refs[0].at[0], refs[0].at[1]])
        refs = refs[2 if two else 1 :]
    return out


def groups_kernel(groups, split, chained, *refs):
    count = len(groups)
    lent = count + sum(split)
    arrived = halves_of(refs[:lent], split)
    m12, wd, wg, wu = refs[lent : lent + 4]
    refs = refs[lent + 4 + (1 if chained else 0) :]
    gab, outs, refs = refs[0], halves_of(refs[1 : 1 + lent], split), refs[1 + lent :]
    m12_v, wd_v, wg_v, wu_v, cot_v, gab_v, rows_v, sem_in, sem_out = refs
    loads, stores, cot_loads, factor_loads = Copies(sem_in), Copies(sem_out), [], []
    load, store = loads.start, stores.start

    down_loads, weight_loads = [], []
    for n, group in enumerate(groups):
        cot_loads.append([load(arrived[n][e], cot_v.at[n, e]) for e in range(2)])
        if n == 0:
            down_loads = [load(wd.at[e], wd_v.at[e]) for e in range(2)]
        factor_loads.append(
            [load(m12.at[e, pl.ds(group * 4 * CAP, 4 * CAP)], m12_v.at[n, e]) for e in range(2)]
        )
        if n == 0:
            weight_loads = [[load(wg.at[e], wg_v.at[e]), load(wu.at[e], wu_v.at[e])] for e in range(2)]
    for n, group in enumerate(groups):
        place = pl.ds(group * 4 * CAP, 4 * CAP)
        for e in range(2):
            cot_loads[n][e].wait()
            if n == 0:
                down_loads[e].wait()
            grad_hidden = nt(cot_v[n, e], wd_v[e])
            factor_loads[n][e].wait()
            gab_v[n, e, :, :HID] = (grad_hidden * m12_v[n, e, :, :HID].astype(F32)).astype(BF)
            gab_v[n, e, :, HID:] = (grad_hidden * m12_v[n, e, :, HID:].astype(F32)).astype(BF)
            store(gab_v.at[n, e], gab.at[e, place])
        for e in range(2):
            if n == 0:
                for item in weight_loads[e]:
                    item.wait()
            rows_v[n, e] = (nt(gab_v[n, e, :, :HID], wg_v[e]) + nt(gab_v[n, e, :, HID:], wu_v[e])).astype(BF)
            store(rows_v.at[n, e], outs[n][e])
    stores.wait()


def groups_pass(groups, arrived, m12, wd, wg, wu, carried):
    chained = carried is not None
    count = len(groups)
    anywhere = pl.BlockSpec(memory_space=pl.ANY)
    slots = jax.ShapeDtypeStruct((2, 16 * CAP, D), BF)
    split = [isinstance(a, tuple) for a in arrived]
    lent = count + sum(split)
    args = [a for two, a in zip(split, arrived) for a in (a if two else (a,))]
    args += [m12, wd, wg, wu] + ([carried] if chained else [])
    row_shapes = []
    for two in split:
        shape = (4 * CAP, D) if two else (2, 4 * CAP, D)
        row_shapes += [jax.ShapeDtypeStruct(shape, BF)] * (2 if two else 1)
    out = pl.pallas_call(
        functools.partial(groups_kernel, groups, split, chained),
        in_specs=[anywhere] * len(args),
        out_specs=[anywhere] * (1 + lent),
        out_shape=[slots] + row_shapes,
        scratch_shapes=[
            pltpu.VMEM((count, 2, 4 * CAP, 2 * HID), BF),
            pltpu.VMEM((2, HID, D), BF),
            pltpu.VMEM((2, D, HID), BF),
            pltpu.VMEM((2, D, HID), BF),
            pltpu.VMEM((count, 2, 4 * CAP, D), BF),
            pltpu.VMEM((count, 2, 4 * CAP, 2 * HID), BF),
            pltpu.VMEM((count, 2, 4 * CAP, D), BF),
            pltpu.SemaphoreType.DMA((6 + 4 * count,)),
            pltpu.SemaphoreType.DMA((4 * count,)),
        ],
        input_output_aliases={lent + 4: 0} if chained else {},
        compiler_params=pltpu.CompilerParams(vmem_limit_bytes=GROUPS_VMEM_LIMIT),
        cost_estimate=pl.CostEstimate(
            flops=2_100_000_000 * count, bytes_accessed=6_000_000 + 9_000_000 * count, transcendentals=0
        ),
        name="groups_" + "".join(str(g) for g in groups),
    )(*args)
    return out[0], out[1:]


def combine_kernel(*refs):
    rows, hots, outs, (rows_v, hots_v, sem_rows, sem_hots) = refs[:5], refs[5:9], refs[9:13], refs[13:]
    rows = halves_of(rows, (False, False, False, True))
    loads = []
    for i in range(4):
        mine = []
        for k in range(4):
            mine.append(
                pltpu.make_async_copy(
                    hots[k].at[i], hots_v.at[i, pl.ds(k * 2 * CAP, 2 * CAP)], sem_hots.at[4 * i + k]
                )
            )
            for e in range(2):
                mine.append(
                    pltpu.make_async_copy(
                        rows[k][e].at[pl.ds(i * CAP, CAP)],
                        rows_v.at[i, pl.ds((2 * k + e) * CAP, CAP)],
                        sem_rows.at[8 * i + 2 * k + e],
                    )
                )
        for item in mine:
            item.start()
        loads.append(mine)
    for i in range(4):
        for item in loads[i]:
            item.wait()
        outs[i][...] = lax.dot_general(
            hots_v[i], rows_v[i], (((0,), (0,)), ((), ())), preferred_element_type=F32
        ).astype(BF)


def combine(rows, hots):
    anywhere = pl.BlockSpec(memory_space=pl.ANY)
    return pl.pallas_call(
        combine_kernel,
        in_specs=[anywhere] * 9,
        out_specs=[pl.BlockSpec(memory_space=pltpu.VMEM)] * 4,
        out_shape=[jax.ShapeDtypeStruct((TOK, D), BF)] * 4,
        scratch_shapes=[
            pltpu.VMEM((4, 8 * CAP, D), BF),
            pltpu.VMEM((4, 8 * CAP, TOK), BF),
            pltpu.SemaphoreType.DMA((32,)),
            pltpu.SemaphoreType.DMA((16,)),
        ],
        compiler_params=pltpu.CompilerParams(vmem_limit_bytes=VMEM_LIMIT),
        cost_estimate=pl.CostEstimate(flops=1_400_000_000, bytes_accessed=9_000_000, transcendentals=0),
        name="combine",
    )(*rows, *hots)


def compress(local_grad, residual):
    carried = local_grad * loss_unscale + residual.astype(F32)
    magnitude = jnp.mean(jnp.abs(carried), axis=-1, keepdims=True) + epsilon
    compressed = (magnitude * jnp.tanh(carried * (1.0 / magnitude))).astype(BF)
    return compressed, (carried - compressed.astype(F32)).astype(BF)


def gate_up_kernel(here, xt, gab, res_gate, res_up, keep, give_gate, give_up, left_gate, left_up, held):
    x, core, _, _ = place_of(here)
    half = pl.program_id(1)
    grads = [jnp.dot(xt[0, u * 256 : (u + 1) * 256], gab[0], preferred_element_type=F32) for u in range(2)]
    for u in range(2):
        rows = slice(u * 256, (u + 1) * 256)
        kept_at = block_place(2 * half + u, x, core)
        given_at = block_place(2 * half + u, x, 1 - core)
        for m, (res, left) in enumerate(((res_gate, left_gate), (res_up, left_up))):
            held[u, m], left[0, rows] = compress(grads[u][:, m * HID : (m + 1) * HID], res[0, rows])
            keep[m, kept_at, 0] = held[u, m, pl.ds(pl.multiple_of(core * 128, 128), 128)]
            give = (give_gate, give_up)[m]
            give[given_at, 0] = held[u, m, pl.ds(pl.multiple_of((1 - core) * 128, 128), 128)]


def gate_up_grads(here, xt, gab, res_gate, res_up):
    tile = pl.BlockSpec((1, HID, HID), lambda e, t, s: (e, t, 0))
    res_shape = jax.ShapeDtypeStruct((2, D, HID), BF)
    keep_shape = jax.ShapeDtypeStruct((2, SIDE, 2, 128, HID), BF)
    give_shape = jax.ShapeDtypeStruct((SIDE, 2, 128, HID), BF)
    return pl.pallas_call(
        gate_up_kernel,
        grid_spec=pltpu.PrefetchScalarGridSpec(
            num_scalar_prefetch=1,
            grid=(2, 2),
            in_specs=[
                pl.BlockSpec((1, 512, 16 * CAP), lambda e, t, s: (e, t, 0)),
                pl.BlockSpec((1, 16 * CAP, 2 * HID), lambda e, t, s: (e, 0, 0)),
                tile,
                tile,
            ],
            out_specs=[pl.BlockSpec((2, SIDE, 1, 128, HID), lambda e, t, s: (0, 0, e, 0, 0))]
            + [pl.BlockSpec((SIDE, 1, 128, HID), lambda e, t, s: (0, e, 0, 0))] * 2
            + [tile, tile],
            scratch_shapes=[pltpu.VMEM((2, 2, 256, HID), BF)],
        ),
        out_shape=[keep_shape, give_shape, give_shape, res_shape, res_shape],
        compiler_params=pltpu.CompilerParams(vmem_limit_bytes=VMEM_LIMIT),
        cost_estimate=pl.CostEstimate(flops=5_400_000_000, bytes_accessed=22_000_000, transcendentals=2_000_000),
        name="gate_up_grads",
    )(here, xt, gab, res_gate, res_up)


def down_kernel(split, here, ht, res, *refs):
    lent = 4 + sum(split)
    arrived, (keep, give, left) = halves_of(refs[:lent], split), refs[lent : lent + 3]
    ht_v, cot_v, res_v, left_v, sent_v, sem_in, sem_out = refs[lent + 3 :]
    x, core, _, _ = place_of(here)
    loads, stores, waits = Copies(sem_in), Copies(sem_out), {}
    for e in range(2):
        waits[e] = [loads.start(ht.at[e], ht_v.at[e])]
        waits[e] += [
            loads.start(arrived[g][e], cot_v.at[e, pl.ds(g * 4 * CAP, 4 * CAP)]) for g in range(4)
        ]
        waits[e] += [loads.start(res.at[e], res_v.at[e])]
    for e in range(2):
        for item in waits[e]:
            item.wait()
        for t in range(2):
            rows = pl.ds(t * 256, 256)
            grads = jnp.dot(ht_v[e, rows], cot_v[e], preferred_element_type=F32)
            compressed, left_v[e, rows] = compress(grads, res_v[e, rows])
            stores.start(left_v.at[e, rows], left.at[e, rows])
            for owner in range(SIDE):
                for c in range(2):
                    at = 2 * owner + c
                    sent_v[core ^ c, block_place(owner, x, c), e, rows] = compressed[:, at * 128 : (at + 1) * 128]
        stores.start(sent_v.at[0, :, e], keep.at[:, e])
        stores.start(sent_v.at[1, :, e], give.at[:, e])
    stores.wait()


def down_grads(here, ht, arrived, res):
    anywhere = pl.BlockSpec(memory_space=pl.ANY)
    blocks = jax.ShapeDtypeStruct((SIDE, 2, HID, 128), BF)
    split = [isinstance(a, tuple) for a in arrived]
    pieces = [a for two, one in zip(split, arrived) for a in (one if two else (one,))]
    return pl.pallas_call(
        functools.partial(down_kernel, split),
        in_specs=[pl.BlockSpec(memory_space=pltpu.SMEM)] + [anywhere] * (2 + len(pieces)),
        out_specs=[anywhere] * 3,
        out_shape=[blocks, blocks, jax.ShapeDtypeStruct((2, HID, D), BF)],
        scratch_shapes=[
            pltpu.VMEM((2, HID, 16 * CAP), BF),
            pltpu.VMEM((2, 16 * CAP, D), BF),
            pltpu.VMEM((2, HID, D), BF),
            pltpu.VMEM((2, HID, D), BF),
            pltpu.VMEM((2, SIDE, 2, HID, 128), BF),
            pltpu.SemaphoreType.DMA((12,)),
            pltpu.SemaphoreType.DMA((8,)),
        ],
        compiler_params=pltpu.CompilerParams(vmem_limit_bytes=VMEM_LIMIT),
        cost_estimate=pl.CostEstimate(flops=2_700_000_000, bytes_accessed=14_000_000, transcendentals=1_000_000),
        name="down_grads",
    )(here, ht, res, *pieces)


def total(*terms):
    out = terms[0].astype(F32)
    for term in terms[1:]:
        out = out + term.astype(F32)
    return out


def add(*terms):
    return total(*terms).astype(BF)


def partner(stage, x, core):
    return x ^ (1 if stage == core else 3)


def halve(passed, nearer, beside):
    first = dp_hop(passed, lambda x, c: (partner(0, x, c), c))
    first, _ = lax.optimization_barrier((first, beside))
    return first, dp_hop(add(*nearer(first)), lambda x, c: (partner(1, x, c), c))


def on_device(x_saved, d_out, routes, probs, w_gate, w_up, w_down, res_gate, res_up, res_down):
    here = jnp.stack([lax.axis_index("dp"), lax.axis_index("expert")]).astype(jnp.int32)

    own = pack(d_out, routes, probs)
    near = (hop(own, 0, 1), hop(own, 0, -1), hop(own, 0, 2))
    terms = forward_terms(0, here, x_saved[0], w_gate, w_up, None)
    near, terms = lax.optimization_barrier((near, terms))
    layout = (((2, 0), (2, 1)), ((1, 0), (1, 1)), ((3, 0),), ((3, 1),))
    (to_plus, to_minus, far_plus, far_minus), (hot1, hot2, hot3) = dispatch((1, 2, 3), layout, here, (own, *near))
    far_plus, far_minus = hop(far_plus[0], 1, 1), hop(far_minus[0], 1, -1)
    group1, group2 = hop(to_plus, 1, 1), hop(to_minus, 1, -1)
    (group0,), (hot0,) = dispatch((0,), (((0, 0), (0, 1)),), here, (own, *near))
    xt, ht, m12 = forward_terms(1, here, x_saved[0], w_gate, w_up, terms)

    run = functools.partial(groups_pass, m12=m12, wd=w_down, wg=w_gate, wu=w_up)
    gab, (rows0,) = run((0,), [group0], carried=None)
    far_plus, far_minus, gab = lax.optimization_barrier((far_plus, far_minus, gab))
    group3 = (hop(far_plus, 1, 1), hop(far_minus, 1, -1))
    gab, (rows1, rows2) = run((1, 2), [group1, group2], carried=gab)
    near_rows = (hop(rows2, 1, 1), hop(rows1, 1, -1))
    gab, (rows3a, rows3b) = run((3,), [group3], carried=gab)
    half_way = (hop(rows3a, 1, 1), hop(rows3b, 1, -1))

    keep, give_gate, give_up, left_gate, left_up = gate_up_grads(here, xt, gab, res_gate[0], res_up[0])
    near_rows, half_way, give_gate, give_up = lax.optimization_barrier((near_rows, half_way, give_gate, give_up))
    got_gate, got_up = (dp_hop(g, lambda x, c: (x, 1 - c)) for g in (give_gate, give_up))
    far_rows = (hop(half_way[0], 1, 1), hop(half_way[1], 1, -1))
    keep_down, give_down, left_down = down_grads(here, ht, (group0, group1, group2, group3), res_down[0])
    got_gate, got_up, give_down = lax.optimization_barrier((got_gate, got_up, give_down))
    got = jnp.stack([got_gate, got_up])
    passed = add(keep[:, 2:], got[:, 2:])
    far_rows, give_down = lax.optimization_barrier((far_rows, give_down))
    got_down = dp_hop(give_down, lambda x, c: (x, 1 - c))
    passed_down = add(keep_down[2:], got_down[2:])

    far_rows, passed_down = lax.optimization_barrier((far_rows, passed_down))
    mine, before, behind, across = combine((rows0, *near_rows, *far_rows), (hot0, hot1, hot2, hot3))
    terms = (mine, hop(behind, 0, 1), hop(before, 0, -1), hop(across, 0, 2))
    first_in, second_in = halve(passed, lambda first: (keep[:, 1], got[:, 1], first[:, 1]), mine)
    first_down, second_down = halve(
        passed_down, lambda first: (keep_down[1], got_down[1], first[1]), mine
    )
    d_tokens, second_in, second_down = lax.optimization_barrier((add(*terms), second_in, second_down))
    mean = [total(keep[m, 0], got[m, 0], first_in[m, 0], second_in[m]) / 8.0 for m in range(2)]
    mean_down = total(keep_down[0], got_down[0], first_down[0], second_down) / 8.0
    return (d_tokens, mean[0], mean[1], mean_down, left_gate[None], left_up[None], left_down[None])


def solution(mesh):
    in_specs = (
        P("dp", "expert", None, None),
        P(("dp", "expert"), None),
        P(("dp", "expert"), None),
        P(("dp", "expert"), None),
        P("expert", None, None),
        P("expert", None, None),
        P("expert", None, None),
        P("dp", "expert", None, None),
        P("dp", "expert", None, None),
        P("dp", "expert", None, None),
    )
    out_specs = (
        P(("dp", "expert"), None),
        P("expert", "dp", None),
        P("expert", "dp", None),
        P("expert", None, "dp"),
        P("dp", "expert", None, None),
        P("dp", "expert", None, None),
        P("dp", "expert", None, None),
    )
    return jax.shard_map(
        on_device, mesh=mesh, in_specs=in_specs, out_specs=out_specs, check_vma=False
    )
```

```python
import functools

import jax
import jax.numpy as jnp
from jax import lax
from jax.experimental import pallas as pl
from jax.experimental.pallas import tpu as pltpu
from jax.sharding import PartitionSpec as P

loss_unscale = 0.0625
epsilon = 1e-05

SIDE = 4
OFFSETS = (0, -1, 1, 2)
CAP = 80
TOK = 256
PACK = TOK + 16
D = 1024
HID = 512
BF = jnp.bfloat16
F32 = jnp.float32
VMEM_LIMIT = 56 * 2**20
GROUPS_VMEM_LIMIT = 63 * 2**20


def place_of(here):
    core = here[0] & 1
    z, y = here[1] // SIDE, here[1] & (SIDE - 1)
    return here[0] // 2, core, jnp.where(core == 0, z, y), jnp.where(core == 0, y, z)


def expert_at(here, first_off, second_off):
    _, core, first, second = place_of(here)
    first, second = (first + first_off + SIDE) & (SIDE - 1), (second + second_off + SIDE) & (SIDE - 1)
    return jnp.where(core == 0, first * SIDE + second, second * SIDE + first)


def block_place(owner, x, core):
    apart = owner ^ x
    return jnp.where(apart == 0, 0, jnp.where(apart == 1, 2 - core, jnp.where(apart == 2, 3, 1 + core)))


def pairs(axis, step):
    out = []
    for dp in range(8):
        core = dp % 2
        for z in range(SIDE):
            for y in range(SIDE):
                along_z = (axis == 0) == (core == 0)
                z2, y2 = ((z + step) % SIDE, y) if along_z else (z, (y + step) % SIDE)
                out.append((dp * 16 + z * SIDE + y, dp * 16 + z2 * SIDE + y2))
    return out


def hop(value, axis, step):
    return lax.ppermute(value, ("dp", "expert"), pairs(axis, step))


def dp_hop(value, move):
    return lax.ppermute(
        value, "dp", [(x * 2 + c, move(x, c)[0] % SIDE * 2 + move(x, c)[1]) for x in range(SIDE) for c in range(2)]
    )


def nt(left, right):
    return lax.dot_general(left, right, (((1,), (1,)), ((), ())), preferred_element_type=F32)


def pack_kernel(tokens, routes, probs, out):
    out[:TOK, :] = tokens[...]
    weights = probs[...]
    high = weights.astype(BF)
    left = weights - high.astype(F32)
    middle = left.astype(BF)
    low = (left - middle.astype(F32)).astype(BF)
    out[TOK : TOK + 8, :] = jnp.concatenate(
        [routes[...].astype(F32).astype(BF), high, middle, low], axis=1
    )
    out[TOK + 8 :, :] = jnp.zeros((8, D), BF)


def pack(tokens, routes, probs):
    return pl.pallas_call(
        pack_kernel,
        out_shape=jax.ShapeDtypeStruct((PACK, D), BF),
        cost_estimate=pl.CostEstimate(flops=0, bytes_accessed=1_100_000, transcendentals=0),
        name="pack",
    )(tokens, routes.T, probs.T)


def forward_kernel(chained, here, *refs):
    xs, (wg, wu), refs = refs[:8], refs[8:10], refs[10 + (3 if chained else 0) :]
    xt, ht, m12, rows = refs
    for i in range(8):
        rows[i * CAP : (i + 1) * CAP, :] = xs[i][0, 0]
    half = 4 * CAP
    pre = []
    for h in range(2):
        saved = rows[h * half : (h + 1) * half, :]
        pre.append(
            (
                jnp.dot(saved, wg[0], preferred_element_type=F32),
                jnp.dot(saved, wu[0], preferred_element_type=F32),
            )
        )
    xt[0] = rows[...].T
    hidden = []
    for h, (gate, up) in enumerate(pre):
        logistic = jax.nn.sigmoid(gate)
        act = gate * logistic
        m12[0, h * half : (h + 1) * half, :HID] = (up * (logistic * (1.0 + gate * (1.0 - logistic)))).astype(BF)
        m12[0, h * half : (h + 1) * half, HID:] = act.astype(BF)
        hidden.append((act * up).astype(BF))
    ht[0] = jnp.concatenate(hidden, axis=0).T


def forward_terms(e, here, x, wg, wu, carried):
    blocks = x.reshape(2, 16, CAP, D)
    chained = carried is not None

    def block_at(i):
        def at(h, here):
            return e, expert_at(here, OFFSETS[i % 4], h if i < 4 else 3 * h - 1), 0, 0

        return pl.BlockSpec((1, 1, CAP, D), at)

    half = 8 * CAP
    return pl.pallas_call(
        functools.partial(forward_kernel, chained),
        grid_spec=pltpu.PrefetchScalarGridSpec(
            num_scalar_prefetch=1,
            grid=(2,),
            in_specs=[block_at(i) for i in range(8)]
            + [pl.BlockSpec((1, D, HID), lambda h, p: (e, 0, 0))] * 2
            + [pl.BlockSpec(memory_space=pl.ANY)] * (3 if chained else 0),
            out_specs=[
                pl.BlockSpec((1, D, half), lambda h, p: (e, 0, h)),
                pl.BlockSpec((1, HID, half), lambda h, p: (e, 0, h)),
                pl.BlockSpec((1, half, 2 * HID), lambda h, p: (e, h, 0)),
            ],
            scratch_shapes=[pltpu.VMEM((half, D), BF)],
        ),
        out_shape=[
            jax.ShapeDtypeStruct((2, D, 16 * CAP), BF),
            jax.ShapeDtypeStruct((2, HID, 16 * CAP), BF),
            jax.ShapeDtypeStruct((2, 16 * CAP, 2 * HID), BF),
        ],
        input_output_aliases={11 + i: i for i in range(3)} if chained else {},
        compiler_params=pltpu.CompilerParams(vmem_limit_bytes=VMEM_LIMIT),
        cost_estimate=pl.CostEstimate(flops=2_700_000_000, bytes_accessed=15_000_000, transcendentals=655_360),
        name="forward_terms",
    )(here, *([blocks] * 8), wg, wu, *(carried or ()))


def dispatch_kernel(targets, layout, here, *refs):
    blocks, outs, hots = refs[:4], refs[4 : 4 + len(layout)], refs[4 + len(layout) :]
    before = (
        lax.broadcasted_iota(jnp.int32, (TOK, TOK), 0) < lax.broadcasted_iota(jnp.int32, (TOK, TOK), 1)
    ).astype(BF)
    slot = lax.broadcasted_iota(jnp.int32, (CAP, TOK), 0).astype(F32)
    names = [(2 * expert_at(here, 0, OFFSETS[t]) + e).astype(F32) for t in targets for e in range(2)]
    named, weights = [], []
    for i in range(4):
        meta = blocks[i][TOK:, :].astype(F32)[:8]
        routes = meta[:, :TOK]
        probs = meta[:, TOK : 2 * TOK] + meta[:, 2 * TOK : 3 * TOK] + meta[:, 3 * TOK :]
        for name in names:
            hit = routes == name
            named.append(jnp.sum(jnp.where(hit, 1.0, 0.0), axis=0, keepdims=True))
            weights.append(jnp.sum(jnp.where(hit, probs, 0.0), axis=0, keepdims=True))
    mask = jnp.concatenate(named, axis=0)
    rank = jnp.dot(mask.astype(BF), before, preferred_element_type=F32)
    key = jnp.where(mask > 0.5, rank, -1.0)
    per = len(names)
    for i in range(4):
        halves, scales = [], []
        for k in range(per):
            hit = slot == key[per * i + k : per * i + k + 1, :]
            halves.append(jnp.where(hit, 1.0, 0.0).astype(BF))
            scales.append(jnp.sum(jnp.where(hit, weights[per * i + k], 0.0), axis=1, keepdims=True))
            hots[k // 2][i, k % 2 * CAP : (k % 2 + 1) * CAP, :] = halves[k]
        chosen = jnp.concatenate(halves, axis=0)
        taken = jnp.dot(chosen, blocks[i][:TOK, :], preferred_element_type=F32)
        scaled = (taken * jnp.concatenate(scales, axis=0)).astype(BF)
        for out, held in zip(outs, layout):
            for n, (target, e) in enumerate(held):
                k = 2 * targets.index(target) + e
                out[n, i * CAP : (i + 1) * CAP, :] = scaled[k * CAP : (k + 1) * CAP]


def dispatch(targets, layout, here, blocks):
    whole = pl.BlockSpec(memory_space=pltpu.VMEM)
    out = pl.pallas_call(
        functools.partial(dispatch_kernel, targets, layout),
        in_specs=[pl.BlockSpec(memory_space=pltpu.SMEM)] + [whole] * 4,
        out_specs=[whole] * (len(layout) + len(targets)),
        out_shape=[jax.ShapeDtypeStruct((len(held), 4 * CAP, D), BF) for held in layout]
        + [jax.ShapeDtypeStruct((4, 2 * CAP, TOK), BF)] * len(targets),
        compiler_params=pltpu.CompilerParams(vmem_limit_bytes=VMEM_LIMIT),
        cost_estimate=pl.CostEstimate(
            flops=400_000_000 * len(targets), bytes_accessed=6_000_000, transcendentals=0
        ),
        name="dispatch_" + "".join(str(t) for t in targets),
    )(here, *blocks)
    return out[: len(layout)], out[len(layout) :]


class Copies:
    def __init__(self, semaphores):
        self.semaphores, self.started = semaphores, []

    def start(self, source, target):
        copy = pltpu.make_async_copy(source, target, self.semaphores.at[len(self.started)])
        copy.start()
        self.started.append(copy)
        return copy

    def wait(self):
        for copy in self.started:
            copy.wait()


def halves_of(refs, split):
    out = []
    for two in split:
        out.append([refs[0], refs[1]] if two else [refs[0].at[0], refs[0].at[1]])
        refs = refs[2 if two else 1 :]
    return out


def groups_kernel(groups, split, chained, *refs):
    count = len(groups)
    lent = count + sum(split)
    arrived = halves_of(refs[:lent], split)
    m12, wd, wg, wu = refs[lent : lent + 4]
    refs = refs[lent + 4 + (1 if chained else 0) :]
    gab, outs, refs = refs[0], halves_of(refs[1 : 1 + lent], split), refs[1 + lent :]
    m12_v, wd_v, wg_v, wu_v, cot_v, gab_v, rows_v, sem_in, sem_out = refs
    loads, stores, cot_loads, factor_loads = Copies(sem_in), Copies(sem_out), [], []
    load, store = loads.start, stores.start

    down_loads, weight_loads = [], []
    for n, group in enumerate(groups):
        cot_loads.append([load(arrived[n][e], cot_v.at[n, e]) for e in range(2)])
        if n == 0:
            down_loads = [load(wd.at[e], wd_v.at[e]) for e in range(2)]
        factor_loads.append(
            [load(m12.at[e, pl.ds(group * 4 * CAP, 4 * CAP)], m12_v.at[n, e]) for e in range(2)]
        )
        if n == 0:
            weight_loads = [[load(wg.at[e], wg_v.at[e]), load(wu.at[e], wu_v.at[e])] for e in range(2)]
    for n, group in enumerate(groups):
        place = pl.ds(group * 4 * CAP, 4 * CAP)
        for e in range(2):
            cot_loads[n][e].wait()
            if n == 0:
                down_loads[e].wait()
            grad_hidden = nt(cot_v[n, e], wd_v[e])
            factor_loads[n][e].wait()
            gab_v[n, e, :, :HID] = (grad_hidden * m12_v[n, e, :, :HID].astype(F32)).astype(BF)
            gab_v[n, e, :, HID:] = (grad_hidden * m12_v[n, e, :, HID:].astype(F32)).astype(BF)
            store(gab_v.at[n, e], gab.at[e, place])
        for e in range(2):
            if n == 0:
                for item in weight_loads[e]:
                    item.wait()
            rows_v[n, e] = (nt(gab_v[n, e, :, :HID], wg_v[e]) + nt(gab_v[n, e, :, HID:], wu_v[e])).astype(BF)
            store(rows_v.at[n, e], outs[n][e])
    stores.wait()


def groups_pass(groups, arrived, m12, wd, wg, wu, carried):
    chained = carried is not None
    count = len(groups)
    anywhere = pl.BlockSpec(memory_space=pl.ANY)
    slots = jax.ShapeDtypeStruct((2, 16 * CAP, D), BF)
    split = [isinstance(a, tuple) for a in arrived]
    lent = count + sum(split)
    args = [a for two, a in zip(split, arrived) for a in (a if two else (a,))]
    args += [m12, wd, wg, wu] + ([carried] if chained else [])
    row_shapes = []
    for two in split:
        shape = (4 * CAP, D) if two else (2, 4 * CAP, D)
        row_shapes += [jax.ShapeDtypeStruct(shape, BF)] * (2 if two else 1)
    out = pl.pallas_call(
        functools.partial(groups_kernel, groups, split, chained),
        in_specs=[anywhere] * len(args),
        out_specs=[anywhere] * (1 + lent),
        out_shape=[slots] + row_shapes,
        scratch_shapes=[
            pltpu.VMEM((count, 2, 4 * CAP, 2 * HID), BF),
            pltpu.VMEM((2, HID, D), BF),
            pltpu.VMEM((2, D, HID), BF),
            pltpu.VMEM((2, D, HID), BF),
            pltpu.VMEM((count, 2, 4 * CAP, D), BF),
            pltpu.VMEM((count, 2, 4 * CAP, 2 * HID), BF),
            pltpu.VMEM((count, 2, 4 * CAP, D), BF),
            pltpu.SemaphoreType.DMA((6 + 4 * count,)),
            pltpu.SemaphoreType.DMA((4 * count,)),
        ],
        input_output_aliases={lent + 4: 0} if chained else {},
        compiler_params=pltpu.CompilerParams(vmem_limit_bytes=GROUPS_VMEM_LIMIT),
        cost_estimate=pl.CostEstimate(
            flops=2_100_000_000 * count, bytes_accessed=6_000_000 + 9_000_000 * count, transcendentals=0
        ),
        name="groups_" + "".join(str(g) for g in groups),
    )(*args)
    return out[0], out[1:]


def combine_kernel(*refs):
    rows, hots, outs, (rows_v, hots_v, sem_rows, sem_hots) = refs[:5], refs[5:9], refs[9:13], refs[13:]
    rows = halves_of(rows, (False, False, False, True))
    loads = []
    for i in range(4):
        mine = []
        for k in range(4):
            mine.append(
                pltpu.make_async_copy(
                    hots[k].at[i], hots_v.at[i, pl.ds(k * 2 * CAP, 2 * CAP)], sem_hots.at[4 * i + k]
                )
            )
            for e in range(2):
                mine.append(
                    pltpu.make_async_copy(
                        rows[k][e].at[pl.ds(i * CAP, CAP)],
                        rows_v.at[i, pl.ds((2 * k + e) * CAP, CAP)],
                        sem_rows.at[8 * i + 2 * k + e],
                    )
                )
        for item in mine:
            item.start()
        loads.append(mine)
    for i in range(4):
        for item in loads[i]:
            item.wait()
        outs[i][...] = lax.dot_general(
            hots_v[i], rows_v[i], (((0,), (0,)), ((), ())), preferred_element_type=F32
        ).astype(BF)


def combine(rows, hots):
    anywhere = pl.BlockSpec(memory_space=pl.ANY)
    return pl.pallas_call(
        combine_kernel,
        in_specs=[anywhere] * 9,
        out_specs=[pl.BlockSpec(memory_space=pltpu.VMEM)] * 4,
        out_shape=[jax.ShapeDtypeStruct((TOK, D), BF)] * 4,
        scratch_shapes=[
            pltpu.VMEM((4, 8 * CAP, D), BF),
            pltpu.VMEM((4, 8 * CAP, TOK), BF),
            pltpu.SemaphoreType.DMA((32,)),
            pltpu.SemaphoreType.DMA((16,)),
        ],
        compiler_params=pltpu.CompilerParams(vmem_limit_bytes=VMEM_LIMIT),
        cost_estimate=pl.CostEstimate(flops=1_400_000_000, bytes_accessed=9_000_000, transcendentals=0),
        name="combine",
    )(*rows, *hots)


def compress(local_grad, residual):
    carried = local_grad * loss_unscale + residual.astype(F32)
    magnitude = jnp.mean(jnp.abs(carried), axis=-1, keepdims=True) + epsilon
    compressed = (magnitude * jnp.tanh(carried * (1.0 / magnitude))).astype(BF)
    return compressed, (carried - compressed.astype(F32)).astype(BF)


def gate_up_kernel(here, xt, gab, res_gate, res_up, keep, give_gate, give_up, left_gate, left_up, held):
    x, core, _, _ = place_of(here)
    half = pl.program_id(1)
    grads = [jnp.dot(xt[0, u * 256 : (u + 1) * 256], gab[0], preferred_element_type=F32) for u in range(2)]
    for u in range(2):
        rows = slice(u * 256, (u + 1) * 256)
        kept_at = block_place(2 * half + u, x, core)
        given_at = block_place(2 * half + u, x, 1 - core)
        for m, (res, left) in enumerate(((res_gate, left_gate), (res_up, left_up))):
            held[u, m], left[0, rows] = compress(grads[u][:, m * HID : (m + 1) * HID], res[0, rows])
            keep[m, kept_at, 0] = held[u, m, pl.ds(pl.multiple_of(core * 128, 128), 128)]
            give = (give_gate, give_up)[m]
            give[given_at, 0] = held[u, m, pl.ds(pl.multiple_of((1 - core) * 128, 128), 128)]


def gate_up_grads(here, xt, gab, res_gate, res_up):
    tile = pl.BlockSpec((1, HID, HID), lambda e, t, s: (e, t, 0))
    res_shape = jax.ShapeDtypeStruct((2, D, HID), BF)
    keep_shape = jax.ShapeDtypeStruct((2, SIDE, 2, 128, HID), BF)
    give_shape = jax.ShapeDtypeStruct((SIDE, 2, 128, HID), BF)
    return pl.pallas_call(
        gate_up_kernel,
        grid_spec=pltpu.PrefetchScalarGridSpec(
            num_scalar_prefetch=1,
            grid=(2, 2),
            in_specs=[
                pl.BlockSpec((1, 512, 16 * CAP), lambda e, t, s: (e, t, 0)),
                pl.BlockSpec((1, 16 * CAP, 2 * HID), lambda e, t, s: (e, 0, 0)),
                tile,
                tile,
            ],
            out_specs=[pl.BlockSpec((2, SIDE, 1, 128, HID), lambda e, t, s: (0, 0, e, 0, 0))]
            + [pl.BlockSpec((SIDE, 1, 128, HID), lambda e, t, s: (0, e, 0, 0))] * 2
            + [tile, tile],
            scratch_shapes=[pltpu.VMEM((2, 2, 256, HID), BF)],
        ),
        out_shape=[keep_shape, give_shape, give_shape, res_shape, res_shape],
        compiler_params=pltpu.CompilerParams(vmem_limit_bytes=VMEM_LIMIT),
        cost_estimate=pl.CostEstimate(flops=5_400_000_000, bytes_accessed=22_000_000, transcendentals=2_000_000),
        name="gate_up_grads",
    )(here, xt, gab, res_gate, res_up)


def down_kernel(split, here, ht, res, *refs):
    lent = 4 + sum(split)
    arrived, (keep, give, left) = halves_of(refs[:lent], split), refs[lent : lent + 3]
    ht_v, cot_v, res_v, left_v, sent_v, sem_in, sem_out = refs[lent + 3 :]
    x, core, _, _ = place_of(here)
    loads, stores, waits = Copies(sem_in), Copies(sem_out), {}
    for e in range(2):
        waits[e] = [loads.start(ht.at[e], ht_v.at[e])]
        waits[e] += [
            loads.start(arrived[g][e], cot_v.at[e, pl.ds(g * 4 * CAP, 4 * CAP)]) for g in range(4)
        ]
        waits[e] += [loads.start(res.at[e], res_v.at[e])]
    for e in range(2):
        for item in waits[e]:
            item.wait()
        for t in range(2):
            rows = pl.ds(t * 256, 256)
            grads = jnp.dot(ht_v[e, rows], cot_v[e], preferred_element_type=F32)
            compressed, left_v[e, rows] = compress(grads, res_v[e, rows])
            stores.start(left_v.at[e, rows], left.at[e, rows])
            for owner in range(SIDE):
                for c in range(2):
                    at = 2 * owner + c
                    sent_v[core ^ c, block_place(owner, x, c), e, rows] = compressed[:, at * 128 : (at + 1) * 128]
        stores.start(sent_v.at[0, :, e], keep.at[:, e])
        stores.start(sent_v.at[1, :, e], give.at[:, e])
    stores.wait()


def down_grads(here, ht, arrived, res):
    anywhere = pl.BlockSpec(memory_space=pl.ANY)
    blocks = jax.ShapeDtypeStruct((SIDE, 2, HID, 128), BF)
    split = [isinstance(a, tuple) for a in arrived]
    pieces = [a for two, one in zip(split, arrived) for a in (one if two else (one,))]
    return pl.pallas_call(
        functools.partial(down_kernel, split),
        in_specs=[pl.BlockSpec(memory_space=pltpu.SMEM)] + [anywhere] * (2 + len(pieces)),
        out_specs=[anywhere] * 3,
        out_shape=[blocks, blocks, jax.ShapeDtypeStruct((2, HID, D), BF)],
        scratch_shapes=[
            pltpu.VMEM((2, HID, 16 * CAP), BF),
            pltpu.VMEM((2, 16 * CAP, D), BF),
            pltpu.VMEM((2, HID, D), BF),
            pltpu.VMEM((2, HID, D), BF),
            pltpu.VMEM((2, SIDE, 2, HID, 128), BF),
            pltpu.SemaphoreType.DMA((12,)),
            pltpu.SemaphoreType.DMA((8,)),
        ],
        compiler_params=pltpu.CompilerParams(vmem_limit_bytes=VMEM_LIMIT),
        cost_estimate=pl.CostEstimate(flops=2_700_000_000, bytes_accessed=14_000_000, transcendentals=1_000_000),
        name="down_grads",
    )(here, ht, res, *pieces)


def total(*terms):
    out = terms[0].astype(F32)
    for term in terms[1:]:
        out = out + term.astype(F32)
    return out


def add(*terms):
    return total(*terms).astype(BF)


def partner(stage, x, core):
    return x ^ (1 if stage == core else 3)


def halve(passed, nearer, beside):
    first = dp_hop(passed, lambda x, c: (partner(0, x, c), c))
    first, _ = lax.optimization_barrier((first, beside))
    return first, dp_hop(add(*nearer(first)), lambda x, c: (partner(1, x, c), c))


def on_device(x_saved, d_out, routes, probs, w_gate, w_up, w_down, res_gate, res_up, res_down):
    here = jnp.stack([lax.axis_index("dp"), lax.axis_index("expert")]).astype(jnp.int32)

    own = pack(d_out, routes, probs)
    near = (hop(own, 0, 1), hop(own, 0, -1), hop(own, 0, 2))
    terms = forward_terms(0, here, x_saved[0], w_gate, w_up, None)
    near, terms = lax.optimization_barrier((near, terms))
    layout = (((2, 0), (2, 1)), ((1, 0), (1, 1)), ((3, 0),), ((3, 1),))
    (to_plus, to_minus, far_plus, far_minus), (hot1, hot2, hot3) = dispatch((1, 2, 3), layout, here, (own, *near))
    far_plus, far_minus = hop(far_plus[0], 1, 1), hop(far_minus[0], 1, -1)
    group1, group2 = hop(to_plus, 1, 1), hop(to_minus, 1, -1)
    (group0,), (hot0,) = dispatch((0,), (((0, 0), (0, 1)),), here, (own, *near))
    xt, ht, m12 = forward_terms(1, here, x_saved[0], w_gate, w_up, terms)

    run = functools.partial(groups_pass, m12=m12, wd=w_down, wg=w_gate, wu=w_up)
    gab, (rows0,) = run((0,), [group0], carried=None)
    far_plus, far_minus, gab = lax.optimization_barrier((far_plus, far_minus, gab))
    group3 = (hop(far_plus, 1, 1), hop(far_minus, 1, -1))
    gab, (rows1, rows2) = run((1, 2), [group1, group2], carried=gab)
    near_rows = (hop(rows2, 1, 1), hop(rows1, 1, -1))
    gab, (rows3a, rows3b) = run((3,), [group3], carried=gab)
    half_way = (hop(rows3a, 1, 1), hop(rows3b, 1, -1))

    keep, give_gate, give_up, left_gate, left_up = gate_up_grads(here, xt, gab, res_gate[0], res_up[0])
    near_rows, half_way, give_gate, give_up = lax.optimization_barrier((near_rows, half_way, give_gate, give_up))
    got_gate, got_up = (dp_hop(g, lambda x, c: (x, 1 - c)) for g in (give_gate, give_up))
    far_rows = (hop(half_way[0], 1, 1), hop(half_way[1], 1, -1))
    keep_down, give_down, left_down = down_grads(here, ht, (group0, group1, group2, group3), res_down[0])
    got = jnp.stack([got_gate, got_up])
    passed = add(keep[:, 2:], got[:, 2:])
    passed, give_down = lax.optimization_barrier((passed, give_down))
    far_rows, give_down = lax.optimization_barrier((far_rows, give_down))
    got_down = dp_hop(give_down, lambda x, c: (x, 1 - c))
    passed_down = add(keep_down[2:], got_down[2:])

    far_rows, passed_down = lax.optimization_barrier((far_rows, passed_down))
    mine, before, behind, across = combine((rows0, *near_rows, *far_rows), (hot0, hot1, hot2, hot3))
    terms = (mine, hop(behind, 0, 1), hop(before, 0, -1), hop(across, 0, 2))
    first_in, second_in = halve(passed, lambda first: (keep[:, 1], got[:, 1], first[:, 1]), mine)
    first_down, second_down = halve(
        passed_down, lambda first: (keep_down[1], got_down[1], first[1]), mine
    )
    d_tokens, second_in = lax.optimization_barrier((add(*terms), second_in))
    mean = [total(keep[m, 0], got[m, 0], first_in[m, 0], second_in[m]) / 8.0 for m in range(2)]
    mean, second_down = lax.optimization_barrier((mean, second_down))
    mean_down = total(keep_down[0], got_down[0], first_down[0], second_down) / 8.0
    return (d_tokens, mean[0], mean[1], mean_down, left_gate[None], left_up[None], left_down[None])


def solution(mesh):
    in_specs = (
        P("dp", "expert", None, None),
        P(("dp", "expert"), None),
        P(("dp", "expert"), None),
        P(("dp", "expert"), None),
        P("expert", None, None),
        P("expert", None, None),
        P("expert", None, None),
        P("dp", "expert", None, None),
        P("dp", "expert", None, None),
        P("dp", "expert", None, None),
    )
    out_specs = (
        P(("dp", "expert"), None),
        P("expert", "dp", None),
        P("expert", "dp", None),
        P("expert", None, "dp"),
        P("dp", "expert", None, None),
        P("dp", "expert", None, None),
        P("dp", "expert", None, None),
    )
    return jax.shard_map(
        on_device, mesh=mesh, in_specs=in_specs, out_specs=out_specs, check_vma=False
    )
```
